512 devices in a mesh: depth: 16 (over z, core), height: 32 (over x, y).
Axes of the slice: x: 4, y: 8, z: 8, core: 2. Of those that a mesh axis runs over, the one named last changes fastest.
Arguments:
- density: float32 [128, 2048, 128], P('depth', 'height'), may hold values from -6 to 6
- light_vector: float32 [3], replicated, may hold values from -1 to 1
- colour_gain: float32 [3], replicated, may hold values from 0.5 to 3
- colour_bias: float32 [3], replicated, may hold values from -1 to 1
- shear_step: int32 [4], replicated, may hold values from 0 to 32
- reverse_view: int32 [4], replicated, may hold values from 0 to 1
Outputs:
- images: float32 [4, 4, 2048, 128], P(None, None, ('height', 'depth'))
The draws below stay inside these ranges and needn't reach their ends.
All inputs are finite; a program needn't handle non-finite values.
Results may differ from the reference program's by a relative error of at most 0.0003.
Values sent between devices are 32-bit elements; how exact they have to be, the bound alone decides.
No kernel may reach another device: no remote copies, remote signals or barrier semaphores. Data moves between devices by JAX's collectives and lax.ppermute only.
A program may use at most 64 MiB of HBM per device.

```python
import jax
import jax.numpy as jnp
from jax import lax

NX = 128
VIEWS = 4
SHEAR_MAX = 32
NZ = 128
NY = 2048


def place_ends(result, key, least, largest):
    place = [jax.random.randint(jax.random.fold_in(key, axis), (), 0, length) for axis, length in enumerate(result.shape)]
    widest = result.shape.index(max(result.shape))
    beside = place[:widest] + [(place[widest] + 1) % result.shape[widest]] + place[widest + 1:]
    return result.at[tuple(place)].set(least).at[tuple(beside)].set(largest)


def block_scale(key, shape, cuts, least, high):
    gain, own = 1.0, jax.random.fold_in(key, 6)
    for axis_at, parts in cuts:
        steps = jnp.exp(jax.random.uniform(jax.random.fold_in(own, axis_at), (parts,), jnp.float32, least / len(cuts), high / len(cuts)))
        gain = gain * jnp.repeat(steps, shape[axis_at] // parts).reshape([-1 if axis == axis_at else 1 for axis in range(len(shape))])
    return gain


def noise(key, shape, scale, limit, shards=(), kind=jnp.bfloat16):
    entries = jax.random.normal(key, shape, jnp.float32) * scale
    if len(shards) > 0:
        entries = block_scale(key, shape, shards, -0.22, 0.18) * entries
    return jnp.clip(entries, min=-limit, max=limit).astype(kind)


def setup_inputs(seed: int = 0) -> dict:
    key_of = jax.random.split(jax.random.key(seed), 7)
    density = noise(key_of[0], (NZ, NY, NX), 1.0, 6.0, ((0, 16), (1, 32)), jnp.float32)
    light_vector = jnp.clip(jax.random.uniform(key_of[1], (3,), jnp.float32, -1.0, 1.0), -1.0, 1.0)
    colour_gain = jnp.clip(jax.random.uniform(key_of[2], (3,), jnp.float32, 0.5, 3.0), 0.5, 3.0)
    colour_bias = jnp.clip(jax.random.uniform(key_of[3], (3,), jnp.float32, -1.0, 1.0), -1.0, 1.0)
    shear_step = place_ends(jax.random.randint(key_of[4], (VIEWS,), 0, SHEAR_MAX + 1), jax.random.fold_in(key_of[4], 1), 0, SHEAR_MAX).astype(jnp.int32)
    reverse_view = place_ends(jax.random.randint(key_of[5], (VIEWS,), 0, 2), jax.random.fold_in(key_of[5], 1), 0, 1).astype(jnp.int32)
    return {"density": density, "light_vector": light_vector, "colour_gain": colour_gain, "colour_bias": colour_bias, "shear_step": shear_step, "reverse_view": reverse_view}


EXTINCTION = 2.5

def shade_block(padded, light_vector, colour_gain, colour_bias, extinction):
    centre = padded[1:-1, 1:-1, 1:-1]
    tilt_depth = 0.5 * (padded[2:, 1:-1, 1:-1] - padded[:-2, 1:-1, 1:-1])
    tilt_rows = 0.5 * (padded[1:-1, 2:, 1:-1] - padded[1:-1, :-2, 1:-1])
    tilt_cols = 0.5 * (padded[1:-1, 1:-1, 2:] - padded[1:-1, 1:-1, :-2])
    facing = (light_vector[0] * tilt_depth + light_vector[1] * tilt_rows + light_vector[2] * tilt_cols) * lax.rsqrt(1.0 + tilt_depth * tilt_depth + tilt_rows * tilt_rows + tilt_cols * tilt_cols)
    shading = 0.25 + 1.5 * jnp.maximum(facing, 0.0)
    optical = extinction * jax.nn.softplus(centre)
    opacity = -jnp.expm1(-optical)
    colour = jax.nn.sigmoid(colour_gain[:, None, None, None] * centre[None] + colour_bias[:, None, None, None])
    emitted = (opacity * shading)[None] * colour
    return jnp.concatenate([emitted, optical[None]], 0)

def reference(density, light_vector, colour_gain, colour_bias, shear_step, reverse_view):
    extinction = EXTINCTION / NZ
    padded = jnp.pad(density, 1)

    def view_image(view):
        step = shear_step[view]
        backward = reverse_view[view]

        def advance(carry, index):
            colour_sum, optical = carry
            plane = jnp.where(backward == 1, NZ - 1 - index, index).astype(jnp.int32)
            block = lax.dynamic_slice_in_dim(padded, plane, 3, 0)
            fields = shade_block(block, light_vector, colour_gain, colour_bias, extinction)[:, 0]
            fields = jnp.pad(fields, ((0, 0), (0, SHEAR_MAX), (0, 0)))
            offset = (plane * step // NZ).astype(jnp.int32)
            sample = lax.dynamic_slice_in_dim(fields, offset, NY, 1)
            colour_sum = colour_sum + sample[:3] * jnp.exp(-optical)[None]
            optical = optical + sample[3]
            return ((colour_sum, optical), None)
        start = (jnp.zeros((3, NY, NX), jnp.float32), jnp.zeros((NY, NX), jnp.float32))
        (colour_sum, optical), _ = lax.scan(advance, start, jnp.arange(NZ, dtype=jnp.int32))
        return jnp.concatenate([colour_sum, -jnp.expm1(-optical)[None]], 0)
    return jnp.stack([view_image(view) for view in range(VIEWS)], 1)
```

```python
import functools

import jax
import jax.numpy as jnp
from jax import lax
from jax.experimental import pallas as pl
from jax.experimental.pallas import tpu as pltpu
from jax.sharding import PartitionSpec as P

EXTINCTION = 2.5
SMEM = pl.BlockSpec(memory_space=pltpu.SMEM)
VMEM = pl.BlockSpec(memory_space=pltpu.VMEM)
PLANES, ROWS, COLS, SHEAR, VIEWS, GROUPS = 8, 64, 128, 32, 4, 16
TOP = 8
TALL = ROWS + SHEAR
PADDED = TOP + TALL + 8
SLABS = PLANES + 1
CHIPS = GROUPS // 2
SHARE = ROWS // GROUPS


def opacity_of(optical):
    series = 1.0 - optical * (1.0 / 6.0)
    for term in (5.0, 4.0, 3.0, 2.0):
        series = 1.0 - optical * (1.0 / term) * series
    return optical * series


def render_kernel(
    place, light, gain, bias, shear, reverse, own, low, high, before, given, kept, brick, fields, starts
):
    depth, height = place[0], place[1]
    total_planes = PLANES * GROUPS
    zeros = jnp.zeros((8, COLS), jnp.float32)
    for plane in range(PLANES):
        brick[plane + 2, TOP - 8 : TOP, :] = jnp.broadcast_to(low[plane : plane + 1, :], (8, COLS))
        brick[plane + 2, TOP : TOP + ROWS, :] = own[plane]
        brick[plane + 2, TOP + ROWS : TOP + TALL, :] = high[plane]
        brick[plane + 2, TOP + TALL :, :] = zeros
    for plane in range(2):
        brick[plane, TOP - 8 : TOP, :] = jnp.broadcast_to(before[plane, TALL : TALL + 1, :], (8, COLS))
        brick[plane, TOP : TOP + TALL, :] = before[plane, :TALL, :]
        brick[plane, TOP + TALL :, :] = zeros
    brick[PLANES + 2] = jnp.zeros((PADDED, COLS), jnp.float32)

    chunk = 32
    lane = lax.broadcasted_iota(jnp.int32, (chunk, COLS), 1)

    def shade(step, _):
        plane = 1 + step // (TALL // chunk)
        row = step % (TALL // chunk) * chunk
        row = pl.multiple_of(row, chunk)
        inside = jnp.where(plane == 1, depth > 0, jnp.where(plane == SLABS, depth == GROUPS - 1, True))
        beyond = jnp.logical_and(height == 31, row >= ROWS)
        extinction = jnp.where(jnp.logical_and(inside, jnp.logical_not(beyond)), EXTINCTION / total_planes, 0.0)
        window = brick[plane, pl.ds(row, chunk + 16), :]
        centre = window[TOP : TOP + chunk]
        tilt_rows = 0.5 * (window[TOP + 1 : TOP + 1 + chunk] - window[TOP - 1 : TOP - 1 + chunk])
        tilt_depth = 0.5 * (brick[plane + 1, pl.ds(row + TOP, chunk), :] - brick[plane - 1, pl.ds(row + TOP, chunk), :])
        right = jnp.where(lane == COLS - 1, 0.0, pltpu.roll(centre, COLS - 1, 1))
        left = jnp.where(lane == 0, 0.0, pltpu.roll(centre, 1, 1))
        tilt_cols = 0.5 * (right - left)
        facing = (light[0] * tilt_depth + light[1] * tilt_rows + light[2] * tilt_cols) * lax.rsqrt(
            1.0 + tilt_depth * tilt_depth + tilt_rows * tilt_rows + tilt_cols * tilt_cols
        )
        shading = 0.25 + 1.5 * jnp.maximum(facing, 0.0)
        optical = extinction * (jnp.maximum(centre, 0.0) + jnp.log1p(jnp.exp(-jnp.abs(centre))))
        strength = opacity_of(optical) * shading
        place_of = pl.multiple_of((plane - 1) * TALL + row, chunk)
        for colour in range(3):
            tone = jax.nn.sigmoid(gain[colour] * centre + bias[colour])
            fields[colour, pl.ds(place_of, chunk), :] = strength * tone
        fields[3, pl.ds(place_of, chunk), :] = optical
        return 0

    lax.fori_loop(0, SLABS * (TALL // chunk), shade, 0)

    for view in range(VIEWS):
        for step in range(SLABS):
            plane = jnp.where(reverse[view] == 1, SLABS - 1 - step, step)
            depth_plane = jnp.maximum(depth * PLANES - 1 + plane, 0)
            offset = lax.shift_right_logical(depth_plane * shear[view], 7)
            starts[view * SLABS + step] = plane * TALL + offset

    core = depth % 2
    upper = lax.broadcasted_iota(jnp.int32, (8, COLS), 0) < SHARE

    def render(tile, _):
        for pair in range(VIEWS // 2):
            sums = []
            for view in (2 * pair, 2 * pair + 1):
                red = green = blue = optical = jnp.zeros((8, COLS), jnp.float32)
                for step in range(SLABS):
                    rows = pl.ds(starts[view * SLABS + step] + 8 * tile, 8)
                    through = jnp.exp(-optical)
                    red = red + fields[0, rows, :] * through
                    green = green + fields[1, rows, :] * through
                    blue = blue + fields[2, rows, :] * through
                    optical = optical + fields[3, rows, :]
                sums.append((red, green, blue, optical))
            for kind in range(4):
                first, second = sums[0][kind], sums[1][kind]
                low_rows = jnp.where(upper, first, pltpu.roll(second, SHARE, 0))
                high_rows = jnp.where(upper, pltpu.roll(first, SHARE, 0), second)
                kept[tile, kind, pair] = jnp.where(core == 1, high_rows, low_rows)
                given[tile, kind, pair] = jnp.where(core == 1, low_rows, high_rows)
        return 0

    lax.fori_loop(0, ROWS // 8, render, 0)


def view_mask(reverse, pair, digit):
    upper = lax.broadcasted_iota(jnp.int32, (8, COLS), 0) < SHARE
    first = jnp.where(reverse[2 * pair] == digit, 1, 0)
    second = jnp.where(reverse[2 * pair + 1] == digit, 1, 0)
    return jnp.where(upper, first, second) == 1


def pair_kernel(place, reverse, kept, gathered, out):
    core = place[0] % 2
    for pair in range(VIEWS // 2):
        mine_front = view_mask(reverse, pair, core)

        def merge(chip, _):
            mine = [kept[chip, kind, pair] for kind in range(4)]
            other = [gathered[1 - core, chip, kind, pair] for kind in range(4)]
            through = jnp.exp(-jnp.where(mine_front, mine[3], other[3]))
            for kind in range(3):
                front = jnp.where(mine_front, mine[kind], other[kind])
                behind = jnp.where(mine_front, other[kind], mine[kind])
                out[chip, kind, pair] = front + through * behind
            out[chip, 3, pair] = mine[3] + other[3]
            return 0

        lax.fori_loop(0, CHIPS, merge, 0, unroll=True)


def final_kernel(reverse, slabs, out):
    for pair in range(VIEWS // 2):
        backward = view_mask(reverse, pair, 1)
        optical = [slabs[chip, 3, pair] for chip in range(CHIPS)]
        ahead, behind = [jnp.zeros((8, COLS), jnp.float32)], [jnp.zeros((8, COLS), jnp.float32)]
        for chip in range(CHIPS - 1):
            ahead.append(ahead[-1] + optical[chip])
            behind.append(behind[-1] + optical[CHIPS - 1 - chip])
        total = ahead[-1] + optical[-1]
        sums = [jnp.zeros((8, COLS), jnp.float32)] * 3
        for chip in range(CHIPS):
            through = jnp.exp(-jnp.where(backward, behind[CHIPS - 1 - chip], ahead[chip]))
            sums = [sums[kind] + slabs[chip, kind, pair] * through for kind in range(3)]
        small = total * (1.0 - total * 0.5 * (1.0 - total * (1.0 / 3.0) * (1.0 - total * 0.25 * (1.0 - total * 0.2))))
        cover = jnp.where(total < 0.0625, small, 1.0 - jnp.exp(-total))
        for kind, value in enumerate((*sums, cover)):
            out[kind, 2 * pair] = value[:SHARE]
            out[kind, 2 * pair + 1] = value[SHARE:]


def on_device(density, light_vector, colour_gain, colour_bias, shear_step, reverse_view):
    depth, height = lax.axis_index("depth"), lax.axis_index("height")
    place = jnp.stack([depth, height]).astype(jnp.int32)
    heights, depths = lax.axis_size("height"), lax.axis_size("depth")
    up = [(i, i + 1) for i in range(heights - 1)]
    down = [(i + 1, i) for i in range(heights - 1)]
    low = lax.ppermute(density[:, ROWS - 1, :], "height", up)
    high = lax.ppermute(density[:, :SHEAR, :], "height", down)
    last = jnp.concatenate(
        [density[PLANES - 2 :], high[PLANES - 2 :], jnp.broadcast_to(low[PLANES - 2 :, None], (2, 8, COLS))], 1
    )
    before = lax.ppermute(last, "depth", [(i, i + 1) for i in range(depths - 1)])

    part = jax.ShapeDtypeStruct((CHIPS, 4, VIEWS // 2, 8, COLS), jnp.float32)
    given, kept = pl.pallas_call(
        render_kernel,
        out_shape=(part, part),
        in_specs=[SMEM] * 6 + [VMEM] * 4,
        out_specs=(VMEM, VMEM),
        scratch_shapes=[
            pltpu.VMEM((PLANES + 3, PADDED, COLS), jnp.float32),
            pltpu.VMEM((4, SLABS * TALL, COLS), jnp.float32),
            pltpu.SMEM((VIEWS * SLABS,), jnp.int32),
        ],
        name="render",
    )(place, light_vector, colour_gain, colour_bias, shear_step, reverse_view, density, low, high, before)

    cores = [[2 * chip, 2 * chip + 1] for chip in range(CHIPS)]
    gathered = lax.all_gather(given, "depth", axis=0, axis_index_groups=cores)
    merged = pl.pallas_call(
        pair_kernel, out_shape=part, in_specs=[SMEM] * 2 + [VMEM] * 2, out_specs=VMEM, name="merge"
    )(place, reverse_view, kept, gathered)
    chips = [[core + 2 * chip for chip in range(CHIPS)] for core in range(2)]
    slabs = lax.all_to_all(merged, "depth", 0, 0, tiled=True, axis_index_groups=chips)
    return pl.pallas_call(
        final_kernel,
        out_shape=jax.ShapeDtypeStruct((4, VIEWS, SHARE, COLS), jnp.float32),
        in_specs=[SMEM, VMEM],
        out_specs=VMEM,
        name="composite",
    )(reverse_view, slabs)


def solution(mesh):
    placed = (P("depth", "height", None), P(), P(), P(), P(), P())
    return jax.shard_map(
        on_device,
        mesh=mesh,
        in_specs=placed,
        out_specs=P(None, None, ("height", "depth"), None),
        check_vma=False,
    )
```

```python
import functools

import jax
import jax.numpy as jnp
from jax import lax
from jax.experimental import pallas as pl
from jax.experimental.pallas import tpu as pltpu
from jax.sharding import PartitionSpec as P

EXTINCTION = 2.5
SMEM = pl.BlockSpec(memory_space=pltpu.SMEM)
VMEM = pl.BlockSpec(memory_space=pltpu.VMEM)
PLANES, ROWS, COLS, SHEAR, VIEWS, GROUPS = 8, 64, 128, 32, 4, 16
TOP = 8
TALL = ROWS + SHEAR
PADDED = TOP + TALL + 8
SLABS = PLANES + 1
CHIPS = GROUPS // 2
SHARE = ROWS // GROUPS
LIMIT = 8 * 2**20


def opacity_of(optical):
    series = 1.0 - optical * (1.0 / 6.0)
    for term in (5.0, 4.0, 3.0, 2.0):
        series = 1.0 - optical * (1.0 / term) * series
    return optical * series


def render_kernel(
    place, light, gain, bias, shear, reverse, own, low, high, before, given, kept, brick, fields, starts
):
    depth, height = place[0], place[1]
    total_planes = PLANES * GROUPS
    zeros = jnp.zeros((8, COLS), jnp.float32)
    for plane in range(PLANES):
        brick[plane + 2, TOP - 8 : TOP, :] = jnp.broadcast_to(low[plane : plane + 1, :], (8, COLS))
        brick[plane + 2, TOP : TOP + ROWS, :] = own[plane]
        brick[plane + 2, TOP + ROWS : TOP + TALL, :] = high[plane]
        brick[plane + 2, TOP + TALL :, :] = zeros
    for plane in range(2):
        brick[plane, TOP - 8 : TOP, :] = jnp.broadcast_to(before[plane, TALL : TALL + 1, :], (8, COLS))
        brick[plane, TOP : TOP + TALL, :] = before[plane, :TALL, :]
        brick[plane, TOP + TALL :, :] = zeros
    brick[PLANES + 2] = jnp.zeros((PADDED, COLS), jnp.float32)

    chunk = 32
    lane = lax.broadcasted_iota(jnp.int32, (chunk, COLS), 1)

    def shade(step, _):
        plane = 1 + step // (TALL // chunk)
        row = step % (TALL // chunk) * chunk
        row = pl.multiple_of(row, chunk)
        inside = jnp.where(plane == 1, depth > 0, jnp.where(plane == SLABS, depth == GROUPS - 1, True))
        beyond = jnp.logical_and(height == 31, row >= ROWS)
        extinction = jnp.where(jnp.logical_and(inside, jnp.logical_not(beyond)), EXTINCTION / total_planes, 0.0)
        window = brick[plane, pl.ds(row, chunk + 16), :]
        centre = window[TOP : TOP + chunk]
        tilt_rows = 0.5 * (window[TOP + 1 : TOP + 1 + chunk] - window[TOP - 1 : TOP - 1 + chunk])
        tilt_depth = 0.5 * (brick[plane + 1, pl.ds(row + TOP, chunk), :] - brick[plane - 1, pl.ds(row + TOP, chunk), :])
        right = jnp.where(lane == COLS - 1, 0.0, pltpu.roll(centre, COLS - 1, 1))
        left = jnp.where(lane == 0, 0.0, pltpu.roll(centre, 1, 1))
        tilt_cols = 0.5 * (right - left)
        facing = (light[0] * tilt_depth + light[1] * tilt_rows + light[2] * tilt_cols) * lax.rsqrt(
            1.0 + tilt_depth * tilt_depth + tilt_rows * tilt_rows + tilt_cols * tilt_cols
        )
        shading = 0.25 + 1.5 * jnp.maximum(facing, 0.0)
        optical = extinction * (jnp.maximum(centre, 0.0) + jnp.log1p(jnp.exp(-jnp.abs(centre))))
        strength = opacity_of(optical) * shading
        place_of = pl.multiple_of((plane - 1) * TALL + row, chunk)
        for colour in range(3):
            tone = jax.nn.sigmoid(gain[colour] * centre + bias[colour])
            fields[colour, pl.ds(place_of, chunk), :] = strength * tone
        fields[3, pl.ds(place_of, chunk), :] = optical
        return 0

    lax.fori_loop(0, SLABS * (TALL // chunk), shade, 0)

    for view in range(VIEWS):
        for step in range(SLABS):
            plane = jnp.where(reverse[view] == 1, SLABS - 1 - step, step)
            depth_plane = jnp.maximum(depth * PLANES - 1 + plane, 0)
            offset = lax.shift_right_logical(depth_plane * shear[view], 7)
            starts[view * SLABS + step] = plane * TALL + offset

    core = depth % 2
    upper = lax.broadcasted_iota(jnp.int32, (8, COLS), 0) < SHARE

    def render(tile, _):
        for pair in range(VIEWS // 2):
            sums = []
            for view in (2 * pair, 2 * pair + 1):
                red = green = blue = optical = jnp.zeros((8, COLS), jnp.float32)
                for step in range(SLABS):
                    rows = pl.ds(starts[view * SLABS + step] + 8 * tile, 8)
                    through = jnp.exp(-optical)
                    red = red + fields[0, rows, :] * through
                    green = green + fields[1, rows, :] * through
                    blue = blue + fields[2, rows, :] * through
                    optical = optical + fields[3, rows, :]
                sums.append((red, green, blue, optical))
            for kind in range(4):
                first, second = sums[0][kind], sums[1][kind]
                low_rows = jnp.where(upper, first, pltpu.roll(second, SHARE, 0))
                high_rows = jnp.where(upper, pltpu.roll(first, SHARE, 0), second)
                kept[tile, kind, pair] = jnp.where(core == 1, high_rows, low_rows)
                given[tile, kind, pair] = jnp.where(core == 1, low_rows, high_rows)
        return 0

    lax.fori_loop(0, ROWS // 8, render, 0)


def view_mask(reverse, pair, digit):
    upper = lax.broadcasted_iota(jnp.int32, (8, COLS), 0) < SHARE
    first = jnp.where(reverse[2 * pair] == digit, 1, 0)
    second = jnp.where(reverse[2 * pair + 1] == digit, 1, 0)
    return jnp.where(upper, first, second) == 1


def pair_kernel(place, reverse, kept, gathered, out):
    core = place[0] % 2
    for pair in range(VIEWS // 2):
        mine_front = view_mask(reverse, pair, core)

        def merge(chip, _):
            mine = [kept[chip, kind, pair] for kind in range(4)]
            other = [gathered[1 - core, chip, kind, pair] for kind in range(4)]
            through = jnp.exp(-jnp.where(mine_front, mine[3], other[3]))
            for kind in range(3):
                front = jnp.where(mine_front, mine[kind], other[kind])
                behind = jnp.where(mine_front, other[kind], mine[kind])
                out[chip, kind, pair] = front + through * behind
            out[chip, 3, pair] = mine[3] + other[3]
            return 0

        lax.fori_loop(0, CHIPS, merge, 0, unroll=True)


def final_kernel(reverse, slabs, out):
    for pair in range(VIEWS // 2):
        backward = view_mask(reverse, pair, 1)
        optical = [slabs[chip, 3, pair] for chip in range(CHIPS)]
        ahead, behind = [jnp.zeros((8, COLS), jnp.float32)], [jnp.zeros((8, COLS), jnp.float32)]
        for chip in range(CHIPS - 1):
            ahead.append(ahead[-1] + optical[chip])
            behind.append(behind[-1] + optical[CHIPS - 1 - chip])
        total = ahead[-1] + optical[-1]
        sums = [jnp.zeros((8, COLS), jnp.float32)] * 3
        for chip in range(CHIPS):
            through = jnp.exp(-jnp.where(backward, behind[CHIPS - 1 - chip], ahead[chip]))
            sums = [sums[kind] + slabs[chip, kind, pair] * through for kind in range(3)]
        small = total * (1.0 - total * 0.5 * (1.0 - total * (1.0 / 3.0) * (1.0 - total * 0.25 * (1.0 - total * 0.2))))
        cover = jnp.where(total < 0.0625, small, 1.0 - jnp.exp(-total))
        for kind, value in enumerate((*sums, cover)):
            out[kind, 2 * pair] = value[:SHARE]
            out[kind, 2 * pair + 1] = value[SHARE:]


def on_device(density, light_vector, colour_gain, colour_bias, shear_step, reverse_view):
    depth, height = lax.axis_index("depth"), lax.axis_index("height")
    place = jnp.stack([depth, height]).astype(jnp.int32)
    heights, depths = lax.axis_size("height"), lax.axis_size("depth")
    up = [(i, i + 1) for i in range(heights - 1)]
    down = [(i + 1, i) for i in range(heights - 1)]
    low = lax.ppermute(density[:, ROWS - 1, :], "height", up)
    high = lax.ppermute(density[:, :SHEAR, :], "height", down)
    last = jnp.concatenate(
        [density[PLANES - 2 :], high[PLANES - 2 :], jnp.broadcast_to(low[PLANES - 2 :, None], (2, 8, COLS))], 1
    )
    before = lax.ppermute(last, "depth", [(i, i + 1) for i in range(depths - 1)])

    part = jax.ShapeDtypeStruct((CHIPS, 4, VIEWS // 2, 8, COLS), jnp.float32)
    given, kept = pl.pallas_call(
        render_kernel,
        out_shape=(part, part),
        in_specs=[SMEM] * 6 + [VMEM] * 4,
        out_specs=(VMEM, VMEM),
        scratch_shapes=[
            pltpu.VMEM((PLANES + 3, PADDED, COLS), jnp.float32),
            pltpu.VMEM((4, SLABS * TALL, COLS), jnp.float32),
            pltpu.SMEM((VIEWS * SLABS,), jnp.int32),
        ],
        compiler_params=pltpu.CompilerParams(vmem_limit_bytes=LIMIT),
        name="render",
    )(place, light_vector, colour_gain, colour_bias, shear_step, reverse_view, density, low, high, before)

    cores = [[2 * chip, 2 * chip + 1] for chip in range(CHIPS)]
    gathered = lax.all_gather(given, "depth", axis=0, axis_index_groups=cores)
    merged = pl.pallas_call(
        pair_kernel, out_shape=part, in_specs=[SMEM] * 2 + [VMEM] * 2, out_specs=VMEM,
        compiler_params=pltpu.CompilerParams(vmem_limit_bytes=LIMIT), name="merge"
    )(place, reverse_view, kept, gathered)
    chips = [[core + 2 * chip for chip in range(CHIPS)] for core in range(2)]
    slabs = lax.all_to_all(merged, "depth", 0, 0, tiled=True, axis_index_groups=chips)
    return pl.pallas_call(
        final_kernel,
        out_shape=jax.ShapeDtypeStruct((4, VIEWS, SHARE, COLS), jnp.float32),
        in_specs=[SMEM, VMEM],
        out_specs=VMEM,
        compiler_params=pltpu.CompilerParams(vmem_limit_bytes=LIMIT),
        name="composite",
    )(reverse_view, slabs)


def solution(mesh):
    placed = (P("depth", "height", None), P(), P(), P(), P(), P())
    return jax.shard_map(
        on_device,
        mesh=mesh,
        in_specs=placed,
        out_specs=P(None, None, ("height", "depth"), None),
        check_vma=False,
    )
```

```python
import jax
import jax.numpy as jnp
from jax import lax
from jax.experimental import pallas as pl
from jax.experimental.pallas import tpu as pltpu
from jax.sharding import PartitionSpec as P

EXTINCTION = 2.5
SMEM = pl.BlockSpec(memory_space=pltpu.SMEM)
VMEM = pl.BlockSpec(memory_space=pltpu.VMEM)
ANY = pl.BlockSpec(memory_space=pl.ANY)
HBM = pl.BlockSpec(memory_space=pltpu.HBM)
PLANES, ROWS, COLS, SHEAR, VIEWS, GROUPS, BRICKS = 8, 64, 128, 32, 4, 16, 32
TOP = 8
TALL = ROWS + SHEAR
PADDED = TOP + TALL + 8
SLABS = PLANES + 1
CHIPS = GROUPS // 2
SHARE = ROWS // GROUPS
PARAMS = pltpu.CompilerParams(vmem_limit_bytes=8 * 2**20)
LIGHT, GAIN, BIAS, PLAIN, BEYOND, NEXT, NEXT_BEYOND = 0, 3, 6, 9, 10, 11, 12
FRONT, BACK, CORE = 0, 2, 4
FIRST = VIEWS * SLABS


def array(*shape):
    return jax.ShapeDtypeStruct(shape, jnp.float32)


def opacity_of(optical):
    series = 1.0 - optical * (1.0 / 6.0)
    for term in (5.0, 4.0, 3.0, 2.0):
        series = 1.0 - optical * (1.0 / term) * series
    return optical * series


def shade(coefficient, extinction, centre, above, below, before, after):
    lane = lax.broadcasted_iota(jnp.int32, centre.shape, 1)
    tilt_rows = 0.5 * (below - above)
    tilt_depth = 0.5 * (after - before)
    right = jnp.where(lane == COLS - 1, 0.0, pltpu.roll(centre, COLS - 1, 1))
    left = jnp.where(lane == 0, 0.0, pltpu.roll(centre, 1, 1))
    tilt_cols = 0.5 * (right - left)
    slope = coefficient(LIGHT) * tilt_depth + coefficient(LIGHT + 1) * tilt_rows + coefficient(LIGHT + 2) * tilt_cols
    facing = slope * lax.rsqrt(1.0 + tilt_depth * tilt_depth + tilt_rows * tilt_rows + tilt_cols * tilt_cols)
    shading = 0.25 + 1.5 * jnp.maximum(facing, 0.0)
    optical = extinction * (jnp.maximum(centre, 0.0) + jnp.log1p(jnp.exp(-jnp.abs(centre))))
    strength = opacity_of(optical) * shading
    tones = [jax.nn.sigmoid(coefficient(GAIN + i) * centre + coefficient(BIAS + i)) for i in range(3)]
    return [strength * tone for tone in tones] + [optical]


def load_kernel(density, own, low, high, semaphore):
    copy = pltpu.make_async_copy(density, own, semaphore)
    copy.start()
    copy.wait()
    high[...] = own[:, :SHEAR, :]
    for plane in range(PLANES):
        low[plane : plane + 1, :] = own[plane, ROWS - 1 : ROWS, :]


def inner_kernel(*refs):
    arguments, (own, fields, table, masks, starts), scalars, semaphores = refs[:5], refs[5:10], refs[10:15], refs[15]
    copies = [pltpu.make_async_copy(arguments[i], scalars[i], semaphores.at[i]) for i in range(5)]
    for copy in copies:
        copy.start()
    depth, height = lax.axis_index("depth"), lax.axis_index("height")
    for copy in copies:
        copy.wait()
    light, gain, bias, shear, reverse = scalars
    extinction = EXTINCTION / (PLANES * GROUPS)
    beyond = jnp.where(height == BRICKS - 1, 0.0, extinction)
    following = jnp.where(depth == GROUPS - 1, 0.0, extinction)
    both = jnp.where(depth == GROUPS - 1, 0.0, beyond)
    values_of = [ref[i] for ref in (light, gain, bias) for i in range(3)] + [extinction, beyond, following, both]
    for row, scalar in enumerate(values_of):
        table[row : row + 1, :] = jnp.full((1, COLS), scalar, jnp.float32)
    upper = lax.broadcasted_iota(jnp.int32, (8, COLS), 0) < SHARE
    core = depth % 2
    for base, digit in ((FRONT, core), (BACK, 1)):
        for pair in range(VIEWS // 2):
            first = jnp.where(reverse[2 * pair] == digit, 1.0, 0.0)
            second = jnp.where(reverse[2 * pair + 1] == digit, 1.0, 0.0)
            masks[base + pair] = jnp.where(upper, first, second)
    masks[CORE] = jnp.full((8, COLS), core, jnp.float32)
    first = jnp.where(depth == 0, 0, 1)
    starts[FIRST] = first
    for view in range(VIEWS):
        for step in range(SLABS):
            slot = jnp.where(reverse[view] == 1, SLABS - 1 - step, jnp.minimum(first + step, SLABS - 1))
            offset = lax.shift_right_logical((depth * PLANES + slot) * shear[view], 7)
            starts[view * SLABS + step] = slot * TALL + jnp.minimum(offset, SHEAR)

    def plane_of(step, _):
        plane = step + 1
        inner = slice(8, ROWS - 8)
        values = shade(
            lambda row: values_of[row],
            extinction,
            own[plane, inner, :],
            own[plane, 7 : ROWS - 9, :],
            own[plane, 9 : ROWS - 7, :],
            own[plane - 1, inner, :],
            own[plane + 1, inner, :],
        )
        rows = pl.ds(pl.multiple_of(plane * TALL + 8, 8), ROWS - 16)
        for kind in range(4):
            fields[kind, rows, :] = values[kind]
        return 0

    lax.fori_loop(0, PLANES - 2, plane_of, 0)


def join_kernel(own, low, high, table, brick, first):
    del table
    for plane in range(PLANES):
        parts = (
            (0, jnp.broadcast_to(low[plane : plane + 1, :], (8, COLS))),
            (TOP, own[plane]),
            (TOP + ROWS, high[plane]),
            (TOP + TALL, jnp.zeros((8, COLS), jnp.float32)),
        )
        for start, part in parts:
            brick[plane, start : start + part.shape[0], :] = part
            if plane < 2:
                first[plane, start : start + part.shape[0], :] = part


def shade_rows(table, extinction, row, count, plane, before, after, fields, slot):
    start = row + TOP
    values = shade(
        lambda at: table[at : at + 1, :],
        table[extinction : extinction + 1, :],
        plane[start : start + count, :],
        plane[start - 1 : start - 1 + count, :],
        plane[start + 1 : start + 1 + count, :],
        0.0 if before is None else before[start : start + count, :],
        after[start : start + count, :],
    )
    rows = pl.ds(pl.multiple_of(slot * TALL + row, 8), count)
    for kind in range(4):
        fields[kind, rows, :] = values[kind]


def edge_kernel(table, brick, held, fields):
    del held

    def plane_of(step, _):
        plane = step + 1
        refs = (brick.at[plane], brick.at[plane - 1], brick.at[plane + 1], fields, plane)
        shade_rows(table, PLAIN, 0, 8, *refs)
        shade_rows(table, PLAIN, ROWS - 8, 8, *refs)
        shade_rows(table, BEYOND, ROWS, SHEAR, *refs)
        return 0

    lax.fori_loop(0, PLANES - 2, plane_of, 0)


def render_kernel(table, masks, starts_in, brick, coming, held, given, kept, fields, starts, semaphore):
    del held
    copy = pltpu.make_async_copy(starts_in, starts, semaphore)
    copy.start()

    def whole_plane(slot, plane, before, after, own, beyond):
        refs = (plane, before, after, fields, slot)
        shade_rows(table, own, 0, SHEAR, *refs)
        shade_rows(table, own, SHEAR, SHEAR, *refs)
        shade_rows(table, beyond, ROWS, SHEAR, *refs)

    whole_plane(PLANES - 1, brick.at[PLANES - 1], brick.at[PLANES - 2], coming.at[0], PLAIN, BEYOND)
    whole_plane(PLANES, coming.at[0], brick.at[PLANES - 1], coming.at[1], NEXT, NEXT_BEYOND)
    copy.wait()
    leading = starts[FIRST] == 0

    @pl.when(leading)
    def _():
        whole_plane(0, brick.at[0], None, brick.at[1], PLAIN, BEYOND)

    def render(planes):
        upper = lax.broadcasted_iota(jnp.int32, (8, COLS), 0) < SHARE
        odd = masks[CORE] > 0.5

        def tile_of(tile, _):
            for pair in range(VIEWS // 2):
                sums = []
                for view in (2 * pair, 2 * pair + 1):
                    red = green = blue = optical = jnp.zeros((8, COLS), jnp.float32)
                    for step in range(planes):
                        rows = pl.ds(starts[view * SLABS + step] + 8 * tile, 8)
                        through = jnp.exp(-optical)
                        red = red + fields[0, rows, :] * through
                        green = green + fields[1, rows, :] * through
                        blue = blue + fields[2, rows, :] * through
                        optical = optical + fields[3, rows, :]
                    sums.append((red, green, blue, optical))
                for kind in range(4):
                    first, second = sums[0][kind], sums[1][kind]
                    even_rows = jnp.where(upper, first, pltpu.roll(second, SHARE, 0))
                    odd_rows = jnp.where(upper, pltpu.roll(first, SHARE, 0), second)
                    kept[tile, kind, pair] = jnp.where(odd, odd_rows, even_rows)
                    given[tile, kind, pair] = jnp.where(odd, even_rows, odd_rows)
            return 0

        lax.fori_loop(0, ROWS // 8, tile_of, 0)

    @pl.when(leading)
    def _():
        render(SLABS)

    @pl.when(jnp.logical_not(leading))
    def _():
        render(PLANES)


def merge_kernel(masks, kept, gathered, out):
    odd = masks[CORE] > 0.5
    for pair in range(VIEWS // 2):
        mine_front = masks[FRONT + pair] > 0.5

        def merge(chip, _):
            mine = [kept[chip, kind, pair] for kind in range(4)]
            other = [jnp.where(odd, gathered[0, chip, kind, pair], gathered[1, chip, kind, pair]) for kind in range(4)]
            through = jnp.exp(-jnp.where(mine_front, mine[3], other[3]))
            for kind in range(3):
                front = jnp.where(mine_front, mine[kind], other[kind])
                behind = jnp.where(mine_front, other[kind], mine[kind])
                out[chip, kind, pair] = front + through * behind
            out[chip, 3, pair] = mine[3] + other[3]
            return 0

        lax.fori_loop(0, CHIPS, merge, 0, unroll=True)


def final_kernel(masks, slabs, out):
    for pair in range(VIEWS // 2):
        backward = masks[BACK + pair] > 0.5
        optical = [slabs[chip, 3, pair] for chip in range(CHIPS)]
        ahead, behind = [jnp.zeros((8, COLS), jnp.float32)], [jnp.zeros((8, COLS), jnp.float32)]
        for chip in range(CHIPS - 1):
            ahead.append(ahead[-1] + optical[chip])
            behind.append(behind[-1] + optical[CHIPS - 1 - chip])
        total = ahead[-1] + optical[-1]
        sums = [jnp.zeros((8, COLS), jnp.float32)] * 3
        for chip in range(CHIPS):
            through = jnp.exp(-jnp.where(backward, behind[CHIPS - 1 - chip], ahead[chip]))
            sums = [sums[kind] + slabs[chip, kind, pair] * through for kind in range(3)]
        cover = jnp.where(total < 0.0625, opacity_of(total), 1.0 - jnp.exp(-total))
        for kind, value in enumerate((*sums, cover)):
            out[kind, 2 * pair] = value[:SHARE]
            out[kind, 2 * pair + 1] = value[SHARE:]


def kernel(body, name, out_shape, in_specs, out_specs, flops=0, **more):
    estimate = pl.CostEstimate(flops=flops, bytes_accessed=2**20, transcendentals=0)
    return pl.pallas_call(
        body,
        out_shape=out_shape,
        in_specs=in_specs,
        out_specs=out_specs,
        compiler_params=PARAMS,
        cost_estimate=estimate,
        name=name,
        **more,
    )


def on_device(density, light_vector, colour_gain, colour_bias, shear_step, reverse_view):
    heights, depths = lax.axis_size("height"), lax.axis_size("depth")

    own, own_low, own_high = kernel(
        load_kernel,
        "load",
        (array(PLANES, ROWS, COLS), array(PLANES, COLS), array(PLANES, SHEAR, COLS)),
        [HBM],
        (VMEM,) * 3,
        flops=10**9,
        scratch_shapes=[pltpu.SemaphoreType.DMA],
    )(density)
    high = lax.ppermute(own_high, "height", [(i + 1, i) for i in range(heights - 1)])
    low = lax.ppermute(own_low, "height", [(i, i + 1) for i in range(heights - 1)])

    fields, table, masks, starts = kernel(
        inner_kernel,
        "inner",
        (
            array(4, SLABS * TALL, COLS),
            array(16, COLS),
            array(5, 8, COLS),
            jax.ShapeDtypeStruct((64,), jnp.int32),
        ),
        [HBM] * 5 + [VMEM],
        (VMEM, VMEM, VMEM, SMEM),
        flops=10**7,
        scratch_shapes=[pltpu.SMEM((3,), jnp.float32)] * 3
        + [pltpu.SMEM((VIEWS,), jnp.int32)] * 2
        + [pltpu.SemaphoreType.DMA((5,))],
    )(light_vector, colour_gain, colour_bias, shear_step, reverse_view, own)

    brick, first = kernel(
        join_kernel, "join", (array(PLANES, PADDED, COLS), array(2, PADDED, COLS)), [VMEM] * 4, (VMEM,) * 2
    )(own, low, high, table)
    coming = lax.ppermute(first, "depth", [(i + 1, i) for i in range(depths - 1)])

    fields = kernel(
        edge_kernel,
        "edge",
        array(4, SLABS * TALL, COLS),
        [VMEM] * 3,
        VMEM,
        flops=10**7,
        input_output_aliases={2: 0},
    )(table, brick, fields)

    part = array(CHIPS, 4, VIEWS // 2, 8, COLS)
    given, kept, _ = kernel(
        render_kernel,
        "render",
        (part, part, array(4, SLABS * TALL, COLS)),
        [VMEM, VMEM, ANY, VMEM, VMEM, VMEM],
        (VMEM,) * 3,
        input_output_aliases={5: 2},
        scratch_shapes=[pltpu.SMEM((64,), jnp.int32), pltpu.SemaphoreType.DMA],
    )(table, masks, starts, brick, coming, fields)

    cores = [[2 * chip, 2 * chip + 1] for chip in range(CHIPS)]
    gathered = lax.all_gather(given, "depth", axis=0, axis_index_groups=cores)
    merged = kernel(merge_kernel, "merge", part, [VMEM] * 3, VMEM)(masks, kept, gathered)
    chips = [[core + 2 * chip for chip in range(CHIPS)] for core in range(2)]
    slabs = lax.all_to_all(merged, "depth", 0, 0, tiled=True, axis_index_groups=chips)
    return kernel(final_kernel, "composite", array(4, VIEWS, SHARE, COLS), [VMEM] * 2, VMEM)(masks, slabs)


def solution(mesh):
    placed = (P("depth", "height", None), P(), P(), P(), P(), P())
    return jax.shard_map(
        on_device,
        mesh=mesh,
        in_specs=placed,
        out_specs=P(None, None, ("height", "depth"), None),
        check_vma=False,
    )
```

```python
import jax
import jax.numpy as jnp
from jax import lax
from jax.experimental import pallas as pl
from jax.experimental.pallas import tpu as pltpu
from jax.sharding import PartitionSpec as P

EXTINCTION = 2.5
SMEM = pl.BlockSpec(memory_space=pltpu.SMEM)
VMEM = pl.BlockSpec(memory_space=pltpu.VMEM)
ANY = pl.BlockSpec(memory_space=pl.ANY)
HBM = pl.BlockSpec(memory_space=pltpu.HBM)
PLANES, ROWS, COLS, SHEAR, VIEWS, GROUPS, BRICKS = 8, 64, 128, 32, 4, 16, 32
TOP = 8
TALL = ROWS + SHEAR
PADDED = TOP + TALL + 8
SLABS = PLANES + 1
CHIPS = GROUPS // 2
SHARE = ROWS // GROUPS
PARAMS = pltpu.CompilerParams(vmem_limit_bytes=8 * 2**20)
LIGHT, GAIN, BIAS, PLAIN, BEYOND, NEXT, NEXT_BEYOND = 0, 3, 6, 9, 10, 11, 12
FRONT, BACK, CORE = 0, 2, 4
FIRST = VIEWS * SLABS


def array(*shape):
    return jax.ShapeDtypeStruct(shape, jnp.float32)


def opacity_of(optical):
    series = 1.0 - optical * (1.0 / 6.0)
    for term in (5.0, 4.0, 3.0, 2.0):
        series = 1.0 - optical * (1.0 / term) * series
    return optical * series


def shade(coefficient, extinction, centre, above, below, before, after):
    lane = lax.broadcasted_iota(jnp.int32, centre.shape, 1)
    tilt_rows = 0.5 * (below - above)
    tilt_depth = 0.5 * (after - before)
    right = jnp.where(lane == COLS - 1, 0.0, pltpu.roll(centre, COLS - 1, 1))
    left = jnp.where(lane == 0, 0.0, pltpu.roll(centre, 1, 1))
    tilt_cols = 0.5 * (right - left)
    slope = coefficient(LIGHT) * tilt_depth + coefficient(LIGHT + 1) * tilt_rows + coefficient(LIGHT + 2) * tilt_cols
    facing = slope * lax.rsqrt(1.0 + tilt_depth * tilt_depth + tilt_rows * tilt_rows + tilt_cols * tilt_cols)
    shading = 0.25 + 1.5 * jnp.maximum(facing, 0.0)
    optical = extinction * (jnp.maximum(centre, 0.0) + jnp.log1p(jnp.exp(-jnp.abs(centre))))
    strength = opacity_of(optical) * shading
    tones = [jax.nn.sigmoid(coefficient(GAIN + i) * centre + coefficient(BIAS + i)) for i in range(3)]
    return [strength * tone for tone in tones] + [optical]


def load_kernel(density, own, low, semaphore):
    copy = pltpu.make_async_copy(density, own, semaphore)
    copy.start()
    copy.wait()
    for plane in range(PLANES):
        low[plane : plane + 1, :] = own[plane, ROWS - 1 : ROWS, :]


def table_kernel(*refs):
    arguments, (table, masks, starts), scalars, semaphores = refs[:5], refs[5:8], refs[8:13], refs[13]
    copies = [pltpu.make_async_copy(arguments[i], scalars[i], semaphores.at[i]) for i in range(5)]
    for copy in copies:
        copy.start()
    depth, height = lax.axis_index("depth"), lax.axis_index("height")
    for copy in copies:
        copy.wait()
    light, gain, bias, shear, reverse = scalars
    extinction = EXTINCTION / (PLANES * GROUPS)
    beyond = jnp.where(height == BRICKS - 1, 0.0, extinction)
    following = jnp.where(depth == GROUPS - 1, 0.0, extinction)
    both = jnp.where(depth == GROUPS - 1, 0.0, beyond)
    values = [ref[i] for ref in (light, gain, bias) for i in range(3)] + [extinction, beyond, following, both]
    for row, value in enumerate(values):
        table[row : row + 1, :] = jnp.full((1, COLS), value, jnp.float32)
    upper = lax.broadcasted_iota(jnp.int32, (8, COLS), 0) < SHARE
    core = depth % 2
    for base, digit in ((FRONT, core), (BACK, 1)):
        for pair in range(VIEWS // 2):
            first = jnp.where(reverse[2 * pair] == digit, 1.0, 0.0)
            second = jnp.where(reverse[2 * pair + 1] == digit, 1.0, 0.0)
            masks[base + pair] = jnp.where(upper, first, second)
    masks[CORE] = jnp.full((8, COLS), core, jnp.float32)
    first = jnp.where(depth == 0, 0, 1)
    starts[FIRST] = first
    for view in range(VIEWS):
        for step in range(SLABS):
            slot = jnp.where(reverse[view] == 1, SLABS - 1 - step, jnp.minimum(first + step, SLABS - 1))
            offset = lax.shift_right_logical((depth * PLANES + slot) * shear[view], 7)
            starts[view * SLABS + step] = slot * TALL + jnp.minimum(offset, SHEAR)


def cut_kernel(own, low, table, high):
    del low, table
    high[...] = own[:, :SHEAR, :]


def inner_kernel(table, own, low, fields):
    top = lax.broadcasted_iota(jnp.int32, (8, COLS), 0) == 0

    def plane_of(step, _):
        plane = step + 1
        for inner, above in (
            (slice(0, 8), jnp.where(top, low[pl.ds(plane, 1), :], pltpu.roll(own[plane, :8, :], 1, 0))),
            (slice(8, ROWS - 8), own[plane, 7 : ROWS - 9, :]),
        ):
            values = shade(
                lambda at: table[at : at + 1, :],
                table[PLAIN : PLAIN + 1, :],
                own[plane, inner, :],
                above,
                own[plane, inner.start + 1 : inner.stop + 1, :],
                own[plane - 1, inner, :],
                own[plane + 1, inner, :],
            )
            rows = pl.ds(pl.multiple_of(plane * TALL + inner.start, 8), inner.stop - inner.start)
            for kind in range(4):
                fields[kind, rows, :] = values[kind]
        return 0

    lax.fori_loop(0, PLANES - 2, plane_of, 0)


def join_kernel(own, low, high, held, brick, first):
    del held
    for plane in range(PLANES):
        parts = (
            (0, jnp.broadcast_to(low[plane : plane + 1, :], (8, COLS))),
            (TOP, own[plane]),
            (TOP + ROWS, high[plane]),
            (TOP + TALL, jnp.zeros((8, COLS), jnp.float32)),
        )
        for start, part in parts:
            brick[plane, start : start + part.shape[0], :] = part
            if plane < 2:
                first[plane, start : start + part.shape[0], :] = part


def shade_rows(table, extinction, row, count, plane, before, after, fields, slot):
    start = row + TOP
    values = shade(
        lambda at: table[at : at + 1, :],
        table[extinction : extinction + 1, :],
        plane[start : start + count, :],
        plane[start - 1 : start - 1 + count, :],
        plane[start + 1 : start + 1 + count, :],
        0.0 if before is None else before[start : start + count, :],
        after[start : start + count, :],
    )
    rows = pl.ds(pl.multiple_of(slot * TALL + row, 8), count)
    for kind in range(4):
        fields[kind, rows, :] = values[kind]


def edge_kernel(table, brick, held, fields):
    del held

    def plane_of(step, _):
        plane = step + 1
        refs = (brick.at[plane], brick.at[plane - 1], brick.at[plane + 1], fields, plane)
        shade_rows(table, PLAIN, ROWS - 8, 8, *refs)
        shade_rows(table, BEYOND, ROWS, SHEAR, *refs)
        return 0

    lax.fori_loop(0, PLANES - 2, plane_of, 0)


def render_kernel(table, masks, starts_in, brick, coming, held, given, kept, fields, starts, semaphore):
    del held
    copy = pltpu.make_async_copy(starts_in, starts, semaphore)
    copy.start()

    def whole_plane(slot, plane, before, after, own, beyond):
        refs = (plane, before, after, fields, slot)
        shade_rows(table, own, 0, SHEAR, *refs)
        shade_rows(table, own, SHEAR, SHEAR, *refs)
        shade_rows(table, beyond, ROWS, SHEAR, *refs)

    whole_plane(PLANES - 1, brick.at[PLANES - 1], brick.at[PLANES - 2], coming.at[0], PLAIN, BEYOND)
    whole_plane(PLANES, coming.at[0], brick.at[PLANES - 1], coming.at[1], NEXT, NEXT_BEYOND)
    copy.wait()
    leading = starts[FIRST] == 0

    @pl.when(leading)
    def _():
        whole_plane(0, brick.at[0], None, brick.at[1], PLAIN, BEYOND)

    def render(planes):
        upper = lax.broadcasted_iota(jnp.int32, (8, COLS), 0) < SHARE
        odd = masks[CORE] > 0.5

        def tile_of(tile, _):
            for pair in range(VIEWS // 2):
                sums = []
                for view in (2 * pair, 2 * pair + 1):
                    red = green = blue = optical = jnp.zeros((8, COLS), jnp.float32)
                    for step in range(planes):
                        rows = pl.ds(starts[view * SLABS + step] + 8 * tile, 8)
                        through = jnp.exp(-optical)
                        red = red + fields[0, rows, :] * through
                        green = green + fields[1, rows, :] * through
                        blue = blue + fields[2, rows, :] * through
                        optical = optical + fields[3, rows, :]
                    sums.append((red, green, blue, optical))
                for kind in range(4):
                    first, second = sums[0][kind], sums[1][kind]
                    even_rows = jnp.where(upper, first, pltpu.roll(second, SHARE, 0))
                    odd_rows = jnp.where(upper, pltpu.roll(first, SHARE, 0), second)
                    kept[tile, kind, pair] = jnp.where(odd, odd_rows, even_rows)
                    given[tile, kind, pair] = jnp.where(odd, even_rows, odd_rows)
            return 0

        lax.fori_loop(0, ROWS // 8, tile_of, 0)

    @pl.when(leading)
    def _():
        render(SLABS)

    @pl.when(jnp.logical_not(leading))
    def _():
        render(PLANES)


def merge_kernel(masks, kept, gathered, out):
    odd = masks[CORE] > 0.5
    for pair in range(VIEWS // 2):
        mine_front = masks[FRONT + pair] > 0.5

        def merge(chip, _):
            mine = [kept[chip, kind, pair] for kind in range(4)]
            other = [jnp.where(odd, gathered[0, chip, kind, pair], gathered[1, chip, kind, pair]) for kind in range(4)]
            through = jnp.exp(-jnp.where(mine_front, mine[3], other[3]))
            for kind in range(3):
                front = jnp.where(mine_front, mine[kind], other[kind])
                behind = jnp.where(mine_front, other[kind], mine[kind])
                out[chip, kind, pair] = front + through * behind
            out[chip, 3, pair] = mine[3] + other[3]
            return 0

        lax.fori_loop(0, CHIPS, merge, 0, unroll=True)


def final_kernel(masks, slabs, out):
    for pair in range(VIEWS // 2):
        backward = masks[BACK + pair] > 0.5
        optical = [slabs[chip, 3, pair] for chip in range(CHIPS)]
        ahead, behind = [jnp.zeros((8, COLS), jnp.float32)], [jnp.zeros((8, COLS), jnp.float32)]
        for chip in range(CHIPS - 1):
            ahead.append(ahead[-1] + optical[chip])
            behind.append(behind[-1] + optical[CHIPS - 1 - chip])
        total = ahead[-1] + optical[-1]
        sums = [jnp.zeros((8, COLS), jnp.float32)] * 3
        for chip in range(CHIPS):
            through = jnp.exp(-jnp.where(backward, behind[CHIPS - 1 - chip], ahead[chip]))
            sums = [sums[kind] + slabs[chip, kind, pair] * through for kind in range(3)]
        cover = jnp.where(total < 0.0625, opacity_of(total), 1.0 - jnp.exp(-total))
        for kind, value in enumerate((*sums, cover)):
            out[kind, 2 * pair] = value[:SHARE]
            out[kind, 2 * pair + 1] = value[SHARE:]


def kernel(body, name, out_shape, in_specs, out_specs, flops=0, **more):
    estimate = pl.CostEstimate(flops=flops, bytes_accessed=2**20, transcendentals=0)
    return pl.pallas_call(
        body,
        out_shape=out_shape,
        in_specs=in_specs,
        out_specs=out_specs,
        compiler_params=PARAMS,
        cost_estimate=estimate,
        name=name,
        **more,
    )


def on_device(density, light_vector, colour_gain, colour_bias, shear_step, reverse_view):
    heights, depths = lax.axis_size("height"), lax.axis_size("depth")

    own, own_low = kernel(
        load_kernel,
        "load",
        (array(PLANES, ROWS, COLS), array(PLANES, COLS)),
        [HBM],
        (VMEM,) * 2,
        flops=10**9,
        scratch_shapes=[pltpu.SemaphoreType.DMA],
    )(density)
    low = lax.ppermute(own_low, "height", [(i, i + 1) for i in range(heights - 1)])
    table, masks, starts = kernel(
        table_kernel,
        "table",
        (array(16, COLS), array(5, 8, COLS), jax.ShapeDtypeStruct((64,), jnp.int32)),
        [HBM] * 5,
        (VMEM, VMEM, SMEM),
        flops=10**7,
        scratch_shapes=[pltpu.SMEM((3,), jnp.float32)] * 3
        + [pltpu.SMEM((VIEWS,), jnp.int32)] * 2
        + [pltpu.SemaphoreType.DMA((5,))],
    )(light_vector, colour_gain, colour_bias, shear_step, reverse_view)
    own_high = kernel(cut_kernel, "cut", array(PLANES, SHEAR, COLS), [VMEM] * 3, VMEM)(own, low, table)
    high = lax.ppermute(own_high, "height", [(i + 1, i) for i in range(heights - 1)])
    fields = kernel(
        inner_kernel, "inner", array(4, SLABS * TALL, COLS), [VMEM] * 3, VMEM, flops=10**7
    )(table, own, low)

    brick, first = kernel(
        join_kernel, "join", (array(PLANES, PADDED, COLS), array(2, PADDED, COLS)), [VMEM] * 4, (VMEM,) * 2
    )(own, low, high, fields)
    coming = lax.ppermute(first, "depth", [(i + 1, i) for i in range(depths - 1)])

    fields = kernel(
        edge_kernel,
        "edge",
        array(4, SLABS * TALL, COLS),
        [VMEM] * 3,
        VMEM,
        flops=10**7,
        input_output_aliases={2: 0},
    )(table, brick, fields)

    part = array(CHIPS, 4, VIEWS // 2, 8, COLS)
    given, kept, _ = kernel(
        render_kernel,
        "render",
        (part, part, array(4, SLABS * TALL, COLS)),
        [VMEM, VMEM, ANY, VMEM, VMEM, VMEM],
        (VMEM,) * 3,
        input_output_aliases={5: 2},
        scratch_shapes=[pltpu.SMEM((64,), jnp.int32), pltpu.SemaphoreType.DMA],
    )(table, masks, starts, brick, coming, fields)

    cores = [[2 * chip, 2 * chip + 1] for chip in range(CHIPS)]
    gathered = lax.all_gather(given, "depth", axis=0, axis_index_groups=cores)
    merged = kernel(merge_kernel, "merge", part, [VMEM] * 3, VMEM)(masks, kept, gathered)
    chips = [[core + 2 * chip for chip in range(CHIPS)] for core in range(2)]
    slabs = lax.all_to_all(merged, "depth", 0, 0, tiled=True, axis_index_groups=chips)
    return kernel(final_kernel, "composite", array(4, VIEWS, SHARE, COLS), [VMEM] * 2, VMEM)(masks, slabs)


def solution(mesh):
    placed = (P("depth", "height", None), P(), P(), P(), P(), P())
    return jax.shard_map(
        on_device,
        mesh=mesh,
        in_specs=placed,
        out_specs=P(None, None, ("height", "depth"), None),
        check_vma=False,
    )
```

```python
import jax
import jax.numpy as jnp
from jax import lax
from jax.experimental import pallas as pl
from jax.experimental.pallas import tpu as pltpu
from jax.sharding import PartitionSpec as P

EXTINCTION = 2.5
SMEM = pl.BlockSpec(memory_space=pltpu.SMEM)
VMEM = pl.BlockSpec(memory_space=pltpu.VMEM)
ANY = pl.BlockSpec(memory_space=pl.ANY)
HBM = pl.BlockSpec(memory_space=pltpu.HBM)
PLANES, ROWS, COLS, SHEAR, VIEWS, GROUPS, BRICKS = 8, 64, 128, 32, 4, 16, 32
TOP = 8
TALL = ROWS + SHEAR
PADDED = TOP + TALL + 8
SLABS = PLANES + 1
CHIPS = GROUPS // 2
SHARE = ROWS // GROUPS
PARAMS = pltpu.CompilerParams(vmem_limit_bytes=8 * 2**20)
LIGHT, GAIN, BIAS, PLAIN, BEYOND, NEXT, NEXT_BEYOND = 0, 3, 6, 9, 10, 11, 12
FRONT, BACK, CORE = 0, 2, 4
FIRST = VIEWS * SLABS


def array(*shape):
    return jax.ShapeDtypeStruct(shape, jnp.float32)


def opacity_of(optical):
    series = 1.0 - optical * (1.0 / 6.0)
    for term in (5.0, 4.0, 3.0, 2.0):
        series = 1.0 - optical * (1.0 / term) * series
    return optical * series


def shade(coefficient, extinction, centre, above, below, before, after):
    lane = lax.broadcasted_iota(jnp.int32, centre.shape, 1)
    tilt_rows = 0.5 * (below - above)
    tilt_depth = 0.5 * (after - before)
    right = jnp.where(lane == COLS - 1, 0.0, pltpu.roll(centre, COLS - 1, 1))
    left = jnp.where(lane == 0, 0.0, pltpu.roll(centre, 1, 1))
    tilt_cols = 0.5 * (right - left)
    slope = coefficient(LIGHT) * tilt_depth + coefficient(LIGHT + 1) * tilt_rows + coefficient(LIGHT + 2) * tilt_cols
    facing = slope * lax.rsqrt(1.0 + tilt_depth * tilt_depth + tilt_rows * tilt_rows + tilt_cols * tilt_cols)
    shading = 0.25 + 1.5 * jnp.maximum(facing, 0.0)
    optical = extinction * (jnp.maximum(centre, 0.0) + jnp.log1p(jnp.exp(-jnp.abs(centre))))
    strength = opacity_of(optical) * shading
    tones = [jax.nn.sigmoid(coefficient(GAIN + i) * centre + coefficient(BIAS + i)) for i in range(3)]
    return [strength * tone for tone in tones] + [optical]


def load_kernel(density, own, low, high, semaphore):
    copy = pltpu.make_async_copy(density, own, semaphore)
    copy.start()
    copy.wait()
    high[...] = own[:, :SHEAR, :]
    for plane in range(PLANES):
        low[plane : plane + 1, :] = own[plane, ROWS - 1 : ROWS, :]


def inner_kernel(*refs):
    arguments, (own, low, fields, table, masks, starts), scalars, semaphores = refs[:5], refs[5:11], refs[11:16], refs[16]
    copies = [pltpu.make_async_copy(arguments[i], scalars[i], semaphores.at[i]) for i in range(5)]
    for copy in copies:
        copy.start()
    depth, height = lax.axis_index("depth"), lax.axis_index("height")
    for copy in copies:
        copy.wait()
    light, gain, bias, shear, reverse = scalars
    extinction = EXTINCTION / (PLANES * GROUPS)
    beyond = jnp.where(height == BRICKS - 1, 0.0, extinction)
    following = jnp.where(depth == GROUPS - 1, 0.0, extinction)
    both = jnp.where(depth == GROUPS - 1, 0.0, beyond)
    values_of = [ref[i] for ref in (light, gain, bias) for i in range(3)] + [extinction, beyond, following, both]
    for row, scalar in enumerate(values_of):
        table[row : row + 1, :] = jnp.full((1, COLS), scalar, jnp.float32)
    upper = lax.broadcasted_iota(jnp.int32, (8, COLS), 0) < SHARE
    core = depth % 2
    for base, digit in ((FRONT, core), (BACK, 1)):
        for pair in range(VIEWS // 2):
            first = jnp.where(reverse[2 * pair] == digit, 1.0, 0.0)
            second = jnp.where(reverse[2 * pair + 1] == digit, 1.0, 0.0)
            masks[base + pair] = jnp.where(upper, first, second)
    masks[CORE] = jnp.full((8, COLS), core, jnp.float32)
    first = jnp.where(depth == 0, 0, 1)
    starts[FIRST] = first
    for view in range(VIEWS):
        for step in range(SLABS):
            slot = jnp.where(reverse[view] == 1, SLABS - 1 - step, jnp.minimum(first + step, SLABS - 1))
            offset = lax.shift_right_logical((depth * PLANES + slot) * shear[view], 7)
            starts[view * SLABS + step] = slot * TALL + jnp.minimum(offset, SHEAR)

    def plane_of(step, _):
        plane = step + 1
        for inner, above in (
            (slice(0, 8), jnp.where(top, low[pl.ds(plane, 1), :], pltpu.roll(own[plane, :8, :], 1, 0))),
            (slice(8, ROWS - 8), own[plane, 7 : ROWS - 9, :]),
        ):
            values = shade(
                lambda row: values_of[row],
                extinction,
                own[plane, inner, :],
                above,
                own[plane, inner.start + 1 : inner.stop + 1, :],
                own[plane - 1, inner, :],
                own[plane + 1, inner, :],
            )
            rows = pl.ds(pl.multiple_of(plane * TALL + inner.start, 8), inner.stop - inner.start)
            for kind in range(4):
                fields[kind, rows, :] = values[kind]
        return 0

    top = lax.broadcasted_iota(jnp.int32, (8, COLS), 0) == 0

    lax.fori_loop(0, PLANES - 2, plane_of, 0)


def join_kernel(own, low, high, table, brick, first):
    del table
    for plane in range(PLANES):
        parts = (
            (0, jnp.broadcast_to(low[plane : plane + 1, :], (8, COLS))),
            (TOP, own[plane]),
            (TOP + ROWS, high[plane]),
            (TOP + TALL, jnp.zeros((8, COLS), jnp.float32)),
        )
        for start, part in parts:
            brick[plane, start : start + part.shape[0], :] = part
            if plane < 2:
                first[plane, start : start + part.shape[0], :] = part


def shade_rows(table, extinction, row, count, plane, before, after, fields, slot):
    start = row + TOP
    values = shade(
        lambda at: table[at : at + 1, :],
        table[extinction : extinction + 1, :],
        plane[start : start + count, :],
        plane[start - 1 : start - 1 + count, :],
        plane[start + 1 : start + 1 + count, :],
        0.0 if before is None else before[start : start + count, :],
        after[start : start + count, :],
    )
    rows = pl.ds(pl.multiple_of(slot * TALL + row, 8), count)
    for kind in range(4):
        fields[kind, rows, :] = values[kind]


def edge_kernel(table, brick, held, fields):
    del held

    def plane_of(step, _):
        plane = step + 1
        refs = (brick.at[plane], brick.at[plane - 1], brick.at[plane + 1], fields, plane)
        shade_rows(table, PLAIN, ROWS - 8, 8, *refs)
        shade_rows(table, BEYOND, ROWS, SHEAR, *refs)
        return 0

    lax.fori_loop(0, PLANES - 2, plane_of, 0)


def render_kernel(table, masks, starts_in, brick, coming, held, given, kept, fields, starts, semaphore):
    del held
    copy = pltpu.make_async_copy(starts_in, starts, semaphore)
    copy.start()

    def whole_plane(slot, plane, before, after, own, beyond):
        refs = (plane, before, after, fields, slot)
        shade_rows(table, own, 0, SHEAR, *refs)
        shade_rows(table, own, SHEAR, SHEAR, *refs)
        shade_rows(table, beyond, ROWS, SHEAR, *refs)

    whole_plane(PLANES - 1, brick.at[PLANES - 1], brick.at[PLANES - 2], coming.at[0], PLAIN, BEYOND)
    whole_plane(PLANES, coming.at[0], brick.at[PLANES - 1], coming.at[1], NEXT, NEXT_BEYOND)
    copy.wait()
    leading = starts[FIRST] == 0

    @pl.when(leading)
    def _():
        whole_plane(0, brick.at[0], None, brick.at[1], PLAIN, BEYOND)

    def render(planes):
        upper = lax.broadcasted_iota(jnp.int32, (8, COLS), 0) < SHARE
        odd = masks[CORE] > 0.5

        def tile_of(tile, _):
            for pair in range(VIEWS // 2):
                sums = []
                for view in (2 * pair, 2 * pair + 1):
                    red = green = blue = optical = jnp.zeros((8, COLS), jnp.float32)
                    for step in range(planes):
                        rows = pl.ds(starts[view * SLABS + step] + 8 * tile, 8)
                        through = jnp.exp(-optical)
                        red = red + fields[0, rows, :] * through
                        green = green + fields[1, rows, :] * through
                        blue = blue + fields[2, rows, :] * through
                        optical = optical + fields[3, rows, :]
                    sums.append((red, green, blue, optical))
                for kind in range(4):
                    first, second = sums[0][kind], sums[1][kind]
                    even_rows = jnp.where(upper, first, pltpu.roll(second, SHARE, 0))
                    odd_rows = jnp.where(upper, pltpu.roll(first, SHARE, 0), second)
                    kept[tile, kind, pair] = jnp.where(odd, odd_rows, even_rows)
                    given[tile, kind, pair] = jnp.where(odd, even_rows, odd_rows)
            return 0

        lax.fori_loop(0, ROWS // 8, tile_of, 0)

    @pl.when(leading)
    def _():
        render(SLABS)

    @pl.when(jnp.logical_not(leading))
    def _():
        render(PLANES)


def merge_kernel(masks, kept, gathered, out):
    odd = masks[CORE] > 0.5
    for pair in range(VIEWS // 2):
        mine_front = masks[FRONT + pair] > 0.5

        def merge(chip, _):
            mine = [kept[chip, kind, pair] for kind in range(4)]
            other = [jnp.where(odd, gathered[0, chip, kind, pair], gathered[1, chip, kind, pair]) for kind in range(4)]
            through = jnp.exp(-jnp.where(mine_front, mine[3], other[3]))
            for kind in range(3):
                front = jnp.where(mine_front, mine[kind], other[kind])
                behind = jnp.where(mine_front, other[kind], mine[kind])
                out[chip, kind, pair] = front + through * behind
            out[chip, 3, pair] = mine[3] + other[3]
            return 0

        lax.fori_loop(0, CHIPS, merge, 0, unroll=True)


def final_kernel(masks, slabs, out):
    for pair in range(VIEWS // 2):
        backward = masks[BACK + pair] > 0.5
        optical = [slabs[chip, 3, pair] for chip in range(CHIPS)]
        ahead, behind = [jnp.zeros((8, COLS), jnp.float32)], [jnp.zeros((8, COLS), jnp.float32)]
        for chip in range(CHIPS - 1):
            ahead.append(ahead[-1] + optical[chip])
            behind.append(behind[-1] + optical[CHIPS - 1 - chip])
        total = ahead[-1] + optical[-1]
        sums = [jnp.zeros((8, COLS), jnp.float32)] * 3
        for chip in range(CHIPS):
            through = jnp.exp(-jnp.where(backward, behind[CHIPS - 1 - chip], ahead[chip]))
            sums = [sums[kind] + slabs[chip, kind, pair] * through for kind in range(3)]
        cover = jnp.where(total < 0.0625, opacity_of(total), 1.0 - jnp.exp(-total))
        for kind, value in enumerate((*sums, cover)):
            out[kind, 2 * pair] = value[:SHARE]
            out[kind, 2 * pair + 1] = value[SHARE:]


def kernel(body, name, out_shape, in_specs, out_specs, flops=0, **more):
    estimate = pl.CostEstimate(flops=flops, bytes_accessed=2**20, transcendentals=0)
    return pl.pallas_call(
        body,
        out_shape=out_shape,
        in_specs=in_specs,
        out_specs=out_specs,
        compiler_params=PARAMS,
        cost_estimate=estimate,
        name=name,
        **more,
    )


def on_device(density, light_vector, colour_gain, colour_bias, shear_step, reverse_view):
    heights, depths = lax.axis_size("height"), lax.axis_size("depth")

    own, own_low, own_high = kernel(
        load_kernel,
        "load",
        (array(PLANES, ROWS, COLS), array(PLANES, COLS), array(PLANES, SHEAR, COLS)),
        [HBM],
        (VMEM,) * 3,
        flops=10**9,
        scratch_shapes=[pltpu.SemaphoreType.DMA],
    )(density)
    high = lax.ppermute(own_high, "height", [(i + 1, i) for i in range(heights - 1)])
    low = lax.ppermute(own_low, "height", [(i, i + 1) for i in range(heights - 1)])

    fields, table, masks, starts = kernel(
        inner_kernel,
        "inner",
        (
            array(4, SLABS * TALL, COLS),
            array(16, COLS),
            array(5, 8, COLS),
            jax.ShapeDtypeStruct((64,), jnp.int32),
        ),
        [HBM] * 5 + [VMEM] * 2,
        (VMEM, VMEM, VMEM, SMEM),
        flops=10**11,
        scratch_shapes=[pltpu.SMEM((3,), jnp.float32)] * 3
        + [pltpu.SMEM((VIEWS,), jnp.int32)] * 2
        + [pltpu.SemaphoreType.DMA((5,))],
    )(light_vector, colour_gain, colour_bias, shear_step, reverse_view, own, low)

    brick, first = kernel(
        join_kernel, "join", (array(PLANES, PADDED, COLS), array(2, PADDED, COLS)), [VMEM] * 4, (VMEM,) * 2
    )(own, low, high, table)
    coming = lax.ppermute(first, "depth", [(i + 1, i) for i in range(depths - 1)])

    fields = kernel(
        edge_kernel,
        "edge",
        array(4, SLABS * TALL, COLS),
        [VMEM] * 3,
        VMEM,
        flops=10**7,
        input_output_aliases={2: 0},
    )(table, brick, fields)

    part = array(CHIPS, 4, VIEWS // 2, 8, COLS)
    given, kept, _ = kernel(
        render_kernel,
        "render",
        (part, part, array(4, SLABS * TALL, COLS)),
        [VMEM, VMEM, ANY, VMEM, VMEM, VMEM],
        (VMEM,) * 3,
        input_output_aliases={5: 2},
        scratch_shapes=[pltpu.SMEM((64,), jnp.int32), pltpu.SemaphoreType.DMA],
    )(table, masks, starts, brick, coming, fields)

    cores = [[2 * chip, 2 * chip + 1] for chip in range(CHIPS)]
    gathered = lax.all_gather(given, "depth", axis=0, axis_index_groups=cores)
    merged = kernel(merge_kernel, "merge", part, [VMEM] * 3, VMEM)(masks, kept, gathered)
    chips = [[core + 2 * chip for chip in range(CHIPS)] for core in range(2)]
    slabs = lax.all_to_all(merged, "depth", 0, 0, tiled=True, axis_index_groups=chips)
    return kernel(final_kernel, "composite", array(4, VIEWS, SHARE, COLS), [VMEM] * 2, VMEM)(masks, slabs)


def solution(mesh):
    placed = (P("depth", "height", None), P(), P(), P(), P(), P())
    return jax.shard_map(
        on_device,
        mesh=mesh,
        in_specs=placed,
        out_specs=P(None, None, ("height", "depth"), None),
        check_vma=False,
    )
```

```python
import jax
import jax.numpy as jnp
from jax import lax
from jax.experimental import pallas as pl
from jax.experimental.pallas import tpu as pltpu
from jax.sharding import PartitionSpec as P

EXTINCTION = 2.5
SMEM = pl.BlockSpec(memory_space=pltpu.SMEM)
VMEM = pl.BlockSpec(memory_space=pltpu.VMEM)
ANY = pl.BlockSpec(memory_space=pl.ANY)
HBM = pl.BlockSpec(memory_space=pltpu.HBM)
PLANES, ROWS, COLS, SHEAR, VIEWS, GROUPS, BRICKS = 8, 64, 128, 32, 4, 16, 32
TALL = ROWS + SHEAR
SLABS = PLANES + 1
CHIPS = GROUPS // 2
SHARE = ROWS // GROUPS
PARAMS = pltpu.CompilerParams(vmem_limit_bytes=8 * 2**20)
LIGHT, GAIN, BIAS, PLAIN, BEYOND, NEXT, NEXT_BEYOND = 0, 3, 6, 9, 10, 11, 12
FRONT, BACK, CORE = 0, 2, 4
INNER = slice(8, ROWS - 8)
FIRST = VIEWS * SLABS


def array(*shape):
    return jax.ShapeDtypeStruct(shape, jnp.float32)


def opacity_of(optical):
    series = 1.0 - optical * (1.0 / 6.0)
    for term in (5.0, 4.0, 3.0, 2.0):
        series = 1.0 - optical * (1.0 / term) * series
    return optical * series


def shade(coefficient, extinction, centre, above, below, before, after):
    lane = lax.broadcasted_iota(jnp.int32, centre.shape, 1)
    tilt_rows = 0.5 * (below - above)
    tilt_depth = 0.5 * (after - before)
    right = jnp.where(lane == COLS - 1, 0.0, pltpu.roll(centre, COLS - 1, 1))
    left = jnp.where(lane == 0, 0.0, pltpu.roll(centre, 1, 1))
    tilt_cols = 0.5 * (right - left)
    slope = coefficient(LIGHT) * tilt_depth + coefficient(LIGHT + 1) * tilt_rows + coefficient(LIGHT + 2) * tilt_cols
    facing = slope * lax.rsqrt(1.0 + tilt_depth * tilt_depth + tilt_rows * tilt_rows + tilt_cols * tilt_cols)
    shading = 0.25 + 1.5 * jnp.maximum(facing, 0.0)
    optical = extinction * (jnp.maximum(centre, 0.0) + jnp.log1p(jnp.exp(-jnp.abs(centre))))
    strength = opacity_of(optical) * shading
    tones = [jax.nn.sigmoid(coefficient(GAIN + i) * centre + coefficient(BIAS + i)) for i in range(3)]
    return [strength * tone for tone in tones] + [optical]


def load_kernel(density, own, first, semaphore):
    copy = pltpu.make_async_copy(density, own, semaphore)
    copy.start()
    copy.wait()
    first[...] = own[:2]


def inner_kernel(*refs):
    arguments, (own, fields, table, masks, starts), scalars, semaphores = refs[:5], refs[5:10], refs[10:15], refs[15]
    copies = [pltpu.make_async_copy(arguments[i], scalars[i], semaphores.at[i]) for i in range(5)]
    for copy in copies:
        copy.start()
    depth, height = lax.axis_index("depth"), lax.axis_index("height")
    for copy in copies:
        copy.wait()
    light, gain, bias, shear, reverse = scalars
    extinction = EXTINCTION / (PLANES * GROUPS)
    beyond = jnp.where(height == BRICKS - 1, 0.0, extinction)
    following = jnp.where(depth == GROUPS - 1, 0.0, extinction)
    both = jnp.where(depth == GROUPS - 1, 0.0, beyond)
    values_of = [ref[i] for ref in (light, gain, bias) for i in range(3)] + [extinction, beyond, following, both]
    for row, scalar in enumerate(values_of):
        table[row : row + 1, :] = jnp.full((1, COLS), scalar, jnp.float32)
    upper = lax.broadcasted_iota(jnp.int32, (8, COLS), 0) < SHARE
    core = depth % 2
    for base, digit in ((FRONT, core), (BACK, 1)):
        for pair in range(VIEWS // 2):
            first = jnp.where(reverse[2 * pair] == digit, 1.0, 0.0)
            second = jnp.where(reverse[2 * pair + 1] == digit, 1.0, 0.0)
            masks[base + pair] = jnp.where(upper, first, second)
    masks[CORE] = jnp.full((8, COLS), core, jnp.float32)
    first = jnp.where(depth == 0, 0, 1)
    starts[FIRST] = first
    for view in range(VIEWS):
        for step in range(SLABS):
            slot = jnp.where(reverse[view] == 1, SLABS - 1 - step, jnp.minimum(first + step, SLABS - 1))
            offset = lax.shift_right_logical((depth * PLANES + slot) * shear[view], 7)
            starts[view * SLABS + step] = slot * TALL + jnp.minimum(offset, SHEAR)

    coefficient = lambda at: values_of[at]

    def plane_of(plane, _):
        shade_inner(coefficient, extinction, own.at[plane], own[plane - 1, INNER, :], own[plane + 1, INNER, :], fields, plane)
        return 0

    lax.fori_loop(1, PLANES - 1, plane_of, 0)

    @pl.when(depth == 0)
    def _():
        shade_inner(coefficient, extinction, own.at[0], 0.0, own[1, INNER, :], fields, 0)


def shade_inner(coefficient, extinction, plane, before, after, fields, slot):
    centre = plane[INNER, :]
    values = shade(coefficient, extinction, centre, plane[7 : ROWS - 9, :], plane[9 : ROWS - 7, :], before, after)
    store(fields, slot, 8, values)


def store(fields, slot, row, values):
    rows = pl.ds(pl.multiple_of(slot * TALL + row, 8), values[0].shape[0])
    for kind in range(4):
        fields[kind, rows, :] = values[kind]


def cut_kernel(own, coming, held, high, low):
    del held
    high[:PLANES] = own[:, :SHEAR, :]
    high[PLANES:] = coming[:, :SHEAR, :]
    for plane in range(PLANES):
        low[plane : plane + 1, :] = own[plane, ROWS - 1 : ROWS, :]
    low[PLANES:, :] = jnp.broadcast_to(coming[0, ROWS - 1 : ROWS, :], (8, COLS))


def next_kernel(table, own, coming, held, fields):
    del held
    coefficient = lambda at: table[at : at + 1, :]
    shade_inner(
        coefficient, coefficient(PLAIN), own.at[PLANES - 1], own[PLANES - 2, INNER, :], coming[0, INNER, :], fields, PLANES - 1
    )
    shade_inner(
        coefficient, coefficient(NEXT), coming.at[0], own[PLANES - 1, INNER, :], coming[1, INNER, :], fields, PLANES
    )


def edge_kernel(table, own, coming, high, held, fields, brick):
    del held
    coefficient = lambda at: table[at : at + 1, :]
    for plane in range(PLANES + 2):
        source = own.at[plane] if plane < PLANES else coming.at[plane - PLANES]
        brick[plane, :16, :] = source[ROWS - 16 :, :]
        brick[plane, 16 : 16 + SHEAR, :] = high[plane]
        brick[plane, 16 + SHEAR :, :] = jnp.zeros((8, COLS), jnp.float32)

    def rows_of(slot, before, plain, beyond):
        for start, count, extinction in ((8, 8, plain), (16, SHEAR, beyond)):
            values = shade(
                coefficient,
                coefficient(extinction),
                brick[slot, start : start + count, :],
                brick[slot, start - 1 : start - 1 + count, :],
                brick[slot, start + 1 : start + 1 + count, :],
                0.0 if before is None else brick[before, start : start + count, :],
                brick[slot + 1, start : start + count, :],
            )
            store(fields, slot, ROWS - 16 + start, values)

    def plane_of(plane, _):
        rows_of(plane, plane - 1, PLAIN, BEYOND)
        return 0

    lax.fori_loop(1, PLANES, plane_of, 0)
    rows_of(PLANES, PLANES - 1, NEXT, NEXT_BEYOND)

    @pl.when(lax.axis_index("depth") == 0)
    def _():
        rows_of(0, None, PLAIN, BEYOND)


def render_kernel(table, masks, starts_in, own, coming, low, held, given, kept, fields, starts, semaphore):
    del held
    copy = pltpu.make_async_copy(starts_in, starts, semaphore)
    copy.start()
    coefficient = lambda at: table[at : at + 1, :]
    top = lax.broadcasted_iota(jnp.int32, (8, COLS), 0) == 0

    def first_rows(slot):
        plane_at = lambda plane: own.at[plane] if plane < PLANES else coming.at[plane - PLANES]
        plane = plane_at(slot)
        centre = plane[:8, :]
        above = jnp.where(top, low[slot : slot + 1, :], pltpu.roll(centre, 1, 0))
        before = 0.0 if slot == 0 else plane_at(slot - 1)[:8, :]
        extinction = coefficient(NEXT if slot == PLANES else PLAIN)
        store(fields, slot, 0, shade(coefficient, extinction, centre, above, plane[1:9, :], before, plane_at(slot + 1)[:8, :]))

    for slot in range(1, SLABS):
        first_rows(slot)
    copy.wait()
    leading = starts[FIRST] == 0

    @pl.when(leading)
    def _():
        first_rows(0)

    def render(planes):
        upper = lax.broadcasted_iota(jnp.int32, (8, COLS), 0) < SHARE
        odd = masks[CORE] > 0.5

        def tile_of(tile, _):
            for pair in range(VIEWS // 2):
                sums = []
                for view in (2 * pair, 2 * pair + 1):
                    red = green = blue = optical = jnp.zeros((8, COLS), jnp.float32)
                    for step in range(planes):
                        rows = pl.ds(starts[view * SLABS + step] + 8 * tile, 8)
                        through = jnp.exp(-optical)
                        red = red + fields[0, rows, :] * through
                        green = green + fields[1, rows, :] * through
                        blue = blue + fields[2, rows, :] * through
                        optical = optical + fields[3, rows, :]
                    sums.append((red, green, blue, optical))
                for kind in range(4):
                    first, second = sums[0][kind], sums[1][kind]
                    even_rows = jnp.where(upper, first, pltpu.roll(second, SHARE, 0))
                    odd_rows = jnp.where(upper, pltpu.roll(first, SHARE, 0), second)
                    kept[tile, kind, pair] = jnp.where(odd, odd_rows, even_rows)
                    given[tile, kind, pair] = jnp.where(odd, even_rows, odd_rows)
            return 0

        lax.fori_loop(0, ROWS // 8, tile_of, 0)

    @pl.when(leading)
    def _():
        render(SLABS)

    @pl.when(jnp.logical_not(leading))
    def _():
        render(PLANES)


def merge_kernel(masks, kept, gathered, out):
    odd = masks[CORE] > 0.5
    for pair in range(VIEWS // 2):
        mine_front = masks[FRONT + pair] > 0.5

        def merge(chip, _):
            mine = [kept[chip, kind, pair] for kind in range(4)]
            other = [jnp.where(odd, gathered[0, chip, kind, pair], gathered[1, chip, kind, pair]) for kind in range(4)]
            through = jnp.exp(-jnp.where(mine_front, mine[3], other[3]))
            for kind in range(3):
                front = jnp.where(mine_front, mine[kind], other[kind])
                behind = jnp.where(mine_front, other[kind], mine[kind])
                out[chip, kind, pair] = front + through * behind
            out[chip, 3, pair] = mine[3] + other[3]
            return 0

        lax.fori_loop(0, CHIPS, merge, 0, unroll=True)


def final_kernel(masks, slabs, out):
    for pair in range(VIEWS // 2):
        backward = masks[BACK + pair] > 0.5
        optical = [slabs[chip, 3, pair] for chip in range(CHIPS)]
        ahead, behind = [jnp.zeros((8, COLS), jnp.float32)], [jnp.zeros((8, COLS), jnp.float32)]
        for chip in range(CHIPS - 1):
            ahead.append(ahead[-1] + optical[chip])
            behind.append(behind[-1] + optical[CHIPS - 1 - chip])
        total = ahead[-1] + optical[-1]
        sums = [jnp.zeros((8, COLS), jnp.float32)] * 3
        for chip in range(CHIPS):
            through = jnp.exp(-jnp.where(backward, behind[CHIPS - 1 - chip], ahead[chip]))
            sums = [sums[kind] + slabs[chip, kind, pair] * through for kind in range(3)]
        cover = jnp.where(total < 0.0625, opacity_of(total), 1.0 - jnp.exp(-total))
        for kind, value in enumerate((*sums, cover)):
            out[kind, 2 * pair] = value[:SHARE]
            out[kind, 2 * pair + 1] = value[SHARE:]


def kernel(body, name, out_shape, in_specs, out_specs, flops=0, **more):
    estimate = pl.CostEstimate(flops=flops, bytes_accessed=2**20, transcendentals=0)
    return pl.pallas_call(
        body,
        out_shape=out_shape,
        in_specs=in_specs,
        out_specs=out_specs,
        compiler_params=PARAMS,
        cost_estimate=estimate,
        name=name,
        **more,
    )


def on_device(density, light_vector, colour_gain, colour_bias, shear_step, reverse_view):
    heights, depths = lax.axis_size("height"), lax.axis_size("depth")

    own, first = kernel(
        load_kernel,
        "load",
        (array(PLANES, ROWS, COLS), array(2, ROWS, COLS)),
        [HBM],
        (VMEM,) * 2,
        flops=10**9,
        scratch_shapes=[pltpu.SemaphoreType.DMA],
    )(density)
    coming = lax.ppermute(first, "depth", [(i + 1, i) for i in range(depths - 1)])

    shaded = array(4, SLABS * TALL, COLS)
    fields, table, masks, starts = kernel(
        inner_kernel,
        "inner",
        (shaded, array(16, COLS), array(5, 8, COLS), jax.ShapeDtypeStruct((64,), jnp.int32)),
        [HBM] * 5 + [VMEM],
        (VMEM, VMEM, VMEM, SMEM),
        flops=10**7,
        scratch_shapes=[pltpu.SMEM((3,), jnp.float32)] * 3
        + [pltpu.SMEM((VIEWS,), jnp.int32)] * 2
        + [pltpu.SemaphoreType.DMA((5,))],
    )(light_vector, colour_gain, colour_bias, shear_step, reverse_view, own)

    own_high, own_low = kernel(
        cut_kernel, "cut", (array(PLANES + 2, SHEAR, COLS), array(PLANES + 8, COLS)), [VMEM] * 3, (VMEM,) * 2
    )(own, coming, fields)
    high = lax.ppermute(own_high, "height", [(i + 1, i) for i in range(heights - 1)])
    low = lax.ppermute(own_low, "height", [(i, i + 1) for i in range(heights - 1)])
    fields = kernel(
        next_kernel, "next", shaded, [VMEM] * 4, VMEM, flops=10**7, input_output_aliases={3: 0}
    )(table, own, coming, fields)
    fields = kernel(
        edge_kernel,
        "edge",
        shaded,
        [VMEM] * 5,
        VMEM,
        flops=10**7,
        input_output_aliases={4: 0},
        scratch_shapes=[pltpu.VMEM((PLANES + 2, 24 + SHEAR, COLS), jnp.float32)],
    )(table, own, coming, high, fields)

    part = array(CHIPS, 4, VIEWS // 2, 8, COLS)
    given, kept, _ = kernel(
        render_kernel,
        "render",
        (part, part, shaded),
        [VMEM, VMEM, ANY, VMEM, VMEM, VMEM, VMEM],
        (VMEM,) * 3,
        input_output_aliases={6: 2},
        scratch_shapes=[pltpu.SMEM((64,), jnp.int32), pltpu.SemaphoreType.DMA],
    )(table, masks, starts, own, coming, low, fields)

    cores = [[2 * chip, 2 * chip + 1] for chip in range(CHIPS)]
    gathered = lax.all_gather(given, "depth", axis=0, axis_index_groups=cores)
    merged = kernel(merge_kernel, "merge", part, [VMEM] * 3, VMEM)(masks, kept, gathered)
    chips = [[core + 2 * chip for chip in range(CHIPS)] for core in range(2)]
    slabs = lax.all_to_all(merged, "depth", 0, 0, tiled=True, axis_index_groups=chips)
    return kernel(final_kernel, "composite", array(4, VIEWS, SHARE, COLS), [VMEM] * 2, VMEM)(masks, slabs)


def solution(mesh):
    placed = (P("depth", "height", None), P(), P(), P(), P(), P())
    return jax.shard_map(
        on_device,
        mesh=mesh,
        in_specs=placed,
        out_specs=P(None, None, ("height", "depth"), None),
        check_vma=False,
    )
```

```python
import jax
import jax.numpy as jnp
from jax import lax
from jax.experimental import pallas as pl
from jax.experimental.pallas import tpu as pltpu
from jax.sharding import PartitionSpec as P

EXTINCTION = 2.5
SMEM = pl.BlockSpec(memory_space=pltpu.SMEM)
VMEM = pl.BlockSpec(memory_space=pltpu.VMEM)
ANY = pl.BlockSpec(memory_space=pl.ANY)
HBM = pl.BlockSpec(memory_space=pltpu.HBM)
PLANES, ROWS, COLS, SHEAR, VIEWS, GROUPS, BRICKS = 8, 64, 128, 32, 4, 16, 32
TALL = ROWS + SHEAR
SLABS = PLANES + 1
CHIPS = GROUPS // 2
SHARE = ROWS // GROUPS
PARAMS = pltpu.CompilerParams(vmem_limit_bytes=8 * 2**20)
LIGHT, GAIN, BIAS, PLAIN, BEYOND, NEXT, NEXT_BEYOND = 0, 3, 6, 9, 10, 11, 12
FRONT, BACK, CORE = 0, 2, 4
INNER = slice(8, ROWS - 8)
FIRST = VIEWS * SLABS


def array(*shape):
    return jax.ShapeDtypeStruct(shape, jnp.float32)


def opacity_of(optical):
    series = 1.0 - optical * (1.0 / 6.0)
    for term in (5.0, 4.0, 3.0, 2.0):
        series = 1.0 - optical * (1.0 / term) * series
    return optical * series


def shade(coefficient, extinction, centre, above, below, before, after):
    lane = lax.broadcasted_iota(jnp.int32, centre.shape, 1)
    tilt_rows = 0.5 * (below - above)
    tilt_depth = 0.5 * (after - before)
    right = jnp.where(lane == COLS - 1, 0.0, pltpu.roll(centre, COLS - 1, 1))
    left = jnp.where(lane == 0, 0.0, pltpu.roll(centre, 1, 1))
    tilt_cols = 0.5 * (right - left)
    slope = coefficient(LIGHT) * tilt_depth + coefficient(LIGHT + 1) * tilt_rows + coefficient(LIGHT + 2) * tilt_cols
    facing = slope * lax.rsqrt(1.0 + tilt_depth * tilt_depth + tilt_rows * tilt_rows + tilt_cols * tilt_cols)
    shading = 0.25 + 1.5 * jnp.maximum(facing, 0.0)
    optical = extinction * (jnp.maximum(centre, 0.0) + jnp.log1p(jnp.exp(-jnp.abs(centre))))
    strength = opacity_of(optical) * shading
    tones = [jax.nn.sigmoid(coefficient(GAIN + i) * centre + coefficient(BIAS + i)) for i in range(3)]
    return [strength * tone for tone in tones] + [optical]


def load_kernel(density, own, first, semaphore):
    copy = pltpu.make_async_copy(density, own, semaphore)
    copy.start()
    copy.wait()
    first[...] = own[:2]


def inner_kernel(*refs):
    arguments, (own, coming, _, fields, table, masks, starts), scalars, semaphores = refs[:5], refs[5:12], refs[12:17], refs[17]
    copies = [pltpu.make_async_copy(arguments[i], scalars[i], semaphores.at[i]) for i in range(5)]
    for copy in copies:
        copy.start()
    depth, height = lax.axis_index("depth"), lax.axis_index("height")
    for copy in copies:
        copy.wait()
    light, gain, bias, shear, reverse = scalars
    extinction = EXTINCTION / (PLANES * GROUPS)
    beyond = jnp.where(height == BRICKS - 1, 0.0, extinction)
    following = jnp.where(depth == GROUPS - 1, 0.0, extinction)
    both = jnp.where(depth == GROUPS - 1, 0.0, beyond)
    values_of = [ref[i] for ref in (light, gain, bias) for i in range(3)] + [extinction, beyond, following, both]
    for row, scalar in enumerate(values_of):
        table[row : row + 1, :] = jnp.full((1, COLS), scalar, jnp.float32)
    upper = lax.broadcasted_iota(jnp.int32, (8, COLS), 0) < SHARE
    core = depth % 2
    for base, digit in ((FRONT, core), (BACK, 1)):
        for pair in range(VIEWS // 2):
            first = jnp.where(reverse[2 * pair] == digit, 1.0, 0.0)
            second = jnp.where(reverse[2 * pair + 1] == digit, 1.0, 0.0)
            masks[base + pair] = jnp.where(upper, first, second)
    masks[CORE] = jnp.full((8, COLS), core, jnp.float32)
    first = jnp.where(depth == 0, 0, 1)
    starts[FIRST] = first
    for view in range(VIEWS):
        for step in range(SLABS):
            slot = jnp.where(reverse[view] == 1, SLABS - 1 - step, jnp.minimum(first + step, SLABS - 1))
            offset = lax.shift_right_logical((depth * PLANES + slot) * shear[view], 7)
            starts[view * SLABS + step] = slot * TALL + jnp.minimum(offset, SHEAR)

    coefficient = lambda at: values_of[at]

    def plane_of(plane, _):
        shade_inner(coefficient, extinction, own.at[plane], own[plane - 1, INNER, :], own[plane + 1, INNER, :], fields, plane)
        return 0

    lax.fori_loop(1, PLANES - 1, plane_of, 0)
    last = own.at[PLANES - 1]
    shade_inner(coefficient, extinction, last, own[PLANES - 2, INNER, :], coming[0, INNER, :], fields, PLANES - 1)
    shade_inner(coefficient, following, coming.at[0], last[INNER, :], coming[1, INNER, :], fields, PLANES)

    @pl.when(depth == 0)
    def _():
        shade_inner(coefficient, extinction, own.at[0], 0.0, own[1, INNER, :], fields, 0)


def shade_inner(coefficient, extinction, plane, before, after, fields, slot):
    centre = plane[INNER, :]
    values = shade(coefficient, extinction, centre, plane[7 : ROWS - 9, :], plane[9 : ROWS - 7, :], before, after)
    store(fields, slot, 8, values)


def store(fields, slot, row, values):
    rows = pl.ds(pl.multiple_of(slot * TALL + row, 8), values[0].shape[0])
    for kind in range(4):
        fields[kind, rows, :] = values[kind]


def cut_kernel(own, coming, high, low):
    high[:PLANES] = own[:, :SHEAR, :]
    high[PLANES:] = coming[:, :SHEAR, :]
    for plane in range(PLANES):
        low[plane : plane + 1, :] = own[plane, ROWS - 1 : ROWS, :]
    low[PLANES:, :] = jnp.broadcast_to(coming[0, ROWS - 1 : ROWS, :], (8, COLS))


def edge_kernel(table, own, coming, high, held, fields, brick):
    del held
    coefficient = lambda at: table[at : at + 1, :]
    for plane in range(PLANES + 2):
        source = own.at[plane] if plane < PLANES else coming.at[plane - PLANES]
        brick[plane, :16, :] = source[ROWS - 16 :, :]
        brick[plane, 16 : 16 + SHEAR, :] = high[plane]
        brick[plane, 16 + SHEAR :, :] = jnp.zeros((8, COLS), jnp.float32)

    def rows_of(slot, before, plain, beyond):
        for start, count, extinction in ((8, 8, plain), (16, SHEAR, beyond)):
            values = shade(
                coefficient,
                coefficient(extinction),
                brick[slot, start : start + count, :],
                brick[slot, start - 1 : start - 1 + count, :],
                brick[slot, start + 1 : start + 1 + count, :],
                0.0 if before is None else brick[before, start : start + count, :],
                brick[slot + 1, start : start + count, :],
            )
            store(fields, slot, ROWS - 16 + start, values)

    def plane_of(plane, _):
        rows_of(plane, plane - 1, PLAIN, BEYOND)
        return 0

    lax.fori_loop(1, PLANES, plane_of, 0)
    rows_of(PLANES, PLANES - 1, NEXT, NEXT_BEYOND)

    @pl.when(lax.axis_index("depth") == 0)
    def _():
        rows_of(0, None, PLAIN, BEYOND)


def render_kernel(masks, starts_in, fields, given, kept, starts, semaphore):
    copy = pltpu.make_async_copy(starts_in, starts, semaphore)
    copy.start()
    copy.wait()
    render(masks, starts, fields, given, kept, 1, ROWS // 8)


def first_kernel(table, masks, starts_in, own, coming, low, held, *refs):
    del held
    given, kept, fields, starts, semaphore = refs[2:]
    copy = pltpu.make_async_copy(starts_in, starts, semaphore)
    copy.start()
    coefficient = lambda at: table[at : at + 1, :]
    top = lax.broadcasted_iota(jnp.int32, (8, COLS), 0) == 0

    def first_rows(slot):
        plane_at = lambda plane: own.at[plane] if plane < PLANES else coming.at[plane - PLANES]
        plane = plane_at(slot)
        centre = plane[:8, :]
        above = jnp.where(top, low[slot : slot + 1, :], pltpu.roll(centre, 1, 0))
        before = 0.0 if slot == 0 else plane_at(slot - 1)[:8, :]
        extinction = coefficient(NEXT if slot == PLANES else PLAIN)
        store(fields, slot, 0, shade(coefficient, extinction, centre, above, plane[1:9, :], before, plane_at(slot + 1)[:8, :]))

    for slot in range(1, SLABS):
        first_rows(slot)

    @pl.when(lax.axis_index("depth") == 0)
    def _():
        first_rows(0)

    copy.wait()
    render(masks, starts, fields, given, kept, 0, 1)


def render(masks, starts, fields, given, kept, tile, tiles):
    upper = lax.broadcasted_iota(jnp.int32, (8, COLS), 0) < SHARE
    odd = masks[CORE] > 0.5

    def of(planes):
        def tile_of(tile, _):
            for pair in range(VIEWS // 2):
                sums = []
                for view in (2 * pair, 2 * pair + 1):
                    red = green = blue = optical = jnp.zeros((8, COLS), jnp.float32)
                    for step in range(planes):
                        rows = pl.ds(starts[view * SLABS + step] + 8 * tile, 8)
                        through = jnp.exp(-optical)
                        red = red + fields[0, rows, :] * through
                        green = green + fields[1, rows, :] * through
                        blue = blue + fields[2, rows, :] * through
                        optical = optical + fields[3, rows, :]
                    sums.append((red, green, blue, optical))
                for kind in range(4):
                    first, second = sums[0][kind], sums[1][kind]
                    even_rows = jnp.where(upper, first, pltpu.roll(second, SHARE, 0))
                    odd_rows = jnp.where(upper, pltpu.roll(first, SHARE, 0), second)
                    kept[tile, kind, pair] = jnp.where(odd, odd_rows, even_rows)
                    given[tile, kind, pair] = jnp.where(odd, even_rows, odd_rows)
            return 0

        lax.fori_loop(tile, tiles, tile_of, 0)

    leading = starts[FIRST] == 0

    @pl.when(leading)
    def _():
        of(SLABS)

    @pl.when(jnp.logical_not(leading))
    def _():
        of(PLANES)


def merge_kernel(masks, kept, gathered, out):
    odd = masks[CORE] > 0.5
    for pair in range(VIEWS // 2):
        mine_front = masks[FRONT + pair] > 0.5

        def merge(chip, _):
            mine = [kept[chip, kind, pair] for kind in range(4)]
            other = [jnp.where(odd, gathered[0, chip, kind, pair], gathered[1, chip, kind, pair]) for kind in range(4)]
            through = jnp.exp(-jnp.where(mine_front, mine[3], other[3]))
            for kind in range(3):
                front = jnp.where(mine_front, mine[kind], other[kind])
                behind = jnp.where(mine_front, other[kind], mine[kind])
                out[chip, kind, pair] = front + through * behind
            out[chip, 3, pair] = mine[3] + other[3]
            return 0

        lax.fori_loop(0, CHIPS, merge, 0, unroll=True)


def final_kernel(masks, slabs, out):
    for pair in range(VIEWS // 2):
        backward = masks[BACK + pair] > 0.5
        optical = [slabs[chip, 3, pair] for chip in range(CHIPS)]
        ahead, behind = [jnp.zeros((8, COLS), jnp.float32)], [jnp.zeros((8, COLS), jnp.float32)]
        for chip in range(CHIPS - 1):
            ahead.append(ahead[-1] + optical[chip])
            behind.append(behind[-1] + optical[CHIPS - 1 - chip])
        total = ahead[-1] + optical[-1]
        sums = [jnp.zeros((8, COLS), jnp.float32)] * 3
        for chip in range(CHIPS):
            through = jnp.exp(-jnp.where(backward, behind[CHIPS - 1 - chip], ahead[chip]))
            sums = [sums[kind] + slabs[chip, kind, pair] * through for kind in range(3)]
        cover = jnp.where(total < 0.0625, opacity_of(total), 1.0 - jnp.exp(-total))
        for kind, value in enumerate((*sums, cover)):
            out[kind, 2 * pair] = value[:SHARE]
            out[kind, 2 * pair + 1] = value[SHARE:]


def kernel(body, name, out_shape, in_specs, out_specs, flops=0, **more):
    estimate = pl.CostEstimate(flops=flops, bytes_accessed=2**20, transcendentals=0)
    return pl.pallas_call(
        body,
        out_shape=out_shape,
        in_specs=in_specs,
        out_specs=out_specs,
        compiler_params=PARAMS,
        cost_estimate=estimate,
        name=name,
        **more,
    )


def on_device(density, light_vector, colour_gain, colour_bias, shear_step, reverse_view):
    heights, depths = lax.axis_size("height"), lax.axis_size("depth")

    own, first = kernel(
        load_kernel,
        "load",
        (array(PLANES, ROWS, COLS), array(2, ROWS, COLS)),
        [HBM],
        (VMEM,) * 2,
        flops=10**9,
        scratch_shapes=[pltpu.SemaphoreType.DMA],
    )(density)
    coming = lax.ppermute(first, "depth", [(i + 1, i) for i in range(depths - 1)])

    own_high, own_low = kernel(
        cut_kernel, "cut", (array(PLANES + 2, SHEAR, COLS), array(PLANES + 8, COLS)), [VMEM] * 2, (VMEM,) * 2
    )(own, coming)
    high = lax.ppermute(own_high, "height", [(i + 1, i) for i in range(heights - 1)])
    low = lax.ppermute(own_low, "height", [(i, i + 1) for i in range(heights - 1)])

    shaded = array(4, SLABS * TALL, COLS)
    fields, table, masks, starts = kernel(
        inner_kernel,
        "inner",
        (shaded, array(16, COLS), array(5, 8, COLS), jax.ShapeDtypeStruct((64,), jnp.int32)),
        [HBM] * 5 + [VMEM] * 3,
        (VMEM, VMEM, VMEM, SMEM),
        flops=10**7,
        scratch_shapes=[pltpu.SMEM((3,), jnp.float32)] * 3
        + [pltpu.SMEM((VIEWS,), jnp.int32)] * 2
        + [pltpu.SemaphoreType.DMA((5,))],
    )(light_vector, colour_gain, colour_bias, shear_step, reverse_view, own, coming, own_low)
    fields = kernel(
        edge_kernel,
        "edge",
        shaded,
        [VMEM] * 5,
        VMEM,
        flops=10**7,
        input_output_aliases={4: 0},
        scratch_shapes=[pltpu.VMEM((PLANES + 2, 24 + SHEAR, COLS), jnp.float32)],
    )(table, own, coming, high, fields)

    part = array(CHIPS, 4, VIEWS // 2, 8, COLS)
    memory = [pltpu.SMEM((64,), jnp.int32), pltpu.SemaphoreType.DMA]
    given, kept = kernel(
        render_kernel, "render", (part, part), [VMEM, ANY, VMEM], (VMEM,) * 2, flops=10**7, scratch_shapes=memory
    )(masks, starts, fields)
    given, kept, _ = kernel(
        first_kernel,
        "first",
        (part, part, shaded),
        [VMEM, VMEM, ANY] + [VMEM] * 6,
        (VMEM,) * 3,
        input_output_aliases={6: 2, 7: 0, 8: 1},
        scratch_shapes=memory,
    )(table, masks, starts, own, coming, low, fields, given, kept)

    cores = [[2 * chip, 2 * chip + 1] for chip in range(CHIPS)]
    gathered = lax.all_gather(given, "depth", axis=0, axis_index_groups=cores)
    merged = kernel(merge_kernel, "merge", part, [VMEM] * 3, VMEM)(masks, kept, gathered)
    chips = [[core + 2 * chip for chip in range(CHIPS)] for core in range(2)]
    slabs = lax.all_to_all(merged, "depth", 0, 0, tiled=True, axis_index_groups=chips)
    return kernel(final_kernel, "composite", array(4, VIEWS, SHARE, COLS), [VMEM] * 2, VMEM)(masks, slabs)


def solution(mesh):
    placed = (P("depth", "height", None), P(), P(), P(), P(), P())
    return jax.shard_map(
        on_device,
        mesh=mesh,
        in_specs=placed,
        out_specs=P(None, None, ("height", "depth"), None),
        check_vma=False,
    )
```

```python
import jax
import jax.numpy as jnp
from jax import lax
from jax.experimental import pallas as pl
from jax.experimental.pallas import tpu as pltpu
from jax.sharding import PartitionSpec as P

EXTINCTION = 2.5
SMEM = pl.BlockSpec(memory_space=pltpu.SMEM)
VMEM = pl.BlockSpec(memory_space=pltpu.VMEM)
ANY = pl.BlockSpec(memory_space=pl.ANY)
HBM = pl.BlockSpec(memory_space=pltpu.HBM)
PLANES, ROWS, COLS, SHEAR, VIEWS, GROUPS, BRICKS = 8, 64, 128, 32, 4, 16, 32
TOP = 8
HALF = ROWS // 2
TALL = ROWS + SHEAR
PADDED = TOP + TALL + 8
SLABS = PLANES + 1
CHIPS = GROUPS // 2
SHARE = ROWS // GROUPS
PARAMS = pltpu.CompilerParams(vmem_limit_bytes=8 * 2**20)
LIGHT, GAIN, BIAS, PLAIN, BEYOND, NEXT, NEXT_BEYOND = 0, 3, 6, 9, 10, 11, 12
FRONT, BACK, CORE = 0, 2, 4
FIRST = VIEWS * SLABS


def array(*shape):
    return jax.ShapeDtypeStruct(shape, jnp.float32)


def opacity_of(optical):
    series = 1.0 - optical * (1.0 / 6.0)
    for term in (5.0, 4.0, 3.0, 2.0):
        series = 1.0 - optical * (1.0 / term) * series
    return optical * series


def shade(coefficient, extinction, centre, above, below, before, after):
    lane = lax.broadcasted_iota(jnp.int32, centre.shape, 1)
    tilt_rows = 0.5 * (below - above)
    tilt_depth = 0.5 * (after - before)
    right = jnp.where(lane == COLS - 1, 0.0, pltpu.roll(centre, COLS - 1, 1))
    left = jnp.where(lane == 0, 0.0, pltpu.roll(centre, 1, 1))
    tilt_cols = 0.5 * (right - left)
    slope = coefficient(LIGHT) * tilt_depth + coefficient(LIGHT + 1) * tilt_rows + coefficient(LIGHT + 2) * tilt_cols
    facing = slope * lax.rsqrt(1.0 + tilt_depth * tilt_depth + tilt_rows * tilt_rows + tilt_cols * tilt_cols)
    shading = 0.25 + 1.5 * jnp.maximum(facing, 0.0)
    optical = extinction * (jnp.maximum(centre, 0.0) + jnp.log1p(jnp.exp(-jnp.abs(centre))))
    strength = opacity_of(optical) * shading
    tones = [jax.nn.sigmoid(coefficient(GAIN + i) * centre + coefficient(BIAS + i)) for i in range(3)]
    return [strength * tone for tone in tones] + [optical]


def load_kernel(density, own, one, two, semaphore):
    copy = pltpu.make_async_copy(density, own, semaphore)
    copy.start()
    odd = lax.axis_index("height") % 2
    copy.wait()
    one[...] = own[:, pl.ds(pl.multiple_of(odd * HALF, HALF), HALF), :]
    two[...] = own[:, pl.ds(pl.multiple_of((1 - odd) * HALF, HALF), HALF), :]


def inner_kernel(*refs):
    arguments, (own, fields, table, masks, starts), scalars, semaphores = refs[:5], refs[5:10], refs[10:15], refs[15]
    copies = [pltpu.make_async_copy(arguments[i], scalars[i], semaphores.at[i]) for i in range(5)]
    for copy in copies:
        copy.start()
    depth, height = lax.axis_index("depth"), lax.axis_index("height")
    for copy in copies:
        copy.wait()
    light, gain, bias, shear, reverse = scalars
    extinction = EXTINCTION / (PLANES * GROUPS)
    beyond = jnp.where(height == BRICKS - 1, 0.0, extinction)
    following = jnp.where(depth == GROUPS - 1, 0.0, extinction)
    both = jnp.where(depth == GROUPS - 1, 0.0, beyond)
    values_of = [ref[i] for ref in (light, gain, bias) for i in range(3)] + [extinction, beyond, following, both]
    for row, scalar in enumerate(values_of):
        table[row : row + 1, :] = jnp.full((1, COLS), scalar, jnp.float32)
    upper = lax.broadcasted_iota(jnp.int32, (8, COLS), 0) < SHARE
    core = depth % 2
    for base, digit in ((FRONT, core), (BACK, 1)):
        for pair in range(VIEWS // 2):
            first = jnp.where(reverse[2 * pair] == digit, 1.0, 0.0)
            second = jnp.where(reverse[2 * pair + 1] == digit, 1.0, 0.0)
            masks[base + pair] = jnp.where(upper, first, second)
    masks[CORE] = jnp.full((8, COLS), core, jnp.float32)
    first = jnp.where(depth == 0, 0, 1)
    starts[FIRST] = first
    for view in range(VIEWS):
        for step in range(SLABS):
            slot = jnp.where(reverse[view] == 1, SLABS - 1 - step, jnp.minimum(first + step, SLABS - 1))
            offset = lax.shift_right_logical((depth * PLANES + slot) * shear[view], 7)
            starts[view * SLABS + step] = slot * TALL + jnp.minimum(offset, SHEAR)

    def plane_of(step, _):
        plane = step + 1
        inner = slice(8, ROWS - 8)
        values = shade(
            lambda row: values_of[row],
            extinction,
            own[plane, inner, :],
            own[plane, 7 : ROWS - 9, :],
            own[plane, 9 : ROWS - 7, :],
            own[plane - 1, inner, :],
            own[plane + 1, inner, :],
        )
        rows = pl.ds(pl.multiple_of(plane * TALL + 8, 8), ROWS - 16)
        for kind in range(4):
            fields[kind, rows, :] = values[kind]
        return 0

    lax.fori_loop(0, PLANES - 2, plane_of, 0)


def join_kernel(own, one, two, table, brick, first):
    del table
    odd = lax.axis_index("height") % 2 == 1
    for plane in range(PLANES):
        low = jnp.where(odd, two[plane, HALF - 1 : HALF, :], one[plane, HALF - 1 : HALF, :])
        parts = (
            (0, jnp.broadcast_to(low, (8, COLS))),
            (TOP, own[plane]),
            (TOP + ROWS, jnp.where(odd, one[plane, :SHEAR, :], two[plane, :SHEAR, :])),
            (TOP + TALL, jnp.zeros((8, COLS), jnp.float32)),
        )
        for start, part in parts:
            brick[plane, start : start + part.shape[0], :] = part
            if plane < 2:
                first[plane, start : start + part.shape[0], :] = part


def shade_rows(table, extinction, row, count, plane, before, after, fields, slot):
    start = row + TOP
    values = shade(
        lambda at: table[at : at + 1, :],
        table[extinction : extinction + 1, :],
        plane[start : start + count, :],
        plane[start - 1 : start - 1 + count, :],
        plane[start + 1 : start + 1 + count, :],
        0.0 if before is None else before[start : start + count, :],
        after[start : start + count, :],
    )
    rows = pl.ds(pl.multiple_of(slot * TALL + row, 8), count)
    for kind in range(4):
        fields[kind, rows, :] = values[kind]


def edge_kernel(table, brick, held, fields):
    del held

    def plane_of(step, _):
        plane = step + 1
        refs = (brick.at[plane], brick.at[plane - 1], brick.at[plane + 1], fields, plane)
        shade_rows(table, PLAIN, 0, 8, *refs)
        shade_rows(table, PLAIN, ROWS - 8, 8, *refs)
        shade_rows(table, BEYOND, ROWS, SHEAR, *refs)
        return 0

    lax.fori_loop(0, PLANES - 2, plane_of, 0)


def render_kernel(table, masks, starts_in, brick, coming, held, given, kept, fields, starts, semaphore):
    del held
    copy = pltpu.make_async_copy(starts_in, starts, semaphore)
    copy.start()

    def whole_plane(slot, plane, before, after, own, beyond):
        refs = (plane, before, after, fields, slot)
        shade_rows(table, own, 0, SHEAR, *refs)
        shade_rows(table, own, SHEAR, SHEAR, *refs)
        shade_rows(table, beyond, ROWS, SHEAR, *refs)

    whole_plane(PLANES - 1, brick.at[PLANES - 1], brick.at[PLANES - 2], coming.at[0], PLAIN, BEYOND)
    whole_plane(PLANES, coming.at[0], brick.at[PLANES - 1], coming.at[1], NEXT, NEXT_BEYOND)
    copy.wait()
    leading = starts[FIRST] == 0

    @pl.when(leading)
    def _():
        whole_plane(0, brick.at[0], None, brick.at[1], PLAIN, BEYOND)

    def render(planes):
        upper = lax.broadcasted_iota(jnp.int32, (8, COLS), 0) < SHARE
        odd = masks[CORE] > 0.5

        def tile_of(tile, _):
            for pair in range(VIEWS // 2):
                sums = []
                for view in (2 * pair, 2 * pair + 1):
                    red = green = blue = optical = jnp.zeros((8, COLS), jnp.float32)
                    for step in range(planes):
                        rows = pl.ds(starts[view * SLABS + step] + 8 * tile, 8)
                        through = jnp.exp(-optical)
                        red = red + fields[0, rows, :] * through
                        green = green + fields[1, rows, :] * through
                        blue = blue + fields[2, rows, :] * through
                        optical = optical + fields[3, rows, :]
                    sums.append((red, green, blue, optical))
                for kind in range(4):
                    first, second = sums[0][kind], sums[1][kind]
                    even_rows = jnp.where(upper, first, pltpu.roll(second, SHARE, 0))
                    odd_rows = jnp.where(upper, pltpu.roll(first, SHARE, 0), second)
                    kept[tile, kind, pair] = jnp.where(odd, odd_rows, even_rows)
                    given[tile, kind, pair] = jnp.where(odd, even_rows, odd_rows)
            return 0

        lax.fori_loop(0, ROWS // 8, tile_of, 0)

    @pl.when(leading)
    def _():
        render(SLABS)

    @pl.when(jnp.logical_not(leading))
    def _():
        render(PLANES)


def merge_kernel(masks, kept, gathered, out):
    odd = masks[CORE] > 0.5
    for pair in range(VIEWS // 2):
        mine_front = masks[FRONT + pair] > 0.5

        def merge(chip, _):
            mine = [kept[chip, kind, pair] for kind in range(4)]
            other = [jnp.where(odd, gathered[0, chip, kind, pair], gathered[1, chip, kind, pair]) for kind in range(4)]
            through = jnp.exp(-jnp.where(mine_front, mine[3], other[3]))
            for kind in range(3):
                front = jnp.where(mine_front, mine[kind], other[kind])
                behind = jnp.where(mine_front, other[kind], mine[kind])
                out[chip, kind, pair] = front + through * behind
            out[chip, 3, pair] = mine[3] + other[3]
            return 0

        lax.fori_loop(0, CHIPS, merge, 0, unroll=True)


def final_kernel(masks, slabs, out):
    for pair in range(VIEWS // 2):
        backward = masks[BACK + pair] > 0.5
        optical = [slabs[chip, 3, pair] for chip in range(CHIPS)]
        ahead, behind = [jnp.zeros((8, COLS), jnp.float32)], [jnp.zeros((8, COLS), jnp.float32)]
        for chip in range(CHIPS - 1):
            ahead.append(ahead[-1] + optical[chip])
            behind.append(behind[-1] + optical[CHIPS - 1 - chip])
        total = ahead[-1] + optical[-1]
        sums = [jnp.zeros((8, COLS), jnp.float32)] * 3
        for chip in range(CHIPS):
            through = jnp.exp(-jnp.where(backward, behind[CHIPS - 1 - chip], ahead[chip]))
            sums = [sums[kind] + slabs[chip, kind, pair] * through for kind in range(3)]
        cover = jnp.where(total < 0.0625, opacity_of(total), 1.0 - jnp.exp(-total))
        for kind, value in enumerate((*sums, cover)):
            out[kind, 2 * pair] = value[:SHARE]
            out[kind, 2 * pair + 1] = value[SHARE:]


def kernel(body, name, out_shape, in_specs, out_specs, flops=0, **more):
    estimate = pl.CostEstimate(flops=flops, bytes_accessed=2**20, transcendentals=0)
    return pl.pallas_call(
        body,
        out_shape=out_shape,
        in_specs=in_specs,
        out_specs=out_specs,
        compiler_params=PARAMS,
        cost_estimate=estimate,
        name=name,
        **more,
    )


def on_device(density, light_vector, colour_gain, colour_bias, shear_step, reverse_view):
    heights, depths = lax.axis_size("height"), lax.axis_size("depth")

    half = array(PLANES, HALF, COLS)
    own, own_one, own_two = kernel(
        load_kernel,
        "load",
        (array(PLANES, ROWS, COLS), half, half),
        [HBM],
        (VMEM,) * 3,
        flops=10**9,
        scratch_shapes=[pltpu.SemaphoreType.DMA],
    )(density)
    swaps = [[(i, i + 1) for i in range(start, heights - 1, 2)] for start in (1, 0)]
    one, two = [
        lax.ppermute(mine, "height", pairs + [(j, i) for i, j in pairs])
        for mine, pairs in zip((own_one, own_two), swaps)
    ]

    fields, table, masks, starts = kernel(
        inner_kernel,
        "inner",
        (
            array(4, SLABS * TALL, COLS),
            array(16, COLS),
            array(5, 8, COLS),
            jax.ShapeDtypeStruct((64,), jnp.int32),
        ),
        [HBM] * 5 + [VMEM],
        (VMEM, VMEM, VMEM, SMEM),
        flops=10**7,
        scratch_shapes=[pltpu.SMEM((3,), jnp.float32)] * 3
        + [pltpu.SMEM((VIEWS,), jnp.int32)] * 2
        + [pltpu.SemaphoreType.DMA((5,))],
    )(light_vector, colour_gain, colour_bias, shear_step, reverse_view, own)

    brick, first = kernel(
        join_kernel, "join", (array(PLANES, PADDED, COLS), array(2, PADDED, COLS)), [VMEM] * 4, (VMEM,) * 2
    )(own, one, two, table)
    coming = lax.ppermute(first, "depth", [(i + 1, i) for i in range(depths - 1)])

    fields = kernel(
        edge_kernel,
        "edge",
        array(4, SLABS * TALL, COLS),
        [VMEM] * 3,
        VMEM,
        flops=10**7,
        input_output_aliases={2: 0},
    )(table, brick, fields)

    part = array(CHIPS, 4, VIEWS // 2, 8, COLS)
    given, kept, _ = kernel(
        render_kernel,
        "render",
        (part, part, array(4, SLABS * TALL, COLS)),
        [VMEM, VMEM, ANY, VMEM, VMEM, VMEM],
        (VMEM,) * 3,
        input_output_aliases={5: 2},
        scratch_shapes=[pltpu.SMEM((64,), jnp.int32), pltpu.SemaphoreType.DMA],
    )(table, masks, starts, brick, coming, fields)

    cores = [[2 * chip, 2 * chip + 1] for chip in range(CHIPS)]
    gathered = lax.all_gather(given, "depth", axis=0, axis_index_groups=cores)
    merged = kernel(merge_kernel, "merge", part, [VMEM] * 3, VMEM)(masks, kept, gathered)
    chips = [[core + 2 * chip for chip in range(CHIPS)] for core in range(2)]
    slabs = lax.all_to_all(merged, "depth", 0, 0, tiled=True, axis_index_groups=chips)
    return kernel(final_kernel, "composite", array(4, VIEWS, SHARE, COLS), [VMEM] * 2, VMEM)(masks, slabs)


def solution(mesh):
    placed = (P("depth", "height", None), P(), P(), P(), P(), P())
    return jax.shard_map(
        on_device,
        mesh=mesh,
        in_specs=placed,
        out_specs=P(None, None, ("height", "depth"), None),
        check_vma=False,
    )
```

```python
import jax
import jax.numpy as jnp
from jax import lax
from jax.experimental import pallas as pl
from jax.experimental.pallas import tpu as pltpu
from jax.sharding import PartitionSpec as P

EXTINCTION = 2.5
SMEM = pl.BlockSpec(memory_space=pltpu.SMEM)
VMEM = pl.BlockSpec(memory_space=pltpu.VMEM)
ANY = pl.BlockSpec(memory_space=pl.ANY)
HBM = pl.BlockSpec(memory_space=pltpu.HBM)
PLANES, ROWS, COLS, SHEAR, VIEWS, GROUPS, BRICKS = 8, 64, 128, 32, 4, 16, 32
TALL = ROWS + SHEAR
SLABS = PLANES + 1
CHIPS = GROUPS // 2
SHARE = ROWS // GROUPS
PARAMS = pltpu.CompilerParams(vmem_limit_bytes=8 * 2**20)
LIGHT, GAIN, BIAS, PLAIN, BEYOND, NEXT, NEXT_BEYOND = 0, 3, 6, 9, 10, 11, 12
FRONT, BACK, CORE = 0, 2, 4
INNER = slice(8, ROWS - 8)
FIRST = VIEWS * SLABS


def array(*shape):
    return jax.ShapeDtypeStruct(shape, jnp.float32)


def opacity_of(optical):
    series = 1.0 - optical * (1.0 / 6.0)
    for term in (5.0, 4.0, 3.0, 2.0):
        series = 1.0 - optical * (1.0 / term) * series
    return optical * series


def shade(coefficient, extinction, centre, above, below, before, after):
    lane = lax.broadcasted_iota(jnp.int32, centre.shape, 1)
    tilt_rows = 0.5 * (below - above)
    tilt_depth = 0.5 * (after - before)
    right = jnp.where(lane == COLS - 1, 0.0, pltpu.roll(centre, COLS - 1, 1))
    left = jnp.where(lane == 0, 0.0, pltpu.roll(centre, 1, 1))
    tilt_cols = 0.5 * (right - left)
    slope = coefficient(LIGHT) * tilt_depth + coefficient(LIGHT + 1) * tilt_rows + coefficient(LIGHT + 2) * tilt_cols
    facing = slope * lax.rsqrt(1.0 + tilt_depth * tilt_depth + tilt_rows * tilt_rows + tilt_cols * tilt_cols)
    shading = 0.25 + 1.5 * jnp.maximum(facing, 0.0)
    optical = extinction * (jnp.maximum(centre, 0.0) + jnp.log1p(jnp.exp(-jnp.abs(centre))))
    strength = opacity_of(optical) * shading
    tones = [jax.nn.sigmoid(coefficient(GAIN + i) * centre + coefficient(BIAS + i)) for i in range(3)]
    return [strength * tone for tone in tones] + [optical]


def load_kernel(density, own, first, semaphore):
    copy = pltpu.make_async_copy(density, own, semaphore)
    copy.start()
    copy.wait()
    first[...] = own[:2]


def inner_kernel(*refs):
    arguments, (own, coming, _, fields, table, masks, starts), scalars, semaphores = refs[:5], refs[5:12], refs[12:17], refs[17]
    copies = [pltpu.make_async_copy(arguments[i], scalars[i], semaphores.at[i]) for i in range(5)]
    for copy in copies:
        copy.start()
    depth, height = lax.axis_index("depth"), lax.axis_index("height")
    for copy in copies:
        copy.wait()
    light, gain, bias, shear, reverse = scalars
    extinction = EXTINCTION / (PLANES * GROUPS)
    beyond = jnp.where(height == BRICKS - 1, 0.0, extinction)
    following = jnp.where(depth == GROUPS - 1, 0.0, extinction)
    both = jnp.where(depth == GROUPS - 1, 0.0, beyond)
    values_of = [ref[i] for ref in (light, gain, bias) for i in range(3)] + [extinction, beyond, following, both]
    for row, scalar in enumerate(values_of):
        table[row : row + 1, :] = jnp.full((1, COLS), scalar, jnp.float32)
    upper = lax.broadcasted_iota(jnp.int32, (8, COLS), 0) < SHARE
    core = depth % 2
    for base, digit in ((FRONT, core), (BACK, 1)):
        for pair in range(VIEWS // 2):
            first = jnp.where(reverse[2 * pair] == digit, 1.0, 0.0)
            second = jnp.where(reverse[2 * pair + 1] == digit, 1.0, 0.0)
            masks[base + pair] = jnp.where(upper, first, second)
    masks[CORE] = jnp.full((8, COLS), core, jnp.float32)
    first = jnp.where(depth == 0, 0, 1)
    starts[FIRST] = first
    for view in range(VIEWS):
        for step in range(SLABS):
            slot = jnp.where(reverse[view] == 1, SLABS - 1 - step, jnp.minimum(first + step, SLABS - 1))
            offset = lax.shift_right_logical((depth * PLANES + slot) * shear[view], 7)
            starts[view * SLABS + step] = slot * TALL + jnp.minimum(offset, SHEAR)

    coefficient = lambda at: values_of[at]

    def plane_of(plane, _):
        shade_inner(coefficient, extinction, own.at[plane], own[plane - 1, INNER, :], own[plane + 1, INNER, :], fields, plane)
        return 0

    lax.fori_loop(1, PLANES - 1, plane_of, 0)
    last = own.at[PLANES - 1]
    shade_inner(coefficient, extinction, last, own[PLANES - 2, INNER, :], coming[0, INNER, :], fields, PLANES - 1)
    shade_inner(coefficient, following, coming.at[0], last[INNER, :], coming[1, INNER, :], fields, PLANES)

    @pl.when(depth == 0)
    def _():
        shade_inner(coefficient, extinction, own.at[0], 0.0, own[1, INNER, :], fields, 0)


def shade_inner(coefficient, extinction, plane, before, after, fields, slot):
    centre = plane[INNER, :]
    values = shade(coefficient, extinction, centre, plane[7 : ROWS - 9, :], plane[9 : ROWS - 7, :], before, after)
    store(fields, slot, 8, values)


def store(fields, slot, row, values):
    rows = pl.ds(pl.multiple_of(slot * TALL + row, 8), values[0].shape[0])
    for kind in range(4):
        fields[kind, rows, :] = values[kind]


def cut_kernel(own, pair, across, coming, high, low):
    odd = lax.axis_index("depth") % 2 == 1
    coming[...] = jnp.where(odd, across[...], pair[1])
    high[:PLANES] = own[:, :SHEAR, :]
    high[PLANES:] = coming[:, :SHEAR, :]
    for plane in range(PLANES):
        low[plane : plane + 1, :] = own[plane, ROWS - 1 : ROWS, :]
    low[PLANES:, :] = jnp.broadcast_to(coming[0, ROWS - 1 : ROWS, :], (8, COLS))


def render_kernel(
    table, masks, starts_in, own, coming, high, held, given, kept, fields, brick, starts, semaphore
):
    del held
    copy = pltpu.make_async_copy(starts_in, starts, semaphore)
    copy.start()
    coefficient = lambda at: table[at : at + 1, :]
    for plane in range(PLANES + 2):
        source = own.at[plane] if plane < PLANES else coming.at[plane - PLANES]
        brick[plane, :16, :] = source[ROWS - 16 :, :]
        brick[plane, 16 : 16 + SHEAR, :] = high[plane]
        brick[plane, 16 + SHEAR :, :] = jnp.zeros((8, COLS), jnp.float32)

    def rows_of(slot, before, plain, beyond):
        for start, count, extinction in ((8, 8, plain), (16, SHEAR, beyond)):
            values = shade(
                coefficient,
                coefficient(extinction),
                brick[slot, start : start + count, :],
                brick[slot, start - 1 : start - 1 + count, :],
                brick[slot, start + 1 : start + 1 + count, :],
                0.0 if before is None else brick[before, start : start + count, :],
                brick[slot + 1, start : start + count, :],
            )
            store(fields, slot, ROWS - 16 + start, values)

    def plane_of(plane, _):
        rows_of(plane, plane - 1, PLAIN, BEYOND)
        return 0

    lax.fori_loop(1, PLANES, plane_of, 0)
    rows_of(PLANES, PLANES - 1, NEXT, NEXT_BEYOND)

    @pl.when(lax.axis_index("depth") == 0)
    def _():
        rows_of(0, None, PLAIN, BEYOND)

    copy.wait()
    render(masks, starts, fields, given, kept, 1, ROWS // 8)


def first_kernel(table, masks, starts_in, own, coming, low, held, *refs):
    del held
    given, kept, fields, starts, semaphore = refs[2:]
    copy = pltpu.make_async_copy(starts_in, starts, semaphore)
    copy.start()
    coefficient = lambda at: table[at : at + 1, :]
    top = lax.broadcasted_iota(jnp.int32, (8, COLS), 0) == 0

    def first_rows(slot):
        plane_at = lambda plane: own.at[plane] if plane < PLANES else coming.at[plane - PLANES]
        plane = plane_at(slot)
        centre = plane[:8, :]
        above = jnp.where(top, low[slot : slot + 1, :], pltpu.roll(centre, 1, 0))
        before = 0.0 if slot == 0 else plane_at(slot - 1)[:8, :]
        extinction = coefficient(NEXT if slot == PLANES else PLAIN)
        store(fields, slot, 0, shade(coefficient, extinction, centre, above, plane[1:9, :], before, plane_at(slot + 1)[:8, :]))

    for slot in range(1, SLABS):
        first_rows(slot)

    @pl.when(lax.axis_index("depth") == 0)
    def _():
        first_rows(0)

    copy.wait()
    render(masks, starts, fields, given, kept, 0, 1)


def render(masks, starts, fields, given, kept, tile, tiles):
    upper = lax.broadcasted_iota(jnp.int32, (8, COLS), 0) < SHARE
    odd = masks[CORE] > 0.5

    def of(planes):
        def tile_of(tile, _):
            for pair in range(VIEWS // 2):
                sums = []
                for view in (2 * pair, 2 * pair + 1):
                    red = green = blue = optical = jnp.zeros((8, COLS), jnp.float32)
                    for step in range(planes):
                        rows = pl.ds(starts[view * SLABS + step] + 8 * tile, 8)
                        through = jnp.exp(-optical)
                        red = red + fields[0, rows, :] * through
                        green = green + fields[1, rows, :] * through
                        blue = blue + fields[2, rows, :] * through
                        optical = optical + fields[3, rows, :]
                    sums.append((red, green, blue, optical))
                for kind in range(4):
                    first, second = sums[0][kind], sums[1][kind]
                    even_rows = jnp.where(upper, first, pltpu.roll(second, SHARE, 0))
                    odd_rows = jnp.where(upper, pltpu.roll(first, SHARE, 0), second)
                    kept[tile, kind, pair] = jnp.where(odd, odd_rows, even_rows)
                    given[tile, kind, pair] = jnp.where(odd, even_rows, odd_rows)
            return 0

        lax.fori_loop(tile, tiles, tile_of, 0)

    leading = starts[FIRST] == 0

    @pl.when(leading)
    def _():
        of(SLABS)

    @pl.when(jnp.logical_not(leading))
    def _():
        of(PLANES)


def merge_kernel(masks, kept, gathered, out):
    odd = masks[CORE] > 0.5
    for pair in range(VIEWS // 2):
        mine_front = masks[FRONT + pair] > 0.5

        def merge(chip, _):
            mine = [kept[chip, kind, pair] for kind in range(4)]
            other = [jnp.where(odd, gathered[0, chip, kind, pair], gathered[1, chip, kind, pair]) for kind in range(4)]
            through = jnp.exp(-jnp.where(mine_front, mine[3], other[3]))
            for kind in range(3):
                front = jnp.where(mine_front, mine[kind], other[kind])
                behind = jnp.where(mine_front, other[kind], mine[kind])
                out[chip, kind, pair] = front + through * behind
            out[chip, 3, pair] = mine[3] + other[3]
            return 0

        lax.fori_loop(0, CHIPS, merge, 0, unroll=True)


def final_kernel(masks, slabs, out):
    for pair in range(VIEWS // 2):
        backward = masks[BACK + pair] > 0.5
        optical = [slabs[chip, 3, pair] for chip in range(CHIPS)]
        ahead, behind = [jnp.zeros((8, COLS), jnp.float32)], [jnp.zeros((8, COLS), jnp.float32)]
        for chip in range(CHIPS - 1):
            ahead.append(ahead[-1] + optical[chip])
            behind.append(behind[-1] + optical[CHIPS - 1 - chip])
        total = ahead[-1] + optical[-1]
        sums = [jnp.zeros((8, COLS), jnp.float32)] * 3
        for chip in range(CHIPS):
            through = jnp.exp(-jnp.where(backward, behind[CHIPS - 1 - chip], ahead[chip]))
            sums = [sums[kind] + slabs[chip, kind, pair] * through for kind in range(3)]
        cover = jnp.where(total < 0.0625, opacity_of(total), 1.0 - jnp.exp(-total))
        for kind, value in enumerate((*sums, cover)):
            out[kind, 2 * pair] = value[:SHARE]
            out[kind, 2 * pair + 1] = value[SHARE:]


def kernel(body, name, out_shape, in_specs, out_specs, flops=0, **more):
    estimate = pl.CostEstimate(flops=flops, bytes_accessed=2**20, transcendentals=0)
    return pl.pallas_call(
        body,
        out_shape=out_shape,
        in_specs=in_specs,
        out_specs=out_specs,
        compiler_params=PARAMS,
        cost_estimate=estimate,
        name=name,
        **more,
    )


def on_device(density, light_vector, colour_gain, colour_bias, shear_step, reverse_view):
    heights, depths = lax.axis_size("height"), lax.axis_size("depth")

    own, first = kernel(
        load_kernel,
        "load",
        (array(PLANES, ROWS, COLS), array(2, ROWS, COLS)),
        [HBM],
        (VMEM,) * 2,
        flops=10**9,
        scratch_shapes=[pltpu.SemaphoreType.DMA],
    )(density)
    cores = [[2 * chip, 2 * chip + 1] for chip in range(CHIPS)]
    across = lax.ppermute(first, "depth", [(i + 1, i) for i in range(1, depths - 1, 2)])
    pair = lax.all_gather(first, "depth", axis=0, axis_index_groups=cores)

    coming, own_high, own_low = kernel(
        cut_kernel,
        "cut",
        (array(2, ROWS, COLS), array(PLANES + 2, SHEAR, COLS), array(PLANES + 8, COLS)),
        [VMEM] * 3,
        (VMEM,) * 3,
    )(own, pair, across)
    high = lax.ppermute(own_high, "height", [(i + 1, i) for i in range(heights - 1)])
    low = lax.ppermute(own_low, "height", [(i, i + 1) for i in range(heights - 1)])

    shaded = array(4, SLABS * TALL, COLS)
    fields, table, masks, starts = kernel(
        inner_kernel,
        "inner",
        (shaded, array(16, COLS), array(5, 8, COLS), jax.ShapeDtypeStruct((64,), jnp.int32)),
        [HBM] * 5 + [VMEM] * 3,
        (VMEM, VMEM, VMEM, SMEM),
        flops=10**7,
        scratch_shapes=[pltpu.SMEM((3,), jnp.float32)] * 3
        + [pltpu.SMEM((VIEWS,), jnp.int32)] * 2
        + [pltpu.SemaphoreType.DMA((5,))],
    )(light_vector, colour_gain, colour_bias, shear_step, reverse_view, own, coming, own_low)
    part = array(CHIPS, 4, VIEWS // 2, 8, COLS)
    memory = [pltpu.SMEM((64,), jnp.int32), pltpu.SemaphoreType.DMA]
    given, kept, fields = kernel(
        render_kernel,
        "render",
        (part, part, shaded),
        [VMEM, VMEM, ANY] + [VMEM] * 4,
        (VMEM,) * 3,
        flops=10**7,
        input_output_aliases={6: 2},
        scratch_shapes=[pltpu.VMEM((PLANES + 2, 24 + SHEAR, COLS), jnp.float32), *memory],
    )(table, masks, starts, own, coming, high, fields)
    given, kept, _ = kernel(
        first_kernel,
        "first",
        (part, part, shaded),
        [VMEM, VMEM, ANY] + [VMEM] * 6,
        (VMEM,) * 3,
        input_output_aliases={6: 2, 7: 0, 8: 1},
        scratch_shapes=memory,
    )(table, masks, starts, own, coming, low, fields, given, kept)

    gathered = lax.all_gather(given, "depth", axis=0, axis_index_groups=cores)
    merged = kernel(merge_kernel, "merge", part, [VMEM] * 3, VMEM)(masks, kept, gathered)
    chips = [[core + 2 * chip for chip in range(CHIPS)] for core in range(2)]
    slabs = lax.all_to_all(merged, "depth", 0, 0, tiled=True, axis_index_groups=chips)
    return kernel(final_kernel, "composite", array(4, VIEWS, SHARE, COLS), [VMEM] * 2, VMEM)(masks, slabs)


def solution(mesh):
    placed = (P("depth", "height", None), P(), P(), P(), P(), P())
    return jax.shard_map(
        on_device,
        mesh=mesh,
        in_specs=placed,
        out_specs=P(None, None, ("height", "depth"), None),
        check_vma=False,
    )
```

```python
import jax
import jax.numpy as jnp
from jax import lax
from jax.experimental import pallas as pl
from jax.experimental.pallas import tpu as pltpu
from jax.sharding import PartitionSpec as P

EXTINCTION = 2.5
SMEM = pl.BlockSpec(memory_space=pltpu.SMEM)
VMEM = pl.BlockSpec(memory_space=pltpu.VMEM)
ANY = pl.BlockSpec(memory_space=pl.ANY)
HBM = pl.BlockSpec(memory_space=pltpu.HBM)
PLANES, ROWS, COLS, SHEAR, VIEWS, GROUPS, BRICKS = 8, 64, 128, 32, 4, 16, 32
TALL = ROWS + SHEAR
SLABS = PLANES + 1
CHIPS = GROUPS // 2
SHARE = ROWS // GROUPS
PARAMS = pltpu.CompilerParams(vmem_limit_bytes=8 * 2**20)
LIGHT, GAIN, BIAS, PLAIN, BEYOND, NEXT, NEXT_BEYOND = 0, 3, 6, 9, 10, 11, 12
FRONT, BACK, CORE = 0, 2, 4
INNER = slice(8, ROWS - 8)
FIRST = VIEWS * SLABS


def array(*shape):
    return jax.ShapeDtypeStruct(shape, jnp.float32)


def opacity_of(optical):
    series = 1.0 - optical * (1.0 / 6.0)
    for term in (5.0, 4.0, 3.0, 2.0):
        series = 1.0 - optical * (1.0 / term) * series
    return optical * series


def shade(coefficient, extinction, centre, above, below, before, after):
    lane = lax.broadcasted_iota(jnp.int32, centre.shape, 1)
    tilt_rows = 0.5 * (below - above)
    tilt_depth = 0.5 * (after - before)
    right = jnp.where(lane == COLS - 1, 0.0, pltpu.roll(centre, COLS - 1, 1))
    left = jnp.where(lane == 0, 0.0, pltpu.roll(centre, 1, 1))
    tilt_cols = 0.5 * (right - left)
    slope = coefficient(LIGHT) * tilt_depth + coefficient(LIGHT + 1) * tilt_rows + coefficient(LIGHT + 2) * tilt_cols
    facing = slope * lax.rsqrt(1.0 + tilt_depth * tilt_depth + tilt_rows * tilt_rows + tilt_cols * tilt_cols)
    shading = 0.25 + 1.5 * jnp.maximum(facing, 0.0)
    optical = extinction * (jnp.maximum(centre, 0.0) + jnp.log1p(jnp.exp(-jnp.abs(centre))))
    strength = opacity_of(optical) * shading
    tones = [jax.nn.sigmoid(coefficient(GAIN + i) * centre + coefficient(BIAS + i)) for i in range(3)]
    return [strength * tone for tone in tones] + [optical]


def load_kernel(density, own, first, semaphore):
    copy = pltpu.make_async_copy(density, own, semaphore)
    copy.start()
    copy.wait()
    first[...] = own[:2]


def inner_kernel(*refs):
    arguments, (own, coming, _, fields, table, masks, starts), scalars, semaphores = refs[:5], refs[5:12], refs[12:17], refs[17]
    copies = [pltpu.make_async_copy(arguments[i], scalars[i], semaphores.at[i]) for i in range(5)]
    for copy in copies:
        copy.start()
    depth, height = lax.axis_index("depth"), lax.axis_index("height")
    for copy in copies:
        copy.wait()
    light, gain, bias, shear, reverse = scalars
    extinction = EXTINCTION / (PLANES * GROUPS)
    beyond = jnp.where(height == BRICKS - 1, 0.0, extinction)
    following = jnp.where(depth == GROUPS - 1, 0.0, extinction)
    both = jnp.where(depth == GROUPS - 1, 0.0, beyond)
    values_of = [ref[i] for ref in (light, gain, bias) for i in range(3)] + [extinction, beyond, following, both]
    for row, scalar in enumerate(values_of):
        table[row : row + 1, :] = jnp.full((1, COLS), scalar, jnp.float32)
    upper = lax.broadcasted_iota(jnp.int32, (8, COLS), 0) < SHARE
    core = depth % 2
    for base, digit in ((FRONT, core), (BACK, 1 - core)):
        for pair in range(VIEWS // 2):
            first = jnp.where(reverse[2 * pair] == digit, 1.0, 0.0)
            second = jnp.where(reverse[2 * pair + 1] == digit, 1.0, 0.0)
            masks[base + pair] = jnp.where(upper, first, second)
    masks[CORE] = jnp.full((8, COLS), core, jnp.float32)
    first = jnp.where(depth == 0, 0, 1)
    starts[FIRST] = first
    for view in range(VIEWS):
        for step in range(SLABS):
            slot = jnp.where(reverse[view] == 1, SLABS - 1 - step, jnp.minimum(first + step, SLABS - 1))
            offset = lax.shift_right_logical((depth * PLANES + slot) * shear[view], 7)
            starts[view * SLABS + step] = slot * TALL + jnp.minimum(offset, SHEAR)

    coefficient = lambda at: values_of[at]

    def plane_of(plane, _):
        shade_inner(coefficient, extinction, own.at[plane], own[plane - 1, INNER, :], own[plane + 1, INNER, :], fields, plane)
        return 0

    lax.fori_loop(1, PLANES - 1, plane_of, 0)
    last = own.at[PLANES - 1]
    shade_inner(coefficient, extinction, last, own[PLANES - 2, INNER, :], coming[0, INNER, :], fields, PLANES - 1)
    shade_inner(coefficient, following, coming.at[0], last[INNER, :], coming[1, INNER, :], fields, PLANES)

    @pl.when(depth == 0)
    def _():
        shade_inner(coefficient, extinction, own.at[0], 0.0, own[1, INNER, :], fields, 0)


def shade_inner(coefficient, extinction, plane, before, after, fields, slot):
    centre = plane[INNER, :]
    values = shade(coefficient, extinction, centre, plane[7 : ROWS - 9, :], plane[9 : ROWS - 7, :], before, after)
    store(fields, slot, 8, values)


def store(fields, slot, row, values):
    rows = pl.ds(pl.multiple_of(slot * TALL + row, 8), values[0].shape[0])
    for kind in range(4):
        fields[kind, rows, :] = values[kind]


def cut_kernel(own, pair, across, coming, high, low):
    odd = lax.axis_index("depth") % 2 == 1
    coming[...] = jnp.where(odd, across[...], pair[1])
    high[:PLANES] = own[:, :SHEAR, :]
    high[PLANES:] = coming[:, :SHEAR, :]
    for plane in range(PLANES):
        low[plane : plane + 1, :] = own[plane, ROWS - 1 : ROWS, :]
    low[PLANES:, :] = jnp.broadcast_to(coming[0, ROWS - 1 : ROWS, :], (8, COLS))


def render_kernel(
    table, masks, starts_in, own, coming, high, held, given, kept, fields, brick, starts, semaphore
):
    del held
    copy = pltpu.make_async_copy(starts_in, starts, semaphore)
    copy.start()
    coefficient = lambda at: table[at : at + 1, :]
    for plane in range(PLANES + 2):
        source = own.at[plane] if plane < PLANES else coming.at[plane - PLANES]
        brick[plane, :16, :] = source[ROWS - 16 :, :]
        brick[plane, 16 : 16 + SHEAR, :] = high[plane]
        brick[plane, 16 + SHEAR :, :] = jnp.zeros((8, COLS), jnp.float32)

    def rows_of(slot, before, plain, beyond):
        for start, count, extinction in ((8, 8, plain), (16, SHEAR, beyond)):
            values = shade(
                coefficient,
                coefficient(extinction),
                brick[slot, start : start + count, :],
                brick[slot, start - 1 : start - 1 + count, :],
                brick[slot, start + 1 : start + 1 + count, :],
                0.0 if before is None else brick[before, start : start + count, :],
                brick[slot + 1, start : start + count, :],
            )
            store(fields, slot, ROWS - 16 + start, values)

    def plane_of(plane, _):
        rows_of(plane, plane - 1, PLAIN, BEYOND)
        return 0

    lax.fori_loop(1, PLANES, plane_of, 0)
    rows_of(PLANES, PLANES - 1, NEXT, NEXT_BEYOND)

    @pl.when(lax.axis_index("depth") == 0)
    def _():
        rows_of(0, None, PLAIN, BEYOND)

    copy.wait()
    render(masks, starts, fields, given, kept, 1, ROWS // 8)


def first_kernel(table, masks, starts_in, own, coming, low, held, *refs):
    del held
    given, kept, fields, starts, semaphore = refs[2:]
    copy = pltpu.make_async_copy(starts_in, starts, semaphore)
    copy.start()
    coefficient = lambda at: table[at : at + 1, :]
    top = lax.broadcasted_iota(jnp.int32, (8, COLS), 0) == 0

    def first_rows(slot):
        plane_at = lambda plane: own.at[plane] if plane < PLANES else coming.at[plane - PLANES]
        plane = plane_at(slot)
        centre = plane[:8, :]
        above = jnp.where(top, low[slot : slot + 1, :], pltpu.roll(centre, 1, 0))
        before = 0.0 if slot == 0 else plane_at(slot - 1)[:8, :]
        extinction = coefficient(NEXT if slot == PLANES else PLAIN)
        store(fields, slot, 0, shade(coefficient, extinction, centre, above, plane[1:9, :], before, plane_at(slot + 1)[:8, :]))

    for slot in range(1, SLABS):
        first_rows(slot)

    @pl.when(lax.axis_index("depth") == 0)
    def _():
        first_rows(0)

    copy.wait()
    render(masks, starts, fields, given, kept, 0, 1)


def render(masks, starts, fields, given, kept, tile, tiles):
    upper = lax.broadcasted_iota(jnp.int32, (8, COLS), 0) < SHARE
    odd = masks[CORE] > 0.5

    def of(planes):
        def tile_of(tile, _):
            for pair in range(VIEWS // 2):
                sums = []
                for view in (2 * pair, 2 * pair + 1):
                    red = green = blue = optical = jnp.zeros((8, COLS), jnp.float32)
                    for step in range(planes):
                        rows = pl.ds(starts[view * SLABS + step] + 8 * tile, 8)
                        through = jnp.exp(-optical)
                        red = red + fields[0, rows, :] * through
                        green = green + fields[1, rows, :] * through
                        blue = blue + fields[2, rows, :] * through
                        optical = optical + fields[3, rows, :]
                    sums.append((red, green, blue, optical))
                for kind in range(4):
                    first, second = sums[0][kind], sums[1][kind]
                    even_rows = jnp.where(upper, first, pltpu.roll(second, SHARE, 0))
                    odd_rows = jnp.where(upper, pltpu.roll(first, SHARE, 0), second)
                    kept[tile, kind, pair] = jnp.where(odd, odd_rows, even_rows)
                    given[tile, kind, pair] = jnp.where(odd, even_rows, odd_rows)
            return 0

        lax.fori_loop(tile, tiles, tile_of, 0)

    leading = starts[FIRST] == 0

    @pl.when(leading)
    def _():
        of(SLABS)

    @pl.when(jnp.logical_not(leading))
    def _():
        of(PLANES)


def merge_kernel(masks, kept, gathered, out):
    odd = masks[CORE] > 0.5
    core = lax.axis_index("depth") % 2
    for pair in range(VIEWS // 2):
        mine_front = masks[FRONT + pair] > 0.5

        def merge(chip, _):
            place = jnp.where(core == 1, CHIPS - 1 - chip, chip)
            mine = [kept[chip, kind, pair] for kind in range(4)]
            other = [jnp.where(odd, gathered[0, chip, kind, pair], gathered[1, chip, kind, pair]) for kind in range(4)]
            through = jnp.exp(-jnp.where(mine_front, mine[3], other[3]))
            for kind in range(3):
                front = jnp.where(mine_front, mine[kind], other[kind])
                behind = jnp.where(mine_front, other[kind], mine[kind])
                out[place, kind, pair] = front + through * behind
            out[place, 3, pair] = mine[3] + other[3]
            return 0

        lax.fori_loop(0, CHIPS, merge, 0, unroll=True)


def final_kernel(masks, slabs, out):
    for pair in range(VIEWS // 2):
        backward = masks[BACK + pair] > 0.5
        optical = [slabs[chip, 3, pair] for chip in range(CHIPS)]
        ahead, behind = [jnp.zeros((8, COLS), jnp.float32)], [jnp.zeros((8, COLS), jnp.float32)]
        for chip in range(CHIPS - 1):
            ahead.append(ahead[-1] + optical[chip])
            behind.append(behind[-1] + optical[CHIPS - 1 - chip])
        total = ahead[-1] + optical[-1]
        sums = [jnp.zeros((8, COLS), jnp.float32)] * 3
        for chip in range(CHIPS):
            through = jnp.exp(-jnp.where(backward, behind[CHIPS - 1 - chip], ahead[chip]))
            sums = [sums[kind] + slabs[chip, kind, pair] * through for kind in range(3)]
        cover = jnp.where(total < 0.0625, opacity_of(total), 1.0 - jnp.exp(-total))
        for kind, value in enumerate((*sums, cover)):
            out[kind, 2 * pair] = value[:SHARE]
            out[kind, 2 * pair + 1] = value[SHARE:]


def kernel(body, name, out_shape, in_specs, out_specs, flops=0, **more):
    estimate = pl.CostEstimate(flops=flops, bytes_accessed=2**20, transcendentals=0)
    return pl.pallas_call(
        body,
        out_shape=out_shape,
        in_specs=in_specs,
        out_specs=out_specs,
        compiler_params=PARAMS,
        cost_estimate=estimate,
        name=name,
        **more,
    )


def on_device(density, light_vector, colour_gain, colour_bias, shear_step, reverse_view):
    heights, depths = lax.axis_size("height"), lax.axis_size("depth")

    own, first = kernel(
        load_kernel,
        "load",
        (array(PLANES, ROWS, COLS), array(2, ROWS, COLS)),
        [HBM],
        (VMEM,) * 2,
        flops=10**9,
        scratch_shapes=[pltpu.SemaphoreType.DMA],
    )(density)
    cores = [[2 * chip, 2 * chip + 1] for chip in range(CHIPS)]
    across = lax.ppermute(first, "depth", [(i + 1, i) for i in range(1, depths - 1, 2)])
    pair = lax.all_gather(first, "depth", axis=0, axis_index_groups=cores)

    coming, own_high, own_low = kernel(
        cut_kernel,
        "cut",
        (array(2, ROWS, COLS), array(PLANES + 2, SHEAR, COLS), array(PLANES + 8, COLS)),
        [VMEM] * 3,
        (VMEM,) * 3,
    )(own, pair, across)
    high = lax.ppermute(own_high, "height", [(i + 1, i) for i in range(heights - 1)])
    low = lax.ppermute(own_low, "height", [(i, i + 1) for i in range(heights - 1)])

    shaded = array(4, SLABS * TALL, COLS)
    fields, table, masks, starts = kernel(
        inner_kernel,
        "inner",
        (shaded, array(16, COLS), array(5, 8, COLS), jax.ShapeDtypeStruct((64,), jnp.int32)),
        [HBM] * 5 + [VMEM] * 3,
        (VMEM, VMEM, VMEM, SMEM),
        flops=10**7,
        scratch_shapes=[pltpu.SMEM((3,), jnp.float32)] * 3
        + [pltpu.SMEM((VIEWS,), jnp.int32)] * 2
        + [pltpu.SemaphoreType.DMA((5,))],
    )(light_vector, colour_gain, colour_bias, shear_step, reverse_view, own, coming, own_low)
    part = array(CHIPS, 4, VIEWS // 2, 8, COLS)
    memory = [pltpu.SMEM((64,), jnp.int32), pltpu.SemaphoreType.DMA]
    given, kept, fields = kernel(
        render_kernel,
        "render",
        (part, part, shaded),
        [VMEM, VMEM, ANY] + [VMEM] * 4,
        (VMEM,) * 3,
        flops=10**7,
        input_output_aliases={6: 2},
        scratch_shapes=[pltpu.VMEM((PLANES + 2, 24 + SHEAR, COLS), jnp.float32), *memory],
    )(table, masks, starts, own, coming, high, fields)
    given, kept, _ = kernel(
        first_kernel,
        "first",
        (part, part, shaded),
        [VMEM, VMEM, ANY] + [VMEM] * 6,
        (VMEM,) * 3,
        input_output_aliases={6: 2, 7: 0, 8: 1},
        scratch_shapes=memory,
    )(table, masks, starts, own, coming, low, fields, given, kept)

    gathered = lax.all_gather(given, "depth", axis=0, axis_index_groups=cores)
    merged = kernel(merge_kernel, "merge", part, [VMEM] * 3, VMEM)(masks, kept, gathered)
    chips = [[2 * chip for chip in range(CHIPS)], [2 * chip + 1 for chip in reversed(range(CHIPS))]]
    slabs = lax.all_to_all(merged, "depth", 0, 0, tiled=True, axis_index_groups=chips)
    return kernel(final_kernel, "composite", array(4, VIEWS, SHARE, COLS), [VMEM] * 2, VMEM)(masks, slabs)


def solution(mesh):
    placed = (P("depth", "height", None), P(), P(), P(), P(), P())
    return jax.shard_map(
        on_device,
        mesh=mesh,
        in_specs=placed,
        out_specs=P(None, None, ("height", "depth"), None),
        check_vma=False,
    )
```

```python
import jax
import jax.numpy as jnp
from jax import lax
from jax.experimental import pallas as pl
from jax.experimental.pallas import tpu as pltpu
from jax.sharding import PartitionSpec as P

EXTINCTION = 2.5
SMEM = pl.BlockSpec(memory_space=pltpu.SMEM)
VMEM = pl.BlockSpec(memory_space=pltpu.VMEM)
ANY = pl.BlockSpec(memory_space=pl.ANY)
HBM = pl.BlockSpec(memory_space=pltpu.HBM)
PLANES, ROWS, COLS, SHEAR, VIEWS, GROUPS, BRICKS = 8, 64, 128, 32, 4, 16, 32
TALL = ROWS + SHEAR
SLABS = PLANES + 1
CHIPS = GROUPS // 2
SHARE = ROWS // GROUPS
ORDERS = ((7, 6, 5, 4, 3, 2, 1, 0), (7, 6, 5, 4, 3, 2, 1, 0))
PARAMS = pltpu.CompilerParams(vmem_limit_bytes=8 * 2**20)
LIGHT, GAIN, BIAS, PLAIN, BEYOND, NEXT, NEXT_BEYOND = 0, 3, 6, 9, 10, 11, 12
FRONT, BACK, CORE = 0, 2, 4
INNER = slice(8, ROWS - 8)
FIRST = VIEWS * SLABS


def array(*shape):
    return jax.ShapeDtypeStruct(shape, jnp.float32)


def opacity_of(optical):
    series = 1.0 - optical * (1.0 / 6.0)
    for term in (5.0, 4.0, 3.0, 2.0):
        series = 1.0 - optical * (1.0 / term) * series
    return optical * series


def shade(coefficient, extinction, centre, above, below, before, after):
    lane = lax.broadcasted_iota(jnp.int32, centre.shape, 1)
    tilt_rows = 0.5 * (below - above)
    tilt_depth = 0.5 * (after - before)
    right = jnp.where(lane == COLS - 1, 0.0, pltpu.roll(centre, COLS - 1, 1))
    left = jnp.where(lane == 0, 0.0, pltpu.roll(centre, 1, 1))
    tilt_cols = 0.5 * (right - left)
    slope = coefficient(LIGHT) * tilt_depth + coefficient(LIGHT + 1) * tilt_rows + coefficient(LIGHT + 2) * tilt_cols
    facing = slope * lax.rsqrt(1.0 + tilt_depth * tilt_depth + tilt_rows * tilt_rows + tilt_cols * tilt_cols)
    shading = 0.25 + 1.5 * jnp.maximum(facing, 0.0)
    optical = extinction * (jnp.maximum(centre, 0.0) + jnp.log1p(jnp.exp(-jnp.abs(centre))))
    strength = opacity_of(optical) * shading
    tones = [jax.nn.sigmoid(coefficient(GAIN + i) * centre + coefficient(BIAS + i)) for i in range(3)]
    return [strength * tone for tone in tones] + [optical]


def load_kernel(density, own, first, semaphore):
    copy = pltpu.make_async_copy(density, own, semaphore)
    copy.start()
    copy.wait()
    first[...] = own[:2]


def inner_kernel(*refs):
    arguments, (own, coming, _, fields, table, masks, starts), scalars, semaphores = refs[:5], refs[5:12], refs[12:17], refs[17]
    copies = [pltpu.make_async_copy(arguments[i], scalars[i], semaphores.at[i]) for i in range(5)]
    for copy in copies:
        copy.start()
    depth, height = lax.axis_index("depth"), lax.axis_index("height")
    for copy in copies:
        copy.wait()
    light, gain, bias, shear, reverse = scalars
    extinction = EXTINCTION / (PLANES * GROUPS)
    beyond = jnp.where(height == BRICKS - 1, 0.0, extinction)
    following = jnp.where(depth == GROUPS - 1, 0.0, extinction)
    both = jnp.where(depth == GROUPS - 1, 0.0, beyond)
    values_of = [ref[i] for ref in (light, gain, bias) for i in range(3)] + [extinction, beyond, following, both]
    for row, scalar in enumerate(values_of):
        table[row : row + 1, :] = jnp.full((1, COLS), scalar, jnp.float32)
    upper = lax.broadcasted_iota(jnp.int32, (8, COLS), 0) < SHARE
    core = depth % 2
    for base, digit in ((FRONT, core), (BACK, 1)):
        for pair in range(VIEWS // 2):
            first = jnp.where(reverse[2 * pair] == digit, 1.0, 0.0)
            second = jnp.where(reverse[2 * pair + 1] == digit, 1.0, 0.0)
            masks[base + pair] = jnp.where(upper, first, second)
    masks[CORE] = jnp.full((8, COLS), core, jnp.float32)
    first = jnp.where(depth == 0, 0, 1)
    starts[FIRST] = first
    for view in range(VIEWS):
        for step in range(SLABS):
            slot = jnp.where(reverse[view] == 1, SLABS - 1 - step, jnp.minimum(first + step, SLABS - 1))
            offset = lax.shift_right_logical((depth * PLANES + slot) * shear[view], 7)
            starts[view * SLABS + step] = slot * TALL + jnp.minimum(offset, SHEAR)

    coefficient = lambda at: values_of[at]

    def plane_of(plane, _):
        shade_inner(coefficient, extinction, own.at[plane], own[plane - 1, INNER, :], own[plane + 1, INNER, :], fields, plane)
        return 0

    lax.fori_loop(1, PLANES - 1, plane_of, 0)
    last = own.at[PLANES - 1]
    shade_inner(coefficient, extinction, last, own[PLANES - 2, INNER, :], coming[0, INNER, :], fields, PLANES - 1)
    shade_inner(coefficient, following, coming.at[0], last[INNER, :], coming[1, INNER, :], fields, PLANES)

    @pl.when(depth == 0)
    def _():
        shade_inner(coefficient, extinction, own.at[0], 0.0, own[1, INNER, :], fields, 0)


def shade_inner(coefficient, extinction, plane, before, after, fields, slot):
    centre = plane[INNER, :]
    values = shade(coefficient, extinction, centre, plane[7 : ROWS - 9, :], plane[9 : ROWS - 7, :], before, after)
    store(fields, slot, 8, values)


def store(fields, slot, row, values):
    rows = pl.ds(pl.multiple_of(slot * TALL + row, 8), values[0].shape[0])
    for kind in range(4):
        fields[kind, rows, :] = values[kind]


def cut_kernel(own, pair, across, coming, high, low):
    odd = lax.axis_index("depth") % 2 == 1
    coming[...] = jnp.where(odd, across[...], pair[1])
    high[:PLANES] = own[:, :SHEAR, :]
    high[PLANES:] = coming[:, :SHEAR, :]
    for plane in range(PLANES):
        low[plane : plane + 1, :] = own[plane, ROWS - 1 : ROWS, :]
    low[PLANES:, :] = jnp.broadcast_to(coming[0, ROWS - 1 : ROWS, :], (8, COLS))


def render_kernel(
    table, masks, starts_in, own, coming, high, held, given, kept, fields, brick, starts, semaphore
):
    del held
    copy = pltpu.make_async_copy(starts_in, starts, semaphore)
    copy.start()
    coefficient = lambda at: table[at : at + 1, :]
    for plane in range(PLANES + 2):
        source = own.at[plane] if plane < PLANES else coming.at[plane - PLANES]
        brick[plane, :16, :] = source[ROWS - 16 :, :]
        brick[plane, 16 : 16 + SHEAR, :] = high[plane]
        brick[plane, 16 + SHEAR :, :] = jnp.zeros((8, COLS), jnp.float32)

    def rows_of(slot, before, plain, beyond):
        for start, count, extinction in ((8, 8, plain), (16, SHEAR, beyond)):
            values = shade(
                coefficient,
                coefficient(extinction),
                brick[slot, start : start + count, :],
                brick[slot, start - 1 : start - 1 + count, :],
                brick[slot, start + 1 : start + 1 + count, :],
                0.0 if before is None else brick[before, start : start + count, :],
                brick[slot + 1, start : start + count, :],
            )
            store(fields, slot, ROWS - 16 + start, values)

    def plane_of(plane, _):
        rows_of(plane, plane - 1, PLAIN, BEYOND)
        return 0

    lax.fori_loop(1, PLANES, plane_of, 0)
    rows_of(PLANES, PLANES - 1, NEXT, NEXT_BEYOND)

    @pl.when(lax.axis_index("depth") == 0)
    def _():
        rows_of(0, None, PLAIN, BEYOND)

    copy.wait()
    render(masks, starts, fields, given, kept, 1, ROWS // 8)


def first_kernel(table, masks, starts_in, own, coming, low, held, *refs):
    del held
    given, kept, fields, starts, semaphore = refs[2:]
    copy = pltpu.make_async_copy(starts_in, starts, semaphore)
    copy.start()
    coefficient = lambda at: table[at : at + 1, :]
    top = lax.broadcasted_iota(jnp.int32, (8, COLS), 0) == 0

    def first_rows(slot):
        plane_at = lambda plane: own.at[plane] if plane < PLANES else coming.at[plane - PLANES]
        plane = plane_at(slot)
        centre = plane[:8, :]
        above = jnp.where(top, low[slot : slot + 1, :], pltpu.roll(centre, 1, 0))
        before = 0.0 if slot == 0 else plane_at(slot - 1)[:8, :]
        extinction = coefficient(NEXT if slot == PLANES else PLAIN)
        store(fields, slot, 0, shade(coefficient, extinction, centre, above, plane[1:9, :], before, plane_at(slot + 1)[:8, :]))

    for slot in range(1, SLABS):
        first_rows(slot)

    @pl.when(lax.axis_index("depth") == 0)
    def _():
        first_rows(0)

    copy.wait()
    render(masks, starts, fields, given, kept, 0, 1)


def render(masks, starts, fields, given, kept, tile, tiles):
    upper = lax.broadcasted_iota(jnp.int32, (8, COLS), 0) < SHARE
    odd = masks[CORE] > 0.5

    def of(planes):
        def tile_of(tile, _):
            for pair in range(VIEWS // 2):
                sums = []
                for view in (2 * pair, 2 * pair + 1):
                    red = green = blue = optical = jnp.zeros((8, COLS), jnp.float32)
                    for step in range(planes):
                        rows = pl.ds(starts[view * SLABS + step] + 8 * tile, 8)
                        through = jnp.exp(-optical)
                        red = red + fields[0, rows, :] * through
                        green = green + fields[1, rows, :] * through
                        blue = blue + fields[2, rows, :] * through
                        optical = optical + fields[3, rows, :]
                    sums.append((red, green, blue, optical))
                for kind in range(4):
                    first, second = sums[0][kind], sums[1][kind]
                    even_rows = jnp.where(upper, first, pltpu.roll(second, SHARE, 0))
                    odd_rows = jnp.where(upper, pltpu.roll(first, SHARE, 0), second)
                    kept[tile, kind, pair] = jnp.where(odd, odd_rows, even_rows)
                    given[tile, kind, pair] = jnp.where(odd, even_rows, odd_rows)
            return 0

        lax.fori_loop(tile, tiles, tile_of, 0)

    leading = starts[FIRST] == 0

    @pl.when(leading)
    def _():
        of(SLABS)

    @pl.when(jnp.logical_not(leading))
    def _():
        of(PLANES)


def place_of(core, chip):
    return jnp.where(core == 1, ORDERS[1].index(chip), ORDERS[0].index(chip))


def merge_kernel(masks, kept, gathered, out):
    odd = masks[CORE] > 0.5
    core = lax.axis_index("depth") % 2
    for pair in range(VIEWS // 2):
        mine_front = masks[FRONT + pair] > 0.5

        for chip in range(CHIPS):
            place = place_of(core, chip)
            mine = [kept[chip, kind, pair] for kind in range(4)]
            other = [jnp.where(odd, gathered[0, chip, kind, pair], gathered[1, chip, kind, pair]) for kind in range(4)]
            through = jnp.exp(-jnp.where(mine_front, mine[3], other[3]))
            for kind in range(3):
                front = jnp.where(mine_front, mine[kind], other[kind])
                behind = jnp.where(mine_front, other[kind], mine[kind])
                out[place, kind, pair] = front + through * behind
            out[place, 3, pair] = mine[3] + other[3]


def final_kernel(masks, slabs, out):
    places = [place_of(lax.axis_index("depth") % 2, chip) for chip in range(CHIPS)]
    for pair in range(VIEWS // 2):
        backward = masks[BACK + pair] > 0.5
        optical = [slabs[place, 3, pair] for place in places]
        ahead, behind = [jnp.zeros((8, COLS), jnp.float32)], [jnp.zeros((8, COLS), jnp.float32)]
        for chip in range(CHIPS - 1):
            ahead.append(ahead[-1] + optical[chip])
            behind.append(behind[-1] + optical[CHIPS - 1 - chip])
        total = ahead[-1] + optical[-1]
        sums = [jnp.zeros((8, COLS), jnp.float32)] * 3
        for chip in range(CHIPS):
            through = jnp.exp(-jnp.where(backward, behind[CHIPS - 1 - chip], ahead[chip]))
            sums = [sums[kind] + slabs[places[chip], kind, pair] * through for kind in range(3)]
        cover = jnp.where(total < 0.0625, opacity_of(total), 1.0 - jnp.exp(-total))
        for kind, value in enumerate((*sums, cover)):
            out[kind, 2 * pair] = value[:SHARE]
            out[kind, 2 * pair + 1] = value[SHARE:]


def kernel(body, name, out_shape, in_specs, out_specs, flops=0, **more):
    estimate = pl.CostEstimate(flops=flops, bytes_accessed=2**20, transcendentals=0)
    return pl.pallas_call(
        body,
        out_shape=out_shape,
        in_specs=in_specs,
        out_specs=out_specs,
        compiler_params=PARAMS,
        cost_estimate=estimate,
        name=name,
        **more,
    )


def on_device(density, light_vector, colour_gain, colour_bias, shear_step, reverse_view):
    heights, depths = lax.axis_size("height"), lax.axis_size("depth")

    own, first = kernel(
        load_kernel,
        "load",
        (array(PLANES, ROWS, COLS), array(2, ROWS, COLS)),
        [HBM],
        (VMEM,) * 2,
        flops=10**9,
        scratch_shapes=[pltpu.SemaphoreType.DMA],
    )(density)
    cores = [[2 * chip, 2 * chip + 1] for chip in range(CHIPS)]
    across = lax.ppermute(first, "depth", [(i + 1, i) for i in range(1, depths - 1, 2)])
    pair = lax.all_gather(first, "depth", axis=0, axis_index_groups=cores)

    coming, own_high, own_low = kernel(
        cut_kernel,
        "cut",
        (array(2, ROWS, COLS), array(PLANES + 2, SHEAR, COLS), array(PLANES + 8, COLS)),
        [VMEM] * 3,
        (VMEM,) * 3,
    )(own, pair, across)
    high = lax.ppermute(own_high, "height", [(i + 1, i) for i in range(heights - 1)])
    low = lax.ppermute(own_low, "height", [(i, i + 1) for i in range(heights - 1)])

    shaded = array(4, SLABS * TALL, COLS)
    fields, table, masks, starts = kernel(
        inner_kernel,
        "inner",
        (shaded, array(16, COLS), array(5, 8, COLS), jax.ShapeDtypeStruct((64,), jnp.int32)),
        [HBM] * 5 + [VMEM] * 3,
        (VMEM, VMEM, VMEM, SMEM),
        flops=10**7,
        scratch_shapes=[pltpu.SMEM((3,), jnp.float32)] * 3
        + [pltpu.SMEM((VIEWS,), jnp.int32)] * 2
        + [pltpu.SemaphoreType.DMA((5,))],
    )(light_vector, colour_gain, colour_bias, shear_step, reverse_view, own, coming, own_low)
    part = array(CHIPS, 4, VIEWS // 2, 8, COLS)
    memory = [pltpu.SMEM((64,), jnp.int32), pltpu.SemaphoreType.DMA]
    given, kept, fields = kernel(
        render_kernel,
        "render",
        (part, part, shaded),
        [VMEM, VMEM, ANY] + [VMEM] * 4,
        (VMEM,) * 3,
        flops=10**7,
        input_output_aliases={6: 2},
        scratch_shapes=[pltpu.VMEM((PLANES + 2, 24 + SHEAR, COLS), jnp.float32), *memory],
    )(table, masks, starts, own, coming, high, fields)
    given, kept, _ = kernel(
        first_kernel,
        "first",
        (part, part, shaded),
        [VMEM, VMEM, ANY] + [VMEM] * 6,
        (VMEM,) * 3,
        input_output_aliases={6: 2, 7: 0, 8: 1},
        scratch_shapes=memory,
    )(table, masks, starts, own, coming, low, fields, given, kept)

    gathered = lax.all_gather(given, "depth", axis=0, axis_index_groups=cores)
    merged = kernel(merge_kernel, "merge", part, [VMEM] * 3, VMEM)(masks, kept, gathered)
    groups = [[2 * chip + core for chip in ORDERS[core]] for core in range(2)]
    slabs = lax.all_to_all(merged, "depth", 0, 0, tiled=True, axis_index_groups=groups)
    return kernel(final_kernel, "composite", array(4, VIEWS, SHARE, COLS), [VMEM] * 2, VMEM)(masks, slabs)


def solution(mesh):
    placed = (P("depth", "height", None), P(), P(), P(), P(), P())
    return jax.shard_map(
        on_device,
        mesh=mesh,
        in_specs=placed,
        out_specs=P(None, None, ("height", "depth"), None),
        check_vma=False,
    )
```

```python
import jax
import jax.numpy as jnp
from jax import lax
from jax.experimental import pallas as pl
from jax.experimental.pallas import tpu as pltpu
from jax.sharding import PartitionSpec as P

EXTINCTION = 2.5
SMEM = pl.BlockSpec(memory_space=pltpu.SMEM)
VMEM = pl.BlockSpec(memory_space=pltpu.VMEM)
ANY = pl.BlockSpec(memory_space=pl.ANY)
HBM = pl.BlockSpec(memory_space=pltpu.HBM)
PLANES, ROWS, COLS, SHEAR, VIEWS, GROUPS, BRICKS = 8, 64, 128, 32, 4, 16, 32
TALL = ROWS + SHEAR
SLABS = PLANES + 1
CHIPS = GROUPS // 2
SHARE = ROWS // GROUPS
ORDERS = ((7, 6, 5, 4, 3, 2, 1, 0), (7, 6, 5, 4, 3, 2, 1, 0))
PARAMS = pltpu.CompilerParams(vmem_limit_bytes=8 * 2**20)
LIGHT, GAIN, BIAS, PLAIN, BEYOND, NEXT, NEXT_BEYOND = 0, 3, 6, 9, 10, 11, 12
FRONT, BACK, CORE = 0, 2, 4
INNER = slice(8, ROWS - 8)
FIRST = VIEWS * SLABS


def array(*shape):
    return jax.ShapeDtypeStruct(shape, jnp.float32)


def opacity_of(optical):
    series = 1.0 - optical * (1.0 / 6.0)
    for term in (5.0, 4.0, 3.0, 2.0):
        series = 1.0 - optical * (1.0 / term) * series
    return optical * series


def shade(coefficient, extinction, centre, above, below, before, after):
    lane = lax.broadcasted_iota(jnp.int32, centre.shape, 1)
    tilt_rows = 0.5 * (below - above)
    tilt_depth = 0.5 * (after - before)
    right = jnp.where(lane == COLS - 1, 0.0, pltpu.roll(centre, COLS - 1, 1))
    left = jnp.where(lane == 0, 0.0, pltpu.roll(centre, 1, 1))
    tilt_cols = 0.5 * (right - left)
    slope = coefficient(LIGHT) * tilt_depth + coefficient(LIGHT + 1) * tilt_rows + coefficient(LIGHT + 2) * tilt_cols
    facing = slope * lax.rsqrt(1.0 + tilt_depth * tilt_depth + tilt_rows * tilt_rows + tilt_cols * tilt_cols)
    shading = 0.25 + 1.5 * jnp.maximum(facing, 0.0)
    optical = extinction * (jnp.maximum(centre, 0.0) + jnp.log1p(jnp.exp(-jnp.abs(centre))))
    strength = opacity_of(optical) * shading
    tones = [jax.nn.sigmoid(coefficient(GAIN + i) * centre + coefficient(BIAS + i)) for i in range(3)]
    return [strength * tone for tone in tones] + [optical]


def load_kernel(density, own, first, semaphore):
    copy = pltpu.make_async_copy(density, own, semaphore)
    copy.start()
    copy.wait()
    first[...] = own[:2]


def inner_kernel(*refs):
    arguments, (own, coming, _, fields, table, masks, starts), scalars, semaphores = refs[:5], refs[5:12], refs[12:17], refs[17]
    copies = [pltpu.make_async_copy(arguments[i], scalars[i], semaphores.at[i]) for i in range(5)]
    for copy in copies:
        copy.start()
    depth, height = lax.axis_index("depth"), lax.axis_index("height")
    for copy in copies:
        copy.wait()
    light, gain, bias, shear, reverse = scalars
    extinction = EXTINCTION / (PLANES * GROUPS)
    beyond = jnp.where(height == BRICKS - 1, 0.0, extinction)
    following = jnp.where(depth == GROUPS - 1, 0.0, extinction)
    both = jnp.where(depth == GROUPS - 1, 0.0, beyond)
    values_of = [ref[i] for ref in (light, gain, bias) for i in range(3)] + [extinction, beyond, following, both]
    for row, scalar in enumerate(values_of):
        table[row : row + 1, :] = jnp.full((1, COLS), scalar, jnp.float32)
    upper = lax.broadcasted_iota(jnp.int32, (8, COLS), 0) < SHARE
    core = depth % 2
    for base, digit in ((FRONT, core), (BACK, 1)):
        for pair in range(VIEWS // 2):
            first = jnp.where(reverse[2 * pair] == digit, 1.0, 0.0)
            second = jnp.where(reverse[2 * pair + 1] == digit, 1.0, 0.0)
            masks[base + pair] = jnp.where(upper, first, second)
    masks[CORE] = jnp.full((8, COLS), core, jnp.float32)
    first = jnp.where(depth == 0, 0, 1)
    starts[FIRST] = first
    for view in range(VIEWS):
        for step in range(SLABS):
            slot = jnp.where(reverse[view] == 1, SLABS - 1 - step, jnp.minimum(first + step, SLABS - 1))
            offset = lax.shift_right_logical((depth * PLANES + slot) * shear[view], 7)
            starts[view * SLABS + step] = slot * TALL + jnp.minimum(offset, SHEAR)

    coefficient = lambda at: values_of[at]

    def plane_of(plane, _):
        shade_inner(coefficient, extinction, own.at[plane], own[plane - 1, INNER, :], own[plane + 1, INNER, :], fields, plane)
        return 0

    lax.fori_loop(1, PLANES - 1, plane_of, 0)
    last = own.at[PLANES - 1]
    shade_inner(coefficient, extinction, last, own[PLANES - 2, INNER, :], coming[0, INNER, :], fields, PLANES - 1)
    shade_inner(coefficient, following, coming.at[0], last[INNER, :], coming[1, INNER, :], fields, PLANES)

    @pl.when(depth == 0)
    def _():
        shade_inner(coefficient, extinction, own.at[0], 0.0, own[1, INNER, :], fields, 0)


def shade_inner(coefficient, extinction, plane, before, after, fields, slot):
    centre = plane[INNER, :]
    values = shade(coefficient, extinction, centre, plane[7 : ROWS - 9, :], plane[9 : ROWS - 7, :], before, after)
    store(fields, slot, 8, values)


def store(fields, slot, row, values):
    rows = pl.ds(pl.multiple_of(slot * TALL + row, 8), values[0].shape[0])
    for kind in range(4):
        fields[kind, rows, :] = values[kind]


def cut_kernel(own, coming, high, low):
    high[:PLANES] = own[:, :SHEAR, :]
    high[PLANES:] = coming[:, :SHEAR, :]
    for plane in range(PLANES):
        low[plane : plane + 1, :] = own[plane, ROWS - 1 : ROWS, :]
    low[PLANES:, :] = jnp.broadcast_to(coming[0, ROWS - 1 : ROWS, :], (8, COLS))


def render_kernel(
    table, masks, starts_in, own, coming, high, held, given, kept, fields, brick, starts, semaphore
):
    del held
    copy = pltpu.make_async_copy(starts_in, starts, semaphore)
    copy.start()
    coefficient = lambda at: table[at : at + 1, :]
    for plane in range(PLANES + 2):
        source = own.at[plane] if plane < PLANES else coming.at[plane - PLANES]
        brick[plane, :16, :] = source[ROWS - 16 :, :]
        brick[plane, 16 : 16 + SHEAR, :] = high[plane]
        brick[plane, 16 + SHEAR :, :] = jnp.zeros((8, COLS), jnp.float32)

    def rows_of(slot, before, plain, beyond):
        for start, count, extinction in ((8, 8, plain), (16, SHEAR, beyond)):
            values = shade(
                coefficient,
                coefficient(extinction),
                brick[slot, start : start + count, :],
                brick[slot, start - 1 : start - 1 + count, :],
                brick[slot, start + 1 : start + 1 + count, :],
                0.0 if before is None else brick[before, start : start + count, :],
                brick[slot + 1, start : start + count, :],
            )
            store(fields, slot, ROWS - 16 + start, values)

    def plane_of(plane, _):
        rows_of(plane, plane - 1, PLAIN, BEYOND)
        return 0

    lax.fori_loop(1, PLANES, plane_of, 0)
    rows_of(PLANES, PLANES - 1, NEXT, NEXT_BEYOND)

    @pl.when(lax.axis_index("depth") == 0)
    def _():
        rows_of(0, None, PLAIN, BEYOND)

    copy.wait()
    render(masks, starts, fields, given, kept, 1, ROWS // 8)


def first_kernel(table, masks, starts_in, own, coming, low, held, *refs):
    del held
    given, kept, fields, starts, semaphore = refs[2:]
    copy = pltpu.make_async_copy(starts_in, starts, semaphore)
    copy.start()
    coefficient = lambda at: table[at : at + 1, :]
    top = lax.broadcasted_iota(jnp.int32, (8, COLS), 0) == 0

    def first_rows(slot):
        plane_at = lambda plane: own.at[plane] if plane < PLANES else coming.at[plane - PLANES]
        plane = plane_at(slot)
        centre = plane[:8, :]
        above = jnp.where(top, low[slot : slot + 1, :], pltpu.roll(centre, 1, 0))
        before = 0.0 if slot == 0 else plane_at(slot - 1)[:8, :]
        extinction = coefficient(NEXT if slot == PLANES else PLAIN)
        store(fields, slot, 0, shade(coefficient, extinction, centre, above, plane[1:9, :], before, plane_at(slot + 1)[:8, :]))

    for slot in range(1, SLABS):
        first_rows(slot)

    @pl.when(lax.axis_index("depth") == 0)
    def _():
        first_rows(0)

    copy.wait()
    render(masks, starts, fields, given, kept, 0, 1)


def render(masks, starts, fields, given, kept, tile, tiles):
    upper = lax.broadcasted_iota(jnp.int32, (8, COLS), 0) < SHARE
    odd = masks[CORE] > 0.5

    def of(planes):
        def tile_of(tile, _):
            for pair in range(VIEWS // 2):
                sums = []
                for view in (2 * pair, 2 * pair + 1):
                    red = green = blue = optical = jnp.zeros((8, COLS), jnp.float32)
                    for step in range(planes):
                        rows = pl.ds(starts[view * SLABS + step] + 8 * tile, 8)
                        through = jnp.exp(-optical)
                        red = red + fields[0, rows, :] * through
                        green = green + fields[1, rows, :] * through
                        blue = blue + fields[2, rows, :] * through
                        optical = optical + fields[3, rows, :]
                    sums.append((red, green, blue, optical))
                for kind in range(4):
                    first, second = sums[0][kind], sums[1][kind]
                    even_rows = jnp.where(upper, first, pltpu.roll(second, SHARE, 0))
                    odd_rows = jnp.where(upper, pltpu.roll(first, SHARE, 0), second)
                    kept[tile, kind, pair] = jnp.where(odd, odd_rows, even_rows)
                    given[tile, kind, pair] = jnp.where(odd, even_rows, odd_rows)
            return 0

        lax.fori_loop(tile, tiles, tile_of, 0)

    leading = starts[FIRST] == 0

    @pl.when(leading)
    def _():
        of(SLABS)

    @pl.when(jnp.logical_not(leading))
    def _():
        of(PLANES)


def place_of(core, chip):
    return jnp.where(core == 1, ORDERS[1].index(chip), ORDERS[0].index(chip))


def merge_kernel(masks, kept, gathered, out):
    odd = masks[CORE] > 0.5
    core = lax.axis_index("depth") % 2
    for pair in range(VIEWS // 2):
        mine_front = masks[FRONT + pair] > 0.5

        for chip in range(CHIPS):
            place = place_of(core, chip)
            mine = [kept[chip, kind, pair] for kind in range(4)]
            other = [jnp.where(odd, gathered[0, chip, kind, pair], gathered[1, chip, kind, pair]) for kind in range(4)]
            through = jnp.exp(-jnp.where(mine_front, mine[3], other[3]))
            for kind in range(3):
                front = jnp.where(mine_front, mine[kind], other[kind])
                behind = jnp.where(mine_front, other[kind], mine[kind])
                out[place, kind, pair] = front + through * behind
            out[place, 3, pair] = mine[3] + other[3]


def final_kernel(masks, slabs, out):
    places = [place_of(lax.axis_index("depth") % 2, chip) for chip in range(CHIPS)]
    for pair in range(VIEWS // 2):
        backward = masks[BACK + pair] > 0.5
        optical = [slabs[place, 3, pair] for place in places]
        ahead, behind = [jnp.zeros((8, COLS), jnp.float32)], [jnp.zeros((8, COLS), jnp.float32)]
        for chip in range(CHIPS - 1):
            ahead.append(ahead[-1] + optical[chip])
            behind.append(behind[-1] + optical[CHIPS - 1 - chip])
        total = ahead[-1] + optical[-1]
        sums = [jnp.zeros((8, COLS), jnp.float32)] * 3
        for chip in range(CHIPS):
            through = jnp.exp(-jnp.where(backward, behind[CHIPS - 1 - chip], ahead[chip]))
            sums = [sums[kind] + slabs[places[chip], kind, pair] * through for kind in range(3)]
        cover = jnp.where(total < 0.0625, opacity_of(total), 1.0 - jnp.exp(-total))
        for kind, value in enumerate((*sums, cover)):
            out[kind, 2 * pair] = value[:SHARE]
            out[kind, 2 * pair + 1] = value[SHARE:]


def kernel(body, name, out_shape, in_specs, out_specs, flops=0, **more):
    estimate = pl.CostEstimate(flops=flops, bytes_accessed=2**20, transcendentals=0)
    return pl.pallas_call(
        body,
        out_shape=out_shape,
        in_specs=in_specs,
        out_specs=out_specs,
        compiler_params=PARAMS,
        cost_estimate=estimate,
        name=name,
        **more,
    )


def on_device(density, light_vector, colour_gain, colour_bias, shear_step, reverse_view):
    heights, depths = lax.axis_size("height"), lax.axis_size("depth")

    own, first = kernel(
        load_kernel,
        "load",
        (array(PLANES, ROWS, COLS), array(2, ROWS, COLS)),
        [HBM],
        (VMEM,) * 2,
        flops=10**9,
        scratch_shapes=[pltpu.SemaphoreType.DMA],
    )(density)
    cores = [[2 * chip, 2 * chip + 1] for chip in range(CHIPS)]
    coming = lax.ppermute(first, "depth", [(i + 1, i) for i in range(depths - 1)])
    own_high, own_low = kernel(
        cut_kernel, "cut", (array(PLANES + 2, SHEAR, COLS), array(PLANES + 8, COLS)), [VMEM] * 2, (VMEM,) * 2
    )(own, coming)
    high = lax.ppermute(own_high, "height", [(i + 1, i) for i in range(heights - 1)])
    low = lax.ppermute(own_low, "height", [(i, i + 1) for i in range(heights - 1)])

    shaded = array(4, SLABS * TALL, COLS)
    fields, table, masks, starts = kernel(
        inner_kernel,
        "inner",
        (shaded, array(16, COLS), array(5, 8, COLS), jax.ShapeDtypeStruct((64,), jnp.int32)),
        [HBM] * 5 + [VMEM] * 3,
        (VMEM, VMEM, VMEM, SMEM),
        flops=10**7,
        scratch_shapes=[pltpu.SMEM((3,), jnp.float32)] * 3
        + [pltpu.SMEM((VIEWS,), jnp.int32)] * 2
        + [pltpu.SemaphoreType.DMA((5,))],
    )(light_vector, colour_gain, colour_bias, shear_step, reverse_view, own, coming, own_low)
    part = array(CHIPS, 4, VIEWS // 2, 8, COLS)
    memory = [pltpu.SMEM((64,), jnp.int32), pltpu.SemaphoreType.DMA]
    given, kept, fields = kernel(
        render_kernel,
        "render",
        (part, part, shaded),
        [VMEM, VMEM, ANY] + [VMEM] * 4,
        (VMEM,) * 3,
        flops=10**7,
        input_output_aliases={6: 2},
        scratch_shapes=[pltpu.VMEM((PLANES + 2, 24 + SHEAR, COLS), jnp.float32), *memory],
    )(table, masks, starts, own, coming, high, fields)
    given, kept, _ = kernel(
        first_kernel,
        "first",
        (part, part, shaded),
        [VMEM, VMEM, ANY] + [VMEM] * 6,
        (VMEM,) * 3,
        input_output_aliases={6: 2, 7: 0, 8: 1},
        scratch_shapes=memory,
    )(table, masks, starts, own, coming, low, fields, given, kept)

    gathered = lax.all_gather(given, "depth", axis=0, axis_index_groups=cores)
    merged = kernel(merge_kernel, "merge", part, [VMEM] * 3, VMEM)(masks, kept, gathered)
    groups = [[2 * chip + core for chip in ORDERS[core]] for core in range(2)]
    slabs = lax.all_to_all(merged, "depth", 0, 0, tiled=True, axis_index_groups=groups)
    return kernel(final_kernel, "composite", array(4, VIEWS, SHARE, COLS), [VMEM] * 2, VMEM)(masks, slabs)


def solution(mesh):
    placed = (P("depth", "height", None), P(), P(), P(), P(), P())
    return jax.shard_map(
        on_device,
        mesh=mesh,
        in_specs=placed,
        out_specs=P(None, None, ("height", "depth"), None),
        check_vma=False,
    )
```

```python
import jax
import jax.numpy as jnp
from jax import lax
from jax.experimental import pallas as pl
from jax.experimental.pallas import tpu as pltpu
from jax.sharding import PartitionSpec as P

EXTINCTION = 2.5
SMEM = pl.BlockSpec(memory_space=pltpu.SMEM)
VMEM = pl.BlockSpec(memory_space=pltpu.VMEM)
ANY = pl.BlockSpec(memory_space=pl.ANY)
HBM = pl.BlockSpec(memory_space=pltpu.HBM)
PLANES, ROWS, COLS, SHEAR, VIEWS, GROUPS, BRICKS = 8, 64, 128, 32, 4, 16, 32
TALL = ROWS + SHEAR
SLABS = PLANES + 1
CHIPS = GROUPS // 2
SHARE = ROWS // GROUPS
ORDERS = ((7, 6, 5, 4, 3, 2, 1, 0), (7, 6, 5, 4, 3, 2, 1, 0))
PARAMS = pltpu.CompilerParams(vmem_limit_bytes=8 * 2**20)
LIGHT, GAIN, BIAS, PLAIN, BEYOND, NEXT, NEXT_BEYOND = 0, 3, 6, 9, 10, 11, 12
FRONT, BACK, CORE = 0, 2, 4
INNER = slice(8, ROWS - 8)
FIRST = VIEWS * SLABS


def array(*shape):
    return jax.ShapeDtypeStruct(shape, jnp.float32)


def opacity_of(optical):
    series = 1.0 - optical * (1.0 / 6.0)
    for term in (5.0, 4.0, 3.0, 2.0):
        series = 1.0 - optical * (1.0 / term) * series
    return optical * series


def shade(coefficient, extinction, centre, above, below, before, after):
    lane = lax.broadcasted_iota(jnp.int32, centre.shape, 1)
    tilt_rows = 0.5 * (below - above)
    tilt_depth = 0.5 * (after - before)
    right = jnp.where(lane == COLS - 1, 0.0, pltpu.roll(centre, COLS - 1, 1))
    left = jnp.where(lane == 0, 0.0, pltpu.roll(centre, 1, 1))
    tilt_cols = 0.5 * (right - left)
    slope = coefficient(LIGHT) * tilt_depth + coefficient(LIGHT + 1) * tilt_rows + coefficient(LIGHT + 2) * tilt_cols
    facing = slope * lax.rsqrt(1.0 + tilt_depth * tilt_depth + tilt_rows * tilt_rows + tilt_cols * tilt_cols)
    shading = 0.25 + 1.5 * jnp.maximum(facing, 0.0)
    optical = extinction * (jnp.maximum(centre, 0.0) + jnp.log1p(jnp.exp(-jnp.abs(centre))))
    strength = opacity_of(optical) * shading
    tones = [jax.nn.sigmoid(coefficient(GAIN + i) * centre + coefficient(BIAS + i)) for i in range(3)]
    return [strength * tone for tone in tones] + [optical]


def load_kernel(density, own, first, semaphore):
    copy = pltpu.make_async_copy(density, own, semaphore)
    copy.start()
    copy.wait()
    first[...] = own[:2]


def inner_kernel(*refs):
    arguments, (own, coming, _, fields, table, masks, starts, heads), scalars, semaphores = refs[:5], refs[5:13], refs[13:18], refs[18]
    copies = [pltpu.make_async_copy(arguments[i], scalars[i], semaphores.at[i]) for i in range(5)]
    for copy in copies:
        copy.start()
    depth, height = lax.axis_index("depth"), lax.axis_index("height")
    for copy in copies:
        copy.wait()
    light, gain, bias, shear, reverse = scalars
    extinction = EXTINCTION / (PLANES * GROUPS)
    beyond = jnp.where(height == BRICKS - 1, 0.0, extinction)
    following = jnp.where(depth == GROUPS - 1, 0.0, extinction)
    both = jnp.where(depth == GROUPS - 1, 0.0, beyond)
    values_of = [ref[i] for ref in (light, gain, bias) for i in range(3)] + [extinction, beyond, following, both]
    for row, scalar in enumerate(values_of):
        table[row : row + 1, :] = jnp.full((1, COLS), scalar, jnp.float32)
    upper = lax.broadcasted_iota(jnp.int32, (8, COLS), 0) < SHARE
    core = depth % 2
    for base, digit in ((FRONT, core), (BACK, 1)):
        for pair in range(VIEWS // 2):
            first = jnp.where(reverse[2 * pair] == digit, 1.0, 0.0)
            second = jnp.where(reverse[2 * pair + 1] == digit, 1.0, 0.0)
            masks[base + pair] = jnp.where(upper, first, second)
    masks[CORE] = jnp.full((8, COLS), core, jnp.float32)
    first = jnp.where(depth == 0, 0, 1)
    starts[FIRST] = first
    for view in range(VIEWS):
        for step in range(SLABS):
            slot = jnp.where(reverse[view] == 1, SLABS - 1 - step, jnp.minimum(first + step, SLABS - 1))
            offset = lax.shift_right_logical((depth * PLANES + slot) * shear[view], 7)
            starts[view * SLABS + step] = slot * TALL + jnp.minimum(offset, SHEAR)

    coefficient = lambda at: values_of[at]

    def plane_of(plane, _):
        shade_inner(coefficient, extinction, own.at[plane], own[plane - 1, INNER, :], own[plane + 1, INNER, :], fields, plane)
        return 0

    lax.fori_loop(1, PLANES - 1, plane_of, 0)
    last = own.at[PLANES - 1]
    shade_inner(coefficient, extinction, last, own[PLANES - 2, INNER, :], coming[0, INNER, :], fields, PLANES - 1)
    shade_inner(coefficient, following, coming.at[0], last[INNER, :], coming[1, INNER, :], fields, PLANES)

    plane_at = lambda plane: own.at[plane] if plane < PLANES else coming.at[plane - PLANES]
    for plane in range(PLANES + 2):
        for row in range(2):
            heads[row, plane : plane + 1, :] = plane_at(plane)[row : row + 1, :]
    for slot in range(1, SLABS):
        first_tile(coefficient, following if slot == PLANES else extinction, plane_at, fields, slot)

    @pl.when(depth == 0)
    def _():
        first_tile(coefficient, extinction, plane_at, fields, 0)
        shade_inner(coefficient, extinction, own.at[0], 0.0, own[1, INNER, :], fields, 0)


def shade_inner(coefficient, extinction, plane, before, after, fields, slot):
    centre = plane[INNER, :]
    values = shade(coefficient, extinction, centre, plane[7 : ROWS - 9, :], plane[9 : ROWS - 7, :], before, after)
    store(fields, slot, 8, values)


def first_tile(coefficient, extinction, plane_at, fields, slot):
    plane = plane_at(slot)
    centre = plane[:8, :]
    before = 0.0 if slot == 0 else plane_at(slot - 1)[:8, :]
    after = plane_at(slot + 1)[:8, :]
    store(fields, slot, 0, shade(coefficient, extinction, centre, pltpu.roll(centre, 1, 0), plane[1:9, :], before, after))


def store(fields, slot, row, values):
    rows = pl.ds(pl.multiple_of(slot * TALL + row, 8), values[0].shape[0])
    for kind in range(4):
        fields[kind, rows, :] = values[kind]


def cut_kernel(own, coming, high, low):
    high[:PLANES] = own[:, :SHEAR, :]
    high[PLANES:] = coming[:, :SHEAR, :]
    for plane in range(PLANES):
        low[plane : plane + 1, :] = own[plane, ROWS - 1 : ROWS, :]
    low[PLANES:, :] = jnp.broadcast_to(coming[0, ROWS - 1 : ROWS, :], (8, COLS))


def render_kernel(
    table, masks, starts_in, own, coming, high, held, given, kept, fields, brick, starts, semaphore
):
    del held
    copy = pltpu.make_async_copy(starts_in, starts, semaphore)
    copy.start()
    coefficient = lambda at: table[at : at + 1, :]
    for plane in range(PLANES + 2):
        source = own.at[plane] if plane < PLANES else coming.at[plane - PLANES]
        brick[plane, :16, :] = source[ROWS - 16 :, :]
        brick[plane, 16 : 16 + SHEAR, :] = high[plane]
        brick[plane, 16 + SHEAR :, :] = jnp.zeros((8, COLS), jnp.float32)

    def rows_of(slot, before, plain, beyond):
        for start, count, extinction in ((8, 8, plain), (16, SHEAR, beyond)):
            values = shade(
                coefficient,
                coefficient(extinction),
                brick[slot, start : start + count, :],
                brick[slot, start - 1 : start - 1 + count, :],
                brick[slot, start + 1 : start + 1 + count, :],
                0.0 if before is None else brick[before, start : start + count, :],
                brick[slot + 1, start : start + count, :],
            )
            store(fields, slot, ROWS - 16 + start, values)

    def plane_of(plane, _):
        rows_of(plane, plane - 1, PLAIN, BEYOND)
        return 0

    lax.fori_loop(1, PLANES, plane_of, 0)
    rows_of(PLANES, PLANES - 1, NEXT, NEXT_BEYOND)

    @pl.when(lax.axis_index("depth") == 0)
    def _():
        rows_of(0, None, PLAIN, BEYOND)

    copy.wait()
    render(masks, starts, fields, given, kept, 1, ROWS // 8)


def first_kernel(table, masks, starts_in, heads, low, held, *refs):
    del held
    given, kept, fields, starts, semaphore = refs[2:]
    copy = pltpu.make_async_copy(starts_in, starts, semaphore)
    copy.start()
    coefficient = lambda at: table[at : at + 1, :]
    last = lax.broadcasted_iota(jnp.int32, (8, COLS), 0) == PLANES - 1
    extinction = jnp.where(last, coefficient(NEXT), coefficient(PLAIN))
    centre, before, after = heads[0, 1:9, :], heads[0, 0:8, :], heads[0, 2:10, :]
    values = shade(coefficient, extinction, centre, low[1:9, :], heads[1, 1:9, :], before, after)
    for slot in range(1, SLABS):
        for kind in range(4):
            fields[kind, slot * TALL : slot * TALL + 1, :] = values[kind][slot - 1 : slot, :]

    @pl.when(lax.axis_index("depth") == 0)
    def _():
        first = shade(coefficient, coefficient(PLAIN), heads[0, 0:8, :], low[0:8, :], heads[1, 0:8, :], 0.0, centre)
        for kind in range(4):
            fields[kind, 0:1, :] = first[kind][0:1, :]

    copy.wait()
    render(masks, starts, fields, given, kept, 0, 1)


def render(masks, starts, fields, given, kept, tile, tiles):
    upper = lax.broadcasted_iota(jnp.int32, (8, COLS), 0) < SHARE
    odd = masks[CORE] > 0.5

    def of(planes):
        def tile_of(tile, _):
            for pair in range(VIEWS // 2):
                sums = []
                for view in (2 * pair, 2 * pair + 1):
                    red = green = blue = optical = jnp.zeros((8, COLS), jnp.float32)
                    for step in range(planes):
                        rows = pl.ds(starts[view * SLABS + step] + 8 * tile, 8)
                        through = jnp.exp(-optical)
                        red = red + fields[0, rows, :] * through
                        green = green + fields[1, rows, :] * through
                        blue = blue + fields[2, rows, :] * through
                        optical = optical + fields[3, rows, :]
                    sums.append((red, green, blue, optical))
                for kind in range(4):
                    first, second = sums[0][kind], sums[1][kind]
                    even_rows = jnp.where(upper, first, pltpu.roll(second, SHARE, 0))
                    odd_rows = jnp.where(upper, pltpu.roll(first, SHARE, 0), second)
                    kept[tile, kind, pair] = jnp.where(odd, odd_rows, even_rows)
                    given[tile, kind, pair] = jnp.where(odd, even_rows, odd_rows)
            return 0

        lax.fori_loop(tile, tiles, tile_of, 0)

    leading = starts[FIRST] == 0

    @pl.when(leading)
    def _():
        of(SLABS)

    @pl.when(jnp.logical_not(leading))
    def _():
        of(PLANES)


def place_of(core, chip):
    return jnp.where(core == 1, ORDERS[1].index(chip), ORDERS[0].index(chip))


def merge_kernel(masks, kept, gathered, out):
    odd = masks[CORE] > 0.5
    core = lax.axis_index("depth") % 2
    for pair in range(VIEWS // 2):
        mine_front = masks[FRONT + pair] > 0.5

        for chip in range(CHIPS):
            place = place_of(core, chip)
            mine = [kept[chip, kind, pair] for kind in range(4)]
            other = [jnp.where(odd, gathered[0, chip, kind, pair], gathered[1, chip, kind, pair]) for kind in range(4)]
            through = jnp.exp(-jnp.where(mine_front, mine[3], other[3]))
            for kind in range(3):
                front = jnp.where(mine_front, mine[kind], other[kind])
                behind = jnp.where(mine_front, other[kind], mine[kind])
                out[place, kind, pair] = front + through * behind
            out[place, 3, pair] = mine[3] + other[3]


def final_kernel(masks, slabs, out):
    places = [place_of(lax.axis_index("depth") % 2, chip) for chip in range(CHIPS)]
    for pair in range(VIEWS // 2):
        backward = masks[BACK + pair] > 0.5
        optical = [slabs[place, 3, pair] for place in places]
        ahead, behind = [jnp.zeros((8, COLS), jnp.float32)], [jnp.zeros((8, COLS), jnp.float32)]
        for chip in range(CHIPS - 1):
            ahead.append(ahead[-1] + optical[chip])
            behind.append(behind[-1] + optical[CHIPS - 1 - chip])
        total = ahead[-1] + optical[-1]
        sums = [jnp.zeros((8, COLS), jnp.float32)] * 3
        for chip in range(CHIPS):
            through = jnp.exp(-jnp.where(backward, behind[CHIPS - 1 - chip], ahead[chip]))
            sums = [sums[kind] + slabs[places[chip], kind, pair] * through for kind in range(3)]
        cover = jnp.where(total < 0.0625, opacity_of(total), 1.0 - jnp.exp(-total))
        for kind, value in enumerate((*sums, cover)):
            out[kind, 2 * pair] = value[:SHARE]
            out[kind, 2 * pair + 1] = value[SHARE:]


def kernel(body, name, out_shape, in_specs, out_specs, flops=0, **more):
    estimate = pl.CostEstimate(flops=flops, bytes_accessed=2**20, transcendentals=0)
    return pl.pallas_call(
        body,
        out_shape=out_shape,
        in_specs=in_specs,
        out_specs=out_specs,
        compiler_params=PARAMS,
        cost_estimate=estimate,
        name=name,
        **more,
    )


def on_device(density, light_vector, colour_gain, colour_bias, shear_step, reverse_view):
    heights, depths = lax.axis_size("height"), lax.axis_size("depth")

    own, first = kernel(
        load_kernel,
        "load",
        (array(PLANES, ROWS, COLS), array(2, ROWS, COLS)),
        [HBM],
        (VMEM,) * 2,
        flops=10**9,
        scratch_shapes=[pltpu.SemaphoreType.DMA],
    )(density)
    cores = [[2 * chip, 2 * chip + 1] for chip in range(CHIPS)]
    coming = lax.ppermute(first, "depth", [(i + 1, i) for i in range(depths - 1)])
    own_high, own_low = kernel(
        cut_kernel, "cut", (array(PLANES + 2, SHEAR, COLS), array(PLANES + 8, COLS)), [VMEM] * 2, (VMEM,) * 2
    )(own, coming)
    high = lax.ppermute(own_high, "height", [(i + 1, i) for i in range(heights - 1)])
    low = lax.ppermute(own_low, "height", [(i, i + 1) for i in range(heights - 1)])

    shaded = array(4, SLABS * TALL, COLS)
    fields, table, masks, starts, heads = kernel(
        inner_kernel,
        "inner",
        (shaded, array(16, COLS), array(5, 8, COLS), jax.ShapeDtypeStruct((64,), jnp.int32), array(2, 16, COLS)),
        [HBM] * 5 + [VMEM] * 3,
        (VMEM, VMEM, VMEM, SMEM, VMEM),
        flops=10**7,
        scratch_shapes=[pltpu.SMEM((3,), jnp.float32)] * 3
        + [pltpu.SMEM((VIEWS,), jnp.int32)] * 2
        + [pltpu.SemaphoreType.DMA((5,))],
    )(light_vector, colour_gain, colour_bias, shear_step, reverse_view, own, coming, own_low)
    part = array(CHIPS, 4, VIEWS // 2, 8, COLS)
    memory = [pltpu.SMEM((64,), jnp.int32), pltpu.SemaphoreType.DMA]
    given, kept, fields = kernel(
        render_kernel,
        "render",
        (part, part, shaded),
        [VMEM, VMEM, ANY] + [VMEM] * 4,
        (VMEM,) * 3,
        flops=10**7,
        input_output_aliases={6: 2},
        scratch_shapes=[pltpu.VMEM((PLANES + 2, 24 + SHEAR, COLS), jnp.float32), *memory],
    )(table, masks, starts, own, coming, high, fields)
    given, kept, _ = kernel(
        first_kernel,
        "first",
        (part, part, shaded),
        [VMEM, VMEM, ANY] + [VMEM] * 5,
        (VMEM,) * 3,
        input_output_aliases={5: 2, 6: 0, 7: 1},
        scratch_shapes=memory,
    )(table, masks, starts, heads, low, fields, given, kept)

    gathered = lax.all_gather(given, "depth", axis=0, axis_index_groups=cores)
    merged = kernel(merge_kernel, "merge", part, [VMEM] * 3, VMEM)(masks, kept, gathered)
    groups = [[2 * chip + core for chip in ORDERS[core]] for core in range(2)]
    slabs = lax.all_to_all(merged, "depth", 0, 0, tiled=True, axis_index_groups=groups)
    return kernel(final_kernel, "composite", array(4, VIEWS, SHARE, COLS), [VMEM] * 2, VMEM)(masks, slabs)


def solution(mesh):
    placed = (P("depth", "height", None), P(), P(), P(), P(), P())
    return jax.shard_map(
        on_device,
        mesh=mesh,
        in_specs=placed,
        out_specs=P(None, None, ("height", "depth"), None),
        check_vma=False,
    )
```

```python
import jax
import jax.numpy as jnp
from jax import lax
from jax.experimental import pallas as pl
from jax.experimental.pallas import tpu as pltpu
from jax.sharding import PartitionSpec as P

EXTINCTION = 2.5
SMEM = pl.BlockSpec(memory_space=pltpu.SMEM)
VMEM = pl.BlockSpec(memory_space=pltpu.VMEM)
ANY = pl.BlockSpec(memory_space=pl.ANY)
HBM = pl.BlockSpec(memory_space=pltpu.HBM)
PLANES, ROWS, COLS, SHEAR, VIEWS, GROUPS, BRICKS = 8, 64, 128, 32, 4, 16, 32
TALL = ROWS + SHEAR
SLABS = PLANES + 1
CHIPS = GROUPS // 2
SHARE = ROWS // GROUPS
ORDERS = ((0, 7, 6, 5, 4, 3, 2, 1), (0, 7, 6, 5, 4, 3, 2, 1))
PARAMS = pltpu.CompilerParams(vmem_limit_bytes=8 * 2**20)
LIGHT, GAIN, BIAS, PLAIN, BEYOND, NEXT, NEXT_BEYOND = 0, 3, 6, 9, 10, 11, 12
FRONT, BACK, CORE = 0, 2, 4
INNER = slice(8, ROWS - 8)
FIRST = VIEWS * SLABS


def array(*shape):
    return jax.ShapeDtypeStruct(shape, jnp.float32)


def opacity_of(optical):
    series = 1.0 - optical * (1.0 / 6.0)
    for term in (5.0, 4.0, 3.0, 2.0):
        series = 1.0 - optical * (1.0 / term) * series
    return optical * series


def shade(coefficient, extinction, centre, above, below, before, after):
    lane = lax.broadcasted_iota(jnp.int32, centre.shape, 1)
    tilt_rows = 0.5 * (below - above)
    tilt_depth = 0.5 * (after - before)
    right = jnp.where(lane == COLS - 1, 0.0, pltpu.roll(centre, COLS - 1, 1))
    left = jnp.where(lane == 0, 0.0, pltpu.roll(centre, 1, 1))
    tilt_cols = 0.5 * (right - left)
    slope = coefficient(LIGHT) * tilt_depth + coefficient(LIGHT + 1) * tilt_rows + coefficient(LIGHT + 2) * tilt_cols
    facing = slope * lax.rsqrt(1.0 + tilt_depth * tilt_depth + tilt_rows * tilt_rows + tilt_cols * tilt_cols)
    shading = 0.25 + 1.5 * jnp.maximum(facing, 0.0)
    optical = extinction * (jnp.maximum(centre, 0.0) + jnp.log1p(jnp.exp(-jnp.abs(centre))))
    strength = opacity_of(optical) * shading
    tones = [jax.nn.sigmoid(coefficient(GAIN + i) * centre + coefficient(BIAS + i)) for i in range(3)]
    return [strength * tone for tone in tones] + [optical]


def load_kernel(density, own, first, semaphore):
    copy = pltpu.make_async_copy(density, own, semaphore)
    copy.start()
    copy.wait()
    first[...] = own[:2]


def inner_kernel(*refs):
    arguments, (own, coming, _, fields, table, masks, starts), scalars, semaphores = refs[:5], refs[5:12], refs[12:17], refs[17]
    copies = [pltpu.make_async_copy(arguments[i], scalars[i], semaphores.at[i]) for i in range(5)]
    for copy in copies:
        copy.start()
    depth, height = lax.axis_index("depth"), lax.axis_index("height")
    for copy in copies:
        copy.wait()
    light, gain, bias, shear, reverse = scalars
    extinction = EXTINCTION / (PLANES * GROUPS)
    beyond = jnp.where(height == BRICKS - 1, 0.0, extinction)
    following = jnp.where(depth == GROUPS - 1, 0.0, extinction)
    both = jnp.where(depth == GROUPS - 1, 0.0, beyond)
    values_of = [ref[i] for ref in (light, gain, bias) for i in range(3)] + [extinction, beyond, following, both]
    for row, scalar in enumerate(values_of):
        table[row : row + 1, :] = jnp.full((1, COLS), scalar, jnp.float32)
    upper = lax.broadcasted_iota(jnp.int32, (8, COLS), 0) < SHARE
    core = depth % 2
    for base, digit in ((FRONT, core), (BACK, 1)):
        for pair in range(VIEWS // 2):
            first = jnp.where(reverse[2 * pair] == digit, 1.0, 0.0)
            second = jnp.where(reverse[2 * pair + 1] == digit, 1.0, 0.0)
            masks[base + pair] = jnp.where(upper, first, second)
    masks[CORE] = jnp.full((8, COLS), core, jnp.float32)
    first = jnp.where(depth == 0, 0, 1)
    starts[FIRST] = first
    for view in range(VIEWS):
        for step in range(SLABS):
            slot = jnp.where(reverse[view] == 1, SLABS - 1 - step, jnp.minimum(first + step, SLABS - 1))
            offset = lax.shift_right_logical((depth * PLANES + slot) * shear[view], 7)
            starts[view * SLABS + step] = slot * TALL + jnp.minimum(offset, SHEAR)

    coefficient = lambda at: values_of[at]

    def plane_of(plane, _):
        shade_inner(coefficient, extinction, own.at[plane], own[plane - 1, INNER, :], own[plane + 1, INNER, :], fields, plane)
        return 0

    lax.fori_loop(1, PLANES - 1, plane_of, 0)
    last = own.at[PLANES - 1]
    shade_inner(coefficient, extinction, last, own[PLANES - 2, INNER, :], coming[0, INNER, :], fields, PLANES - 1)
    shade_inner(coefficient, following, coming.at[0], last[INNER, :], coming[1, INNER, :], fields, PLANES)

    @pl.when(depth == 0)
    def _():
        shade_inner(coefficient, extinction, own.at[0], 0.0, own[1, INNER, :], fields, 0)


def shade_inner(coefficient, extinction, plane, before, after, fields, slot):
    centre = plane[INNER, :]
    values = shade(coefficient, extinction, centre, plane[7 : ROWS - 9, :], plane[9 : ROWS - 7, :], before, after)
    store(fields, slot, 8, values)


def store(fields, slot, row, values):
    rows = pl.ds(pl.multiple_of(slot * TALL + row, 8), values[0].shape[0])
    for kind in range(4):
        fields[kind, rows, :] = values[kind]


def cut_kernel(own, coming, high, low):
    high[:PLANES] = own[:, :SHEAR, :]
    high[PLANES:] = coming[:, :SHEAR, :]
    for plane in range(PLANES):
        low[plane : plane + 1, :] = own[plane, ROWS - 1 : ROWS, :]
    low[PLANES:, :] = jnp.broadcast_to(coming[0, ROWS - 1 : ROWS, :], (8, COLS))


def render_kernel(
    table, masks, starts_in, own, coming, high, held, given, kept, fields, brick, starts, semaphore
):
    del held
    copy = pltpu.make_async_copy(starts_in, starts, semaphore)
    copy.start()
    coefficient = lambda at: table[at : at + 1, :]
    for plane in range(PLANES + 2):
        source = own.at[plane] if plane < PLANES else coming.at[plane - PLANES]
        brick[plane, :16, :] = source[ROWS - 16 :, :]
        brick[plane, 16 : 16 + SHEAR, :] = high[plane]
        brick[plane, 16 + SHEAR :, :] = jnp.zeros((8, COLS), jnp.float32)

    def rows_of(slot, before, plain, beyond):
        for start, count, extinction in ((8, 8, plain), (16, SHEAR, beyond)):
            values = shade(
                coefficient,
                coefficient(extinction),
                brick[slot, start : start + count, :],
                brick[slot, start - 1 : start - 1 + count, :],
                brick[slot, start + 1 : start + 1 + count, :],
                0.0 if before is None else brick[before, start : start + count, :],
                brick[slot + 1, start : start + count, :],
            )
            store(fields, slot, ROWS - 16 + start, values)

    def plane_of(plane, _):
        rows_of(plane, plane - 1, PLAIN, BEYOND)
        return 0

    lax.fori_loop(1, PLANES, plane_of, 0)
    rows_of(PLANES, PLANES - 1, NEXT, NEXT_BEYOND)

    @pl.when(lax.axis_index("depth") == 0)
    def _():
        rows_of(0, None, PLAIN, BEYOND)

    copy.wait()
    render(masks, starts, fields, given, kept, 1, ROWS // 8)


def first_kernel(table, masks, starts_in, own, coming, low, held, *refs):
    del held
    given, kept, fields, starts, semaphore = refs[2:]
    copy = pltpu.make_async_copy(starts_in, starts, semaphore)
    copy.start()
    coefficient = lambda at: table[at : at + 1, :]
    top = lax.broadcasted_iota(jnp.int32, (8, COLS), 0) == 0

    def first_rows(slot):
        plane_at = lambda plane: own.at[plane] if plane < PLANES else coming.at[plane - PLANES]
        plane = plane_at(slot)
        centre = plane[:8, :]
        above = jnp.where(top, low[slot : slot + 1, :], pltpu.roll(centre, 1, 0))
        before = 0.0 if slot == 0 else plane_at(slot - 1)[:8, :]
        extinction = coefficient(NEXT if slot == PLANES else PLAIN)
        store(fields, slot, 0, shade(coefficient, extinction, centre, above, plane[1:9, :], before, plane_at(slot + 1)[:8, :]))

    for slot in range(1, SLABS):
        first_rows(slot)

    @pl.when(lax.axis_index("depth") == 0)
    def _():
        first_rows(0)

    copy.wait()
    render(masks, starts, fields, given, kept, 0, 1)


def render(masks, starts, fields, given, kept, tile, tiles):
    upper = lax.broadcasted_iota(jnp.int32, (8, COLS), 0) < SHARE
    odd = masks[CORE] > 0.5

    def of(planes):
        def tile_of(tile, _):
            for pair in range(VIEWS // 2):
                sums = []
                for view in (2 * pair, 2 * pair + 1):
                    red = green = blue = optical = jnp.zeros((8, COLS), jnp.float32)
                    for step in range(planes):
                        rows = pl.ds(starts[view * SLABS + step] + 8 * tile, 8)
                        through = jnp.exp(-optical)
                        red = red + fields[0, rows, :] * through
                        green = green + fields[1, rows, :] * through
                        blue = blue + fields[2, rows, :] * through
                        optical = optical + fields[3, rows, :]
                    sums.append((red, green, blue, optical))
                for kind in range(4):
                    first, second = sums[0][kind], sums[1][kind]
                    even_rows = jnp.where(upper, first, pltpu.roll(second, SHARE, 0))
                    odd_rows = jnp.where(upper, pltpu.roll(first, SHARE, 0), second)
                    kept[tile, kind, pair] = jnp.where(odd, odd_rows, even_rows)
                    given[tile, kind, pair] = jnp.where(odd, even_rows, odd_rows)
            return 0

        lax.fori_loop(tile, tiles, tile_of, 0)

    leading = starts[FIRST] == 0

    @pl.when(leading)
    def _():
        of(SLABS)

    @pl.when(jnp.logical_not(leading))
    def _():
        of(PLANES)


def place_of(core, chip):
    return jnp.where(core == 1, ORDERS[1].index(chip), ORDERS[0].index(chip))


def merge_kernel(masks, kept, gathered, out):
    odd = masks[CORE] > 0.5
    core = lax.axis_index("depth") % 2
    for pair in range(VIEWS // 2):
        mine_front = masks[FRONT + pair] > 0.5

        for chip in range(CHIPS):
            place = place_of(core, chip)
            mine = [kept[chip, kind, pair] for kind in range(4)]
            other = [jnp.where(odd, gathered[0, chip, kind, pair], gathered[1, chip, kind, pair]) for kind in range(4)]
            through = jnp.exp(-jnp.where(mine_front, mine[3], other[3]))
            for kind in range(3):
                front = jnp.where(mine_front, mine[kind], other[kind])
                behind = jnp.where(mine_front, other[kind], mine[kind])
                out[place, kind, pair] = front + through * behind
            out[place, 3, pair] = mine[3] + other[3]


def final_kernel(masks, slabs, out):
    places = [place_of(lax.axis_index("depth") % 2, chip) for chip in range(CHIPS)]
    for pair in range(VIEWS // 2):
        backward = masks[BACK + pair] > 0.5
        optical = [slabs[place, 3, pair] for place in places]
        ahead, behind = [jnp.zeros((8, COLS), jnp.float32)], [jnp.zeros((8, COLS), jnp.float32)]
        for chip in range(CHIPS - 1):
            ahead.append(ahead[-1] + optical[chip])
            behind.append(behind[-1] + optical[CHIPS - 1 - chip])
        total = ahead[-1] + optical[-1]
        sums = [jnp.zeros((8, COLS), jnp.float32)] * 3
        for chip in range(CHIPS):
            through = jnp.exp(-jnp.where(backward, behind[CHIPS - 1 - chip], ahead[chip]))
            sums = [sums[kind] + slabs[places[chip], kind, pair] * through for kind in range(3)]
        cover = jnp.where(total < 0.0625, opacity_of(total), 1.0 - jnp.exp(-total))
        for kind, value in enumerate((*sums, cover)):
            out[kind, 2 * pair] = value[:SHARE]
            out[kind, 2 * pair + 1] = value[SHARE:]


def kernel(body, name, out_shape, in_specs, out_specs, flops=0, **more):
    estimate = pl.CostEstimate(flops=flops, bytes_accessed=2**20, transcendentals=0)
    return pl.pallas_call(
        body,
        out_shape=out_shape,
        in_specs=in_specs,
        out_specs=out_specs,
        compiler_params=PARAMS,
        cost_estimate=estimate,
        name=name,
        **more,
    )


def on_device(density, light_vector, colour_gain, colour_bias, shear_step, reverse_view):
    heights, depths = lax.axis_size("height"), lax.axis_size("depth")

    own, first = kernel(
        load_kernel,
        "load",
        (array(PLANES, ROWS, COLS), array(2, ROWS, COLS)),
        [HBM],
        (VMEM,) * 2,
        flops=10**9,
        scratch_shapes=[pltpu.SemaphoreType.DMA],
    )(density)
    cores = [[2 * chip, 2 * chip + 1] for chip in range(CHIPS)]
    coming = lax.ppermute(first, "depth", [(i + 1, i) for i in range(depths - 1)])
    own_high, own_low = kernel(
        cut_kernel, "cut", (array(PLANES + 2, SHEAR, COLS), array(PLANES + 8, COLS)), [VMEM] * 2, (VMEM,) * 2
    )(own, coming)
    high = lax.ppermute(own_high, "height", [(i + 1, i) for i in range(heights - 1)])
    low = lax.ppermute(own_low, "height", [(i, i + 1) for i in range(heights - 1)])

    shaded = array(4, SLABS * TALL, COLS)
    fields, table, masks, starts = kernel(
        inner_kernel,
        "inner",
        (shaded, array(16, COLS), array(5, 8, COLS), jax.ShapeDtypeStruct((64,), jnp.int32)),
        [HBM] * 5 + [VMEM] * 3,
        (VMEM, VMEM, VMEM, SMEM),
        flops=10**7,
        scratch_shapes=[pltpu.SMEM((3,), jnp.float32)] * 3
        + [pltpu.SMEM((VIEWS,), jnp.int32)] * 2
        + [pltpu.SemaphoreType.DMA((5,))],
    )(light_vector, colour_gain, colour_bias, shear_step, reverse_view, own, coming, own_low)
    part = array(CHIPS, 4, VIEWS // 2, 8, COLS)
    memory = [pltpu.SMEM((64,), jnp.int32), pltpu.SemaphoreType.DMA]
    given, kept, fields = kernel(
        render_kernel,
        "render",
        (part, part, shaded),
        [VMEM, VMEM, ANY] + [VMEM] * 4,
        (VMEM,) * 3,
        flops=10**7,
        input_output_aliases={6: 2},
        scratch_shapes=[pltpu.VMEM((PLANES + 2, 24 + SHEAR, COLS), jnp.float32), *memory],
    )(table, masks, starts, own, coming, high, fields)
    given, kept, _ = kernel(
        first_kernel,
        "first",
        (part, part, shaded),
        [VMEM, VMEM, ANY] + [VMEM] * 6,
        (VMEM,) * 3,
        input_output_aliases={6: 2, 7: 0, 8: 1},
        scratch_shapes=memory,
    )(table, masks, starts, own, coming, low, fields, given, kept)

    gathered = lax.all_gather(given, "depth", axis=0, axis_index_groups=cores)
    merged = kernel(merge_kernel, "merge", part, [VMEM] * 3, VMEM)(masks, kept, gathered)
    groups = [[2 * chip + core for chip in ORDERS[core]] for core in range(2)]
    slabs = lax.all_to_all(merged, "depth", 0, 0, tiled=True, axis_index_groups=groups)
    return kernel(final_kernel, "composite", array(4, VIEWS, SHARE, COLS), [VMEM] * 2, VMEM)(masks, slabs)


def solution(mesh):
    placed = (P("depth", "height", None), P(), P(), P(), P(), P())
    return jax.shard_map(
        on_device,
        mesh=mesh,
        in_specs=placed,
        out_specs=P(None, None, ("height", "depth"), None),
        check_vma=False,
    )
```

```python
import jax
import jax.numpy as jnp
from jax import lax
from jax.experimental import pallas as pl
from jax.experimental.pallas import tpu as pltpu
from jax.sharding import PartitionSpec as P

EXTINCTION = 2.5
SMEM = pl.BlockSpec(memory_space=pltpu.SMEM)
VMEM = pl.BlockSpec(memory_space=pltpu.VMEM)
ANY = pl.BlockSpec(memory_space=pl.ANY)
HBM = pl.BlockSpec(memory_space=pltpu.HBM)
PLANES, ROWS, COLS, SHEAR, VIEWS, GROUPS, BRICKS = 8, 64, 128, 32, 4, 16, 32
TALL = ROWS + SHEAR
SLABS = PLANES + 1
CHIPS = GROUPS // 2
SHARE = ROWS // GROUPS
ORDERS = ((7, 6, 5, 4, 3, 2, 1, 0), (7, 6, 5, 4, 3, 2, 0, 1))
PARAMS = pltpu.CompilerParams(vmem_limit_bytes=8 * 2**20)
LIGHT, GAIN, BIAS, PLAIN, BEYOND, NEXT, NEXT_BEYOND = 0, 3, 6, 9, 10, 11, 12
FRONT, BACK, CORE = 0, 2, 4
INNER = slice(8, ROWS - 8)
FIRST = VIEWS * SLABS


def array(*shape):
    return jax.ShapeDtypeStruct(shape, jnp.float32)


def opacity_of(optical):
    series = 1.0 - optical * (1.0 / 6.0)
    for term in (5.0, 4.0, 3.0, 2.0):
        series = 1.0 - optical * (1.0 / term) * series
    return optical * series


def shade(coefficient, extinction, centre, above, below, before, after):
    lane = lax.broadcasted_iota(jnp.int32, centre.shape, 1)
    tilt_rows = 0.5 * (below - above)
    tilt_depth = 0.5 * (after - before)
    right = jnp.where(lane == COLS - 1, 0.0, pltpu.roll(centre, COLS - 1, 1))
    left = jnp.where(lane == 0, 0.0, pltpu.roll(centre, 1, 1))
    tilt_cols = 0.5 * (right - left)
    slope = coefficient(LIGHT) * tilt_depth + coefficient(LIGHT + 1) * tilt_rows + coefficient(LIGHT + 2) * tilt_cols
    facing = slope * lax.rsqrt(1.0 + tilt_depth * tilt_depth + tilt_rows * tilt_rows + tilt_cols * tilt_cols)
    shading = 0.25 + 1.5 * jnp.maximum(facing, 0.0)
    optical = extinction * (jnp.maximum(centre, 0.0) + jnp.log1p(jnp.exp(-jnp.abs(centre))))
    strength = opacity_of(optical) * shading
    tones = [jax.nn.sigmoid(coefficient(GAIN + i) * centre + coefficient(BIAS + i)) for i in range(3)]
    return [strength * tone for tone in tones] + [optical]


def load_kernel(density, own, first, semaphore):
    copy = pltpu.make_async_copy(density, own, semaphore)
    copy.start()
    copy.wait()
    first[...] = own[:2]


def inner_kernel(*refs):
    arguments, (own, coming, _, fields, table, masks, starts), scalars, semaphores = refs[:5], refs[5:12], refs[12:17], refs[17]
    copies = [pltpu.make_async_copy(arguments[i], scalars[i], semaphores.at[i]) for i in range(5)]
    for copy in copies:
        copy.start()
    depth, height = lax.axis_index("depth"), lax.axis_index("height")
    for copy in copies:
        copy.wait()
    light, gain, bias, shear, reverse = scalars
    extinction = EXTINCTION / (PLANES * GROUPS)
    beyond = jnp.where(height == BRICKS - 1, 0.0, extinction)
    following = jnp.where(depth == GROUPS - 1, 0.0, extinction)
    both = jnp.where(depth == GROUPS - 1, 0.0, beyond)
    values_of = [ref[i] for ref in (light, gain, bias) for i in range(3)] + [extinction, beyond, following, both]
    for row, scalar in enumerate(values_of):
        table[row : row + 1, :] = jnp.full((1, COLS), scalar, jnp.float32)
    upper = lax.broadcasted_iota(jnp.int32, (8, COLS), 0) < SHARE
    core = depth % 2
    for base, digit in ((FRONT, core), (BACK, 1)):
        for pair in range(VIEWS // 2):
            first = jnp.where(reverse[2 * pair] == digit, 1.0, 0.0)
            second = jnp.where(reverse[2 * pair + 1] == digit, 1.0, 0.0)
            masks[base + pair] = jnp.where(upper, first, second)
    masks[CORE] = jnp.full((8, COLS), core, jnp.float32)
    first = jnp.where(depth == 0, 0, 1)
    starts[FIRST] = first
    for view in range(VIEWS):
        for step in range(SLABS):
            slot = jnp.where(reverse[view] == 1, SLABS - 1 - step, jnp.minimum(first + step, SLABS - 1))
            offset = lax.shift_right_logical((depth * PLANES + slot) * shear[view], 7)
            starts[view * SLABS + step] = slot * TALL + jnp.minimum(offset, SHEAR)

    coefficient = lambda at: values_of[at]

    def plane_of(plane, _):
        shade_inner(coefficient, extinction, own.at[plane], own[plane - 1, INNER, :], own[plane + 1, INNER, :], fields, plane)
        return 0

    lax.fori_loop(1, PLANES - 1, plane_of, 0)
    last = own.at[PLANES - 1]
    shade_inner(coefficient, extinction, last, own[PLANES - 2, INNER, :], coming[0, INNER, :], fields, PLANES - 1)
    shade_inner(coefficient, following, coming.at[0], last[INNER, :], coming[1, INNER, :], fields, PLANES)

    @pl.when(depth == 0)
    def _():
        shade_inner(coefficient, extinction, own.at[0], 0.0, own[1, INNER, :], fields, 0)


def shade_inner(coefficient, extinction, plane, before, after, fields, slot):
    centre = plane[INNER, :]
    values = shade(coefficient, extinction, centre, plane[7 : ROWS - 9, :], plane[9 : ROWS - 7, :], before, after)
    store(fields, slot, 8, values)


def store(fields, slot, row, values):
    rows = pl.ds(pl.multiple_of(slot * TALL + row, 8), values[0].shape[0])
    for kind in range(4):
        fields[kind, rows, :] = values[kind]


def cut_kernel(own, coming, high, low):
    high[:PLANES] = own[:, :SHEAR, :]
    high[PLANES:] = coming[:, :SHEAR, :]
    for plane in range(PLANES):
        low[plane : plane + 1, :] = own[plane, ROWS - 1 : ROWS, :]
    low[PLANES:, :] = jnp.broadcast_to(coming[0, ROWS - 1 : ROWS, :], (8, COLS))


def render_kernel(
    table, masks, starts_in, own, coming, high, held, given, kept, fields, brick, starts, semaphore
):
    del held
    copy = pltpu.make_async_copy(starts_in, starts, semaphore)
    copy.start()
    coefficient = lambda at: table[at : at + 1, :]
    for plane in range(PLANES + 2):
        source = own.at[plane] if plane < PLANES else coming.at[plane - PLANES]
        brick[plane, :16, :] = source[ROWS - 16 :, :]
        brick[plane, 16 : 16 + SHEAR, :] = high[plane]
        brick[plane, 16 + SHEAR :, :] = jnp.zeros((8, COLS), jnp.float32)

    def rows_of(slot, before, plain, beyond):
        for start, count, extinction in ((8, 8, plain), (16, SHEAR, beyond)):
            values = shade(
                coefficient,
                coefficient(extinction),
                brick[slot, start : start + count, :],
                brick[slot, start - 1 : start - 1 + count, :],
                brick[slot, start + 1 : start + 1 + count, :],
                0.0 if before is None else brick[before, start : start + count, :],
                brick[slot + 1, start : start + count, :],
            )
            store(fields, slot, ROWS - 16 + start, values)

    def plane_of(plane, _):
        rows_of(plane, plane - 1, PLAIN, BEYOND)
        return 0

    lax.fori_loop(1, PLANES, plane_of, 0)
    rows_of(PLANES, PLANES - 1, NEXT, NEXT_BEYOND)

    @pl.when(lax.axis_index("depth") == 0)
    def _():
        rows_of(0, None, PLAIN, BEYOND)

    copy.wait()
    render(masks, starts, fields, given, kept, 1, ROWS // 8)


def first_kernel(table, masks, starts_in, own, coming, low, held, *refs):
    del held
    given, kept, fields, starts, semaphore = refs[2:]
    copy = pltpu.make_async_copy(starts_in, starts, semaphore)
    copy.start()
    coefficient = lambda at: table[at : at + 1, :]
    top = lax.broadcasted_iota(jnp.int32, (8, COLS), 0) == 0

    def first_rows(slot):
        plane_at = lambda plane: own.at[plane] if plane < PLANES else coming.at[plane - PLANES]
        plane = plane_at(slot)
        centre = plane[:8, :]
        above = jnp.where(top, low[slot : slot + 1, :], pltpu.roll(centre, 1, 0))
        before = 0.0 if slot == 0 else plane_at(slot - 1)[:8, :]
        extinction = coefficient(NEXT if slot == PLANES else PLAIN)
        store(fields, slot, 0, shade(coefficient, extinction, centre, above, plane[1:9, :], before, plane_at(slot + 1)[:8, :]))

    for slot in range(1, SLABS):
        first_rows(slot)

    @pl.when(lax.axis_index("depth") == 0)
    def _():
        first_rows(0)

    copy.wait()
    render(masks, starts, fields, given, kept, 0, 1)


def render(masks, starts, fields, given, kept, tile, tiles):
    upper = lax.broadcasted_iota(jnp.int32, (8, COLS), 0) < SHARE
    odd = masks[CORE] > 0.5

    def of(planes):
        def tile_of(tile, _):
            for pair in range(VIEWS // 2):
                sums = []
                for view in (2 * pair, 2 * pair + 1):
                    red = green = blue = optical = jnp.zeros((8, COLS), jnp.float32)
                    for step in range(planes):
                        rows = pl.ds(starts[view * SLABS + step] + 8 * tile, 8)
                        through = jnp.exp(-optical)
                        red = red + fields[0, rows, :] * through
                        green = green + fields[1, rows, :] * through
                        blue = blue + fields[2, rows, :] * through
                        optical = optical + fields[3, rows, :]
                    sums.append((red, green, blue, optical))
                for kind in range(4):
                    first, second = sums[0][kind], sums[1][kind]
                    even_rows = jnp.where(upper, first, pltpu.roll(second, SHARE, 0))
                    odd_rows = jnp.where(upper, pltpu.roll(first, SHARE, 0), second)
                    kept[tile, kind, pair] = jnp.where(odd, odd_rows, even_rows)
                    given[tile, kind, pair] = jnp.where(odd, even_rows, odd_rows)
            return 0

        lax.fori_loop(tile, tiles, tile_of, 0)

    leading = starts[FIRST] == 0

    @pl.when(leading)
    def _():
        of(SLABS)

    @pl.when(jnp.logical_not(leading))
    def _():
        of(PLANES)


def place_of(core, chip):
    return jnp.where(core == 1, ORDERS[1].index(chip), ORDERS[0].index(chip))


def merge_kernel(masks, kept, gathered, out):
    odd = masks[CORE] > 0.5
    core = lax.axis_index("depth") % 2
    for pair in range(VIEWS // 2):
        mine_front = masks[FRONT + pair] > 0.5

        for chip in range(CHIPS):
            place = place_of(core, chip)
            mine = [kept[chip, kind, pair] for kind in range(4)]
            other = [jnp.where(odd, gathered[0, chip, kind, pair], gathered[1, chip, kind, pair]) for kind in range(4)]
            through = jnp.exp(-jnp.where(mine_front, mine[3], other[3]))
            for kind in range(3):
                front = jnp.where(mine_front, mine[kind], other[kind])
                behind = jnp.where(mine_front, other[kind], mine[kind])
                out[place, kind, pair] = front + through * behind
            out[place, 3, pair] = mine[3] + other[3]


def final_kernel(masks, slabs, out):
    places = [place_of(lax.axis_index("depth") % 2, chip) for chip in range(CHIPS)]
    for pair in range(VIEWS // 2):
        backward = masks[BACK + pair] > 0.5
        optical = [slabs[place, 3, pair] for place in places]
        ahead, behind = [jnp.zeros((8, COLS), jnp.float32)], [jnp.zeros((8, COLS), jnp.float32)]
        for chip in range(CHIPS - 1):
            ahead.append(ahead[-1] + optical[chip])
            behind.append(behind[-1] + optical[CHIPS - 1 - chip])
        total = ahead[-1] + optical[-1]
        sums = [jnp.zeros((8, COLS), jnp.float32)] * 3
        for chip in range(CHIPS):
            through = jnp.exp(-jnp.where(backward, behind[CHIPS - 1 - chip], ahead[chip]))
            sums = [sums[kind] + slabs[places[chip], kind, pair] * through for kind in range(3)]
        cover = jnp.where(total < 0.0625, opacity_of(total), 1.0 - jnp.exp(-total))
        for kind, value in enumerate((*sums, cover)):
            out[kind, 2 * pair] = value[:SHARE]
            out[kind, 2 * pair + 1] = value[SHARE:]


def kernel(body, name, out_shape, in_specs, out_specs, flops=0, **more):
    estimate = pl.CostEstimate(flops=flops, bytes_accessed=2**20, transcendentals=0)
    return pl.pallas_call(
        body,
        out_shape=out_shape,
        in_specs=in_specs,
        out_specs=out_specs,
        compiler_params=PARAMS,
        cost_estimate=estimate,
        name=name,
        **more,
    )


def on_device(density, light_vector, colour_gain, colour_bias, shear_step, reverse_view):
    heights, depths = lax.axis_size("height"), lax.axis_size("depth")

    own, first = kernel(
        load_kernel,
        "load",
        (array(PLANES, ROWS, COLS), array(2, ROWS, COLS)),
        [HBM],
        (VMEM,) * 2,
        flops=10**9,
        scratch_shapes=[pltpu.SemaphoreType.DMA],
    )(density)
    cores = [[2 * chip, 2 * chip + 1] for chip in range(CHIPS)]
    coming = lax.ppermute(first, "depth", [(i + 1, i) for i in range(depths - 1)])
    own_high, own_low = kernel(
        cut_kernel, "cut", (array(PLANES + 2, SHEAR, COLS), array(PLANES + 8, COLS)), [VMEM] * 2, (VMEM,) * 2
    )(own, coming)
    high = lax.ppermute(own_high, "height", [(i + 1, i) for i in range(heights - 1)])
    low = lax.ppermute(own_low, "height", [(i, i + 1) for i in range(heights - 1)])

    shaded = array(4, SLABS * TALL, COLS)
    fields, table, masks, starts = kernel(
        inner_kernel,
        "inner",
        (shaded, array(16, COLS), array(5, 8, COLS), jax.ShapeDtypeStruct((64,), jnp.int32)),
        [HBM] * 5 + [VMEM] * 3,
        (VMEM, VMEM, VMEM, SMEM),
        flops=10**7,
        scratch_shapes=[pltpu.SMEM((3,), jnp.float32)] * 3
        + [pltpu.SMEM((VIEWS,), jnp.int32)] * 2
        + [pltpu.SemaphoreType.DMA((5,))],
    )(light_vector, colour_gain, colour_bias, shear_step, reverse_view, own, coming, own_low)
    part = array(CHIPS, 4, VIEWS // 2, 8, COLS)
    memory = [pltpu.SMEM((64,), jnp.int32), pltpu.SemaphoreType.DMA]
    given, kept, fields = kernel(
        render_kernel,
        "render",
        (part, part, shaded),
        [VMEM, VMEM, ANY] + [VMEM] * 4,
        (VMEM,) * 3,
        flops=10**7,
        input_output_aliases={6: 2},
        scratch_shapes=[pltpu.VMEM((PLANES + 2, 24 + SHEAR, COLS), jnp.float32), *memory],
    )(table, masks, starts, own, coming, high, fields)
    given, kept, _ = kernel(
        first_kernel,
        "first",
        (part, part, shaded),
        [VMEM, VMEM, ANY] + [VMEM] * 6,
        (VMEM,) * 3,
        input_output_aliases={6: 2, 7: 0, 8: 1},
        scratch_shapes=memory,
    )(table, masks, starts, own, coming, low, fields, given, kept)

    gathered = lax.all_gather(given, "depth", axis=0, axis_index_groups=cores)
    merged = kernel(merge_kernel, "merge", part, [VMEM] * 3, VMEM)(masks, kept, gathered)
    groups = [[2 * chip + core for chip in ORDERS[core]] for core in range(2)]
    slabs = lax.all_to_all(merged, "depth", 0, 0, tiled=True, axis_index_groups=groups)
    return kernel(final_kernel, "composite", array(4, VIEWS, SHARE, COLS), [VMEM] * 2, VMEM)(masks, slabs)


def solution(mesh):
    placed = (P("depth", "height", None), P(), P(), P(), P(), P())
    return jax.shard_map(
        on_device,
        mesh=mesh,
        in_specs=placed,
        out_specs=P(None, None, ("height", "depth"), None),
        check_vma=False,
    )
```

```python
import jax
import jax.numpy as jnp
from jax import lax
from jax.experimental import pallas as pl
from jax.experimental.pallas import tpu as pltpu
from jax.sharding import PartitionSpec as P

EXTINCTION = 2.5
SMEM = pl.BlockSpec(memory_space=pltpu.SMEM)
VMEM = pl.BlockSpec(memory_space=pltpu.VMEM)
ANY = pl.BlockSpec(memory_space=pl.ANY)
HBM = pl.BlockSpec(memory_space=pltpu.HBM)
PLANES, ROWS, COLS, SHEAR, VIEWS, GROUPS, BRICKS = 8, 64, 128, 32, 4, 16, 32
TALL = ROWS + SHEAR
SLABS = PLANES + 1
CHIPS = GROUPS // 2
SHARE = ROWS // GROUPS
ORDERS = ((7, 6, 5, 4, 3, 2, 0, 1), (7, 6, 5, 4, 3, 2, 1, 0))
PARAMS = pltpu.CompilerParams(vmem_limit_bytes=8 * 2**20)
LIGHT, GAIN, BIAS, PLAIN, BEYOND, NEXT, NEXT_BEYOND = 0, 3, 6, 9, 10, 11, 12
FRONT, BACK, CORE = 0, 2, 4
INNER = slice(8, ROWS - 8)
FIRST = VIEWS * SLABS


def array(*shape):
    return jax.ShapeDtypeStruct(shape, jnp.float32)


def opacity_of(optical):
    series = 1.0 - optical * (1.0 / 6.0)
    for term in (5.0, 4.0, 3.0, 2.0):
        series = 1.0 - optical * (1.0 / term) * series
    return optical * series


def shade(coefficient, extinction, centre, above, below, before, after):
    lane = lax.broadcasted_iota(jnp.int32, centre.shape, 1)
    tilt_rows = 0.5 * (below - above)
    tilt_depth = 0.5 * (after - before)
    right = jnp.where(lane == COLS - 1, 0.0, pltpu.roll(centre, COLS - 1, 1))
    left = jnp.where(lane == 0, 0.0, pltpu.roll(centre, 1, 1))
    tilt_cols = 0.5 * (right - left)
    slope = coefficient(LIGHT) * tilt_depth + coefficient(LIGHT + 1) * tilt_rows + coefficient(LIGHT + 2) * tilt_cols
    facing = slope * lax.rsqrt(1.0 + tilt_depth * tilt_depth + tilt_rows * tilt_rows + tilt_cols * tilt_cols)
    shading = 0.25 + 1.5 * jnp.maximum(facing, 0.0)
    optical = extinction * (jnp.maximum(centre, 0.0) + jnp.log1p(jnp.exp(-jnp.abs(centre))))
    strength = opacity_of(optical) * shading
    tones = [jax.nn.sigmoid(coefficient(GAIN + i) * centre + coefficient(BIAS + i)) for i in range(3)]
    return [strength * tone for tone in tones] + [optical]


def load_kernel(density, own, first, semaphore):
    copy = pltpu.make_async_copy(density, own, semaphore)
    copy.start()
    copy.wait()
    first[...] = own[:2]


def inner_kernel(*refs):
    arguments, (own, coming, _, fields, table, masks, starts), scalars, semaphores = refs[:5], refs[5:12], refs[12:17], refs[17]
    copies = [pltpu.make_async_copy(arguments[i], scalars[i], semaphores.at[i]) for i in range(5)]
    for copy in copies:
        copy.start()
    depth, height = lax.axis_index("depth"), lax.axis_index("height")
    for copy in copies:
        copy.wait()
    light, gain, bias, shear, reverse = scalars
    extinction = EXTINCTION / (PLANES * GROUPS)
    beyond = jnp.where(height == BRICKS - 1, 0.0, extinction)
    following = jnp.where(depth == GROUPS - 1, 0.0, extinction)
    both = jnp.where(depth == GROUPS - 1, 0.0, beyond)
    values_of = [ref[i] for ref in (light, gain, bias) for i in range(3)] + [extinction, beyond, following, both]
    for row, scalar in enumerate(values_of):
        table[row : row + 1, :] = jnp.full((1, COLS), scalar, jnp.float32)
    upper = lax.broadcasted_iota(jnp.int32, (8, COLS), 0) < SHARE
    core = depth % 2
    for base, digit in ((FRONT, core), (BACK, 1)):
        for pair in range(VIEWS // 2):
            first = jnp.where(reverse[2 * pair] == digit, 1.0, 0.0)
            second = jnp.where(reverse[2 * pair + 1] == digit, 1.0, 0.0)
            masks[base + pair] = jnp.where(upper, first, second)
    masks[CORE] = jnp.full((8, COLS), core, jnp.float32)
    first = jnp.where(depth == 0, 0, 1)
    starts[FIRST] = first
    for view in range(VIEWS):
        for step in range(SLABS):
            slot = jnp.where(reverse[view] == 1, SLABS - 1 - step, jnp.minimum(first + step, SLABS - 1))
            offset = lax.shift_right_logical((depth * PLANES + slot) * shear[view], 7)
            starts[view * SLABS + step] = slot * TALL + jnp.minimum(offset, SHEAR)

    coefficient = lambda at: values_of[at]

    def plane_of(plane, _):
        shade_inner(coefficient, extinction, own.at[plane], own[plane - 1, INNER, :], own[plane + 1, INNER, :], fields, plane)
        return 0

    lax.fori_loop(1, PLANES - 1, plane_of, 0)
    last = own.at[PLANES - 1]
    shade_inner(coefficient, extinction, last, own[PLANES - 2, INNER, :], coming[0, INNER, :], fields, PLANES - 1)
    shade_inner(coefficient, following, coming.at[0], last[INNER, :], coming[1, INNER, :], fields, PLANES)

    @pl.when(depth == 0)
    def _():
        shade_inner(coefficient, extinction, own.at[0], 0.0, own[1, INNER, :], fields, 0)


def shade_inner(coefficient, extinction, plane, before, after, fields, slot):
    centre = plane[INNER, :]
    values = shade(coefficient, extinction, centre, plane[7 : ROWS - 9, :], plane[9 : ROWS - 7, :], before, after)
    store(fields, slot, 8, values)


def store(fields, slot, row, values):
    rows = pl.ds(pl.multiple_of(slot * TALL + row, 8), values[0].shape[0])
    for kind in range(4):
        fields[kind, rows, :] = values[kind]


def cut_kernel(own, coming, high, low):
    high[:PLANES] = own[:, :SHEAR, :]
    high[PLANES:] = coming[:, :SHEAR, :]
    for plane in range(PLANES):
        low[plane : plane + 1, :] = own[plane, ROWS - 1 : ROWS, :]
    low[PLANES:, :] = jnp.broadcast_to(coming[0, ROWS - 1 : ROWS, :], (8, COLS))


def render_kernel(
    table, masks, starts_in, own, coming, high, held, given, kept, fields, brick, starts, semaphore
):
    del held
    copy = pltpu.make_async_copy(starts_in, starts, semaphore)
    copy.start()
    coefficient = lambda at: table[at : at + 1, :]
    for plane in range(PLANES + 2):
        source = own.at[plane] if plane < PLANES else coming.at[plane - PLANES]
        brick[plane, :16, :] = source[ROWS - 16 :, :]
        brick[plane, 16 : 16 + SHEAR, :] = high[plane]
        brick[plane, 16 + SHEAR :, :] = jnp.zeros((8, COLS), jnp.float32)

    def rows_of(slot, before, plain, beyond):
        for start, count, extinction in ((8, 8, plain), (16, SHEAR, beyond)):
            values = shade(
                coefficient,
                coefficient(extinction),
                brick[slot, start : start + count, :],
                brick[slot, start - 1 : start - 1 + count, :],
                brick[slot, start + 1 : start + 1 + count, :],
                0.0 if before is None else brick[before, start : start + count, :],
                brick[slot + 1, start : start + count, :],
            )
            store(fields, slot, ROWS - 16 + start, values)

    def plane_of(plane, _):
        rows_of(plane, plane - 1, PLAIN, BEYOND)
        return 0

    lax.fori_loop(1, PLANES, plane_of, 0)
    rows_of(PLANES, PLANES - 1, NEXT, NEXT_BEYOND)

    @pl.when(lax.axis_index("depth") == 0)
    def _():
        rows_of(0, None, PLAIN, BEYOND)

    copy.wait()
    render(masks, starts, fields, given, kept, 1, ROWS // 8)


def first_kernel(table, masks, starts_in, own, coming, low, held, *refs):
    del held
    given, kept, fields, starts, semaphore = refs[2:]
    copy = pltpu.make_async_copy(starts_in, starts, semaphore)
    copy.start()
    coefficient = lambda at: table[at : at + 1, :]
    top = lax.broadcasted_iota(jnp.int32, (8, COLS), 0) == 0

    def first_rows(slot):
        plane_at = lambda plane: own.at[plane] if plane < PLANES else coming.at[plane - PLANES]
        plane = plane_at(slot)
        centre = plane[:8, :]
        above = jnp.where(top, low[slot : slot + 1, :], pltpu.roll(centre, 1, 0))
        before = 0.0 if slot == 0 else plane_at(slot - 1)[:8, :]
        extinction = coefficient(NEXT if slot == PLANES else PLAIN)
        store(fields, slot, 0, shade(coefficient, extinction, centre, above, plane[1:9, :], before, plane_at(slot + 1)[:8, :]))

    for slot in range(1, SLABS):
        first_rows(slot)

    @pl.when(lax.axis_index("depth") == 0)
    def _():
        first_rows(0)

    copy.wait()
    render(masks, starts, fields, given, kept, 0, 1)


def render(masks, starts, fields, given, kept, tile, tiles):
    upper = lax.broadcasted_iota(jnp.int32, (8, COLS), 0) < SHARE
    odd = masks[CORE] > 0.5

    def of(planes):
        def tile_of(tile, _):
            for pair in range(VIEWS // 2):
                sums = []
                for view in (2 * pair, 2 * pair + 1):
                    red = green = blue = optical = jnp.zeros((8, COLS), jnp.float32)
                    for step in range(planes):
                        rows = pl.ds(starts[view * SLABS + step] + 8 * tile, 8)
                        through = jnp.exp(-optical)
                        red = red + fields[0, rows, :] * through
                        green = green + fields[1, rows, :] * through
                        blue = blue + fields[2, rows, :] * through
                        optical = optical + fields[3, rows, :]
                    sums.append((red, green, blue, optical))
                for kind in range(4):
                    first, second = sums[0][kind], sums[1][kind]
                    even_rows = jnp.where(upper, first, pltpu.roll(second, SHARE, 0))
                    odd_rows = jnp.where(upper, pltpu.roll(first, SHARE, 0), second)
                    kept[tile, kind, pair] = jnp.where(odd, odd_rows, even_rows)
                    given[tile, kind, pair] = jnp.where(odd, even_rows, odd_rows)
            return 0

        lax.fori_loop(tile, tiles, tile_of, 0)

    leading = starts[FIRST] == 0

    @pl.when(leading)
    def _():
        of(SLABS)

    @pl.when(jnp.logical_not(leading))
    def _():
        of(PLANES)


def place_of(core, chip):
    return jnp.where(core == 1, ORDERS[1].index(chip), ORDERS[0].index(chip))


def merge_kernel(masks, kept, gathered, out):
    odd = masks[CORE] > 0.5
    core = lax.axis_index("depth") % 2
    for pair in range(VIEWS // 2):
        mine_front = masks[FRONT + pair] > 0.5

        for chip in range(CHIPS):
            place = place_of(core, chip)
            mine = [kept[chip, kind, pair] for kind in range(4)]
            other = [jnp.where(odd, gathered[0, chip, kind, pair], gathered[1, chip, kind, pair]) for kind in range(4)]
            through = jnp.exp(-jnp.where(mine_front, mine[3], other[3]))
            for kind in range(3):
                front = jnp.where(mine_front, mine[kind], other[kind])
                behind = jnp.where(mine_front, other[kind], mine[kind])
                out[place, kind, pair] = front + through * behind
            out[place, 3, pair] = mine[3] + other[3]


def final_kernel(masks, slabs, out):
    places = [place_of(lax.axis_index("depth") % 2, chip) for chip in range(CHIPS)]
    for pair in range(VIEWS // 2):
        backward = masks[BACK + pair] > 0.5
        optical = [slabs[place, 3, pair] for place in places]
        ahead, behind = [jnp.zeros((8, COLS), jnp.float32)], [jnp.zeros((8, COLS), jnp.float32)]
        for chip in range(CHIPS - 1):
            ahead.append(ahead[-1] + optical[chip])
            behind.append(behind[-1] + optical[CHIPS - 1 - chip])
        total = ahead[-1] + optical[-1]
        sums = [jnp.zeros((8, COLS), jnp.float32)] * 3
        for chip in range(CHIPS):
            through = jnp.exp(-jnp.where(backward, behind[CHIPS - 1 - chip], ahead[chip]))
            sums = [sums[kind] + slabs[places[chip], kind, pair] * through for kind in range(3)]
        cover = jnp.where(total < 0.0625, opacity_of(total), 1.0 - jnp.exp(-total))
        for kind, value in enumerate((*sums, cover)):
            out[kind, 2 * pair] = value[:SHARE]
            out[kind, 2 * pair + 1] = value[SHARE:]


def kernel(body, name, out_shape, in_specs, out_specs, flops=0, **more):
    estimate = pl.CostEstimate(flops=flops, bytes_accessed=2**20, transcendentals=0)
    return pl.pallas_call(
        body,
        out_shape=out_shape,
        in_specs=in_specs,
        out_specs=out_specs,
        compiler_params=PARAMS,
        cost_estimate=estimate,
        name=name,
        **more,
    )


def on_device(density, light_vector, colour_gain, colour_bias, shear_step, reverse_view):
    heights, depths = lax.axis_size("height"), lax.axis_size("depth")

    own, first = kernel(
        load_kernel,
        "load",
        (array(PLANES, ROWS, COLS), array(2, ROWS, COLS)),
        [HBM],
        (VMEM,) * 2,
        flops=10**9,
        scratch_shapes=[pltpu.SemaphoreType.DMA],
    )(density)
    cores = [[2 * chip, 2 * chip + 1] for chip in range(CHIPS)]
    coming = lax.ppermute(first, "depth", [(i + 1, i) for i in range(depths - 1)])
    own_high, own_low = kernel(
        cut_kernel, "cut", (array(PLANES + 2, SHEAR, COLS), array(PLANES + 8, COLS)), [VMEM] * 2, (VMEM,) * 2
    )(own, coming)
    high = lax.ppermute(own_high, "height", [(i + 1, i) for i in range(heights - 1)])
    low = lax.ppermute(own_low, "height", [(i, i + 1) for i in range(heights - 1)])

    shaded = array(4, SLABS * TALL, COLS)
    fields, table, masks, starts = kernel(
        inner_kernel,
        "inner",
        (shaded, array(16, COLS), array(5, 8, COLS), jax.ShapeDtypeStruct((64,), jnp.int32)),
        [HBM] * 5 + [VMEM] * 3,
        (VMEM, VMEM, VMEM, SMEM),
        flops=10**7,
        scratch_shapes=[pltpu.SMEM((3,), jnp.float32)] * 3
        + [pltpu.SMEM((VIEWS,), jnp.int32)] * 2
        + [pltpu.SemaphoreType.DMA((5,))],
    )(light_vector, colour_gain, colour_bias, shear_step, reverse_view, own, coming, own_low)
    part = array(CHIPS, 4, VIEWS // 2, 8, COLS)
    memory = [pltpu.SMEM((64,), jnp.int32), pltpu.SemaphoreType.DMA]
    given, kept, fields = kernel(
        render_kernel,
        "render",
        (part, part, shaded),
        [VMEM, VMEM, ANY] + [VMEM] * 4,
        (VMEM,) * 3,
        flops=10**7,
        input_output_aliases={6: 2},
        scratch_shapes=[pltpu.VMEM((PLANES + 2, 24 + SHEAR, COLS), jnp.float32), *memory],
    )(table, masks, starts, own, coming, high, fields)
    given, kept, _ = kernel(
        first_kernel,
        "first",
        (part, part, shaded),
        [VMEM, VMEM, ANY] + [VMEM] * 6,
        (VMEM,) * 3,
        input_output_aliases={6: 2, 7: 0, 8: 1},
        scratch_shapes=memory,
    )(table, masks, starts, own, coming, low, fields, given, kept)

    gathered = lax.all_gather(given, "depth", axis=0, axis_index_groups=cores)
    merged = kernel(merge_kernel, "merge", part, [VMEM] * 3, VMEM)(masks, kept, gathered)
    groups = [[2 * chip + core for chip in ORDERS[core]] for core in range(2)]
    slabs = lax.all_to_all(merged, "depth", 0, 0, tiled=True, axis_index_groups=groups)
    return kernel(final_kernel, "composite", array(4, VIEWS, SHARE, COLS), [VMEM] * 2, VMEM)(masks, slabs)


def solution(mesh):
    placed = (P("depth", "height", None), P(), P(), P(), P(), P())
    return jax.shard_map(
        on_device,
        mesh=mesh,
        in_specs=placed,
        out_specs=P(None, None, ("height", "depth"), None),
        check_vma=False,
    )
```
